32 devices in a mesh: tile: 16 (over z, x, core), spec: 2 (over y).
Axes of the slice: x: 2, y: 2, z: 4, core: 2. Of those that a mesh axis runs over, the one named last changes fastest.
Arguments:
- mixing: float32 [72, 1, 6, 128, 128], P('spec', None, None, 'tile'), may hold values from -6 to 6
- layer_mass: float32 [1, 6, 128, 128], P(None, None, 'tile', 'spec'), may hold values from 0.6 to 1.4
- mass_east: float32 [1, 6, 128, 128], P(None, None, 'tile', 'spec'), may hold values from -0.12 to 0.12
- mass_north: float32 [1, 6, 128, 128], P(None, None, 'tile', 'spec'), may hold values from -0.12 to 0.12
- face_slot: int32 [6], replicated, may hold values from 0 to 5, each once
Outputs:
- advected: float32 [72, 1, 6, 128, 128], P('spec', None, None, 'tile')
The draws below stay inside these ranges and needn't reach their ends.
Inputs may be any that keep to these rules, and one draw needn't show every extreme that they name: face_slot[s] names the cube face kept in storage slot s; each of the six faces appears once.
All inputs are finite; a program needn't handle non-finite values.
Results may differ from the reference program's by a relative error of at most 0.00002.
Values sent between devices are 32-bit elements; how exact they have to be, the bound alone decides.
No kernel may reach another device: no remote copies, remote signals or barrier semaphores. Data moves between devices by JAX's collectives and lax.ppermute only.
A program may use at most 128 MiB of HBM per device.

```python
import jax
import jax.numpy as jnp
from jax import lax

SPECIES = 72
LEV = 1
N = 128


def block_levels(key, extent, cuts, smallest, top_value):
    level, own = 1.0, jax.random.fold_in(key, 6)
    for dim, parts in cuts:
        steps = jnp.exp(jax.random.uniform(jax.random.fold_in(own, dim), (parts,), jnp.float32, smallest / len(cuts), top_value / len(cuts)))
        level = level * jnp.repeat(steps, extent[dim] // parts).reshape([-1 if axis == dim else 1 for axis in range(len(extent))])
    return level


def normal_values(key, shape, deviation, bound, pieces=(), kind=jnp.bfloat16):
    gain = block_levels(key, shape, pieces, -0.22, 0.18) if pieces else 1.0
    drawn = jax.random.normal(key, shape, jnp.float32) * deviation * gain
    return jnp.minimum(jnp.maximum(drawn, -bound), bound).astype(kind)


def setup_inputs(seed: int = 0) -> dict:
    arg_keys = jax.random.split(jax.random.key(seed), 6)
    return {
        "mixing": normal_values(arg_keys[0], (SPECIES, LEV, 6, N, N), 1.0, 6.0, ((0, 2), (3, 16)), jnp.float32),
        "layer_mass": jnp.clip(0.6 + 0.79999995 * jax.random.uniform(arg_keys[1], (LEV, 6, N, N), jnp.float32) ** block_levels(arg_keys[1], (LEV, 6, N, N), ((2, 16), (3, 2)), -0.2, 0.2), 0.6, 1.4),
        "mass_east": jnp.clip(jax.random.uniform(arg_keys[2], (LEV, 6, N, N), jnp.float32, -0.12, 0.12) * block_levels(arg_keys[2], (LEV, 6, N, N), ((2, 16), (3, 2)), -0.4, 0.0), -0.12, 0.12),
        "mass_north": jnp.clip(jax.random.uniform(arg_keys[3], (LEV, 6, N, N), jnp.float32, -0.12, 0.12) * block_levels(arg_keys[3], (LEV, 6, N, N), ((2, 16), (3, 2)), -0.4, 0.0), -0.12, 0.12),
        "face_slot": jax.random.permutation(arg_keys[4], 6).astype(jnp.int32),
    }


def sides_x(plain, turned):
    size = plain.shape[-1]
    wests = []
    easts = []
    for face in range(6):
        if face % 2 == 0:
            easts.append(plain[..., (face + 1) % 6, :, 0:2])
            wests.append(jnp.swapaxes(jnp.flip(turned[..., (face - 2) % 6, size - 2:, :], -1), -1, -2))
        else:
            easts.append(jnp.swapaxes(jnp.flip(turned[..., (face + 2) % 6, 0:2, :], -1), -1, -2))
            wests.append(plain[..., (face - 1) % 6, :, size - 2:])
    return jnp.stack(wests, -3), jnp.stack(easts, -3)


def sides_y(plain, turned):
    size = plain.shape[-1]
    souths = []
    norths = []
    for face in range(6):
        if face % 2 == 0:
            souths.append(plain[..., (face - 1) % 6, size - 2:, :])
            norths.append(jnp.swapaxes(jnp.flip(turned[..., (face + 2) % 6, :, 0:2], -2), -1, -2))
        else:
            souths.append(jnp.swapaxes(jnp.flip(turned[..., (face - 2) % 6, :, size - 2:], -2), -1, -2))
            norths.append(plain[..., (face + 1) % 6, 0:2, :])
    return jnp.stack(souths, -3), jnp.stack(norths, -3)


def advect(tracer, layer, wide, tall, mass_wide, mass_tall, east_flow, north_flow):
    cols = tracer.shape[-1]
    rows = tracer.shape[-2]
    edge_x = (7.0 * (wide[..., 1:cols + 2] + wide[..., 2:cols + 3]) - (wide[..., 0:cols + 1] + wide[..., 3:cols + 4])) / 12.0
    courant_x = east_flow / (0.5 * (mass_wide[..., 1:cols + 2] + mass_wide[..., 2:cols + 3]))
    flux_x = east_flow * edge_x + 0.5 * jnp.abs(east_flow) * (1.0 - jnp.abs(courant_x)) * (wide[..., 1:cols + 2] - wide[..., 2:cols + 3])
    edge_y = (7.0 * (tall[..., 1:rows + 2, :] + tall[..., 2:rows + 3, :]) - (tall[..., 0:rows + 1, :] + tall[..., 3:rows + 4, :])) / 12.0
    courant_y = north_flow / (0.5 * (mass_tall[..., 1:rows + 2, :] + mass_tall[..., 2:rows + 3, :]))
    flux_y = north_flow * edge_y + 0.5 * jnp.abs(north_flow) * (1.0 - jnp.abs(courant_y)) * (tall[..., 1:rows + 2, :] - tall[..., 2:rows + 3, :])
    layer_new = layer - (east_flow[..., 1:] - east_flow[..., :-1]) - (north_flow[..., 1:, :] - north_flow[..., :-1, :])
    change = (flux_x[..., 1:] - flux_x[..., :-1]) + (flux_y[..., 1:, :] - flux_y[..., :-1, :])
    return (tracer * layer - change) / layer_new


def reference(mixing, layer_mass, mass_east, mass_north, face_slot):
    faces_iota = jnp.arange(6, dtype=jnp.int32)
    match = (face_slot[None, :] == faces_iota[:, None]).astype(jnp.int32)
    inverse = jnp.sum(faces_iota[None, :] * match, axis=1).astype(jnp.int32)
    layer = jnp.take(layer_mass, inverse, axis=1)
    east = jnp.take(mass_east, inverse, axis=1)
    north = jnp.take(mass_north, inverse, axis=1)
    tracer = jnp.take(mixing, inverse, axis=2)
    mass_w, mass_e = sides_x(layer, layer)
    mass_wide = jnp.concatenate([mass_w, layer, mass_e], axis=-1)
    mass_s, mass_n = sides_y(layer, layer)
    mass_tall = jnp.concatenate([mass_s, layer, mass_n], axis=-2)
    flow_w, flow_e = sides_x(east, north)
    east_flow = jnp.concatenate([east, flow_e[..., 0:1]], axis=-1)
    flow_s, flow_n = sides_y(north, east)
    north_flow = jnp.concatenate([north, flow_n[..., 0:1, :]], axis=-2)

    def single(values):
        west_part, east_part = sides_x(values, values)
        south_part, north_part = sides_y(values, values)
        wide = jnp.concatenate([west_part, values, east_part], axis=-1)
        tall = jnp.concatenate([south_part, values, north_part], axis=-2)
        return advect(values, layer, wide, tall, mass_wide, mass_tall, east_flow, north_flow)

    result = lax.map(single, tracer)
    return jnp.take(result, face_slot, axis=2)
```

```python
import jax
import jax.numpy as jnp
from jax import lax
from jax.experimental import pallas as pl
from jax.experimental.pallas import tpu as pltpu
from jax.sharding import PartitionSpec as P

F32 = jnp.float32


def up(value, unit):
    return -(-value // unit) * unit


class Sizes:
    def __init__(self, mixing, halves, tiles):
        self.species, _, _, self.rows, self.width = mixing.shape
        self.tiles, self.halves = tiles, halves
        self.group = up(2 * self.species, 8)
        self.flux = 3 * self.group
        self.block = up(self.flux + 6, 8)
        self.lanes = up(self.block, 128)
        self.extra = 2 * self.block
        self.sent = self.extra + 8 * (self.lanes // 128)


def slots(face_slot):
    return [sum(jnp.where(face_slot[s] == f, s, 0) for s in range(6)) for f in range(6)]


def reversal(width):
    i = lax.broadcasted_iota(jnp.int32, (width, width), 0)
    j = lax.broadcasted_iota(jnp.int32, (width, width), 1)
    return jnp.where(i + j == width - 1, 1.0, 0.0).astype(F32)


def pack_kernel(z, face_slot, mixing, own, other, to_a, to_b, slots_out, kept, full):
    place = lax.axis_index("tile")
    half = lax.axis_index("spec")
    slot = slots(face_slot)
    even = lax.rem(place, 2) == 0
    first = place == 0
    width, species = z.width, z.species
    for c in range(3):
        for f in range(6):
            if z.halves == 2:
                a, b = own[c, slot[f]], other[c, slot[f]]
                parts = [jnp.where(half == 0, a, b), jnp.where(half == 0, b, a)]
            else:
                parts = [other[n, c, slot[f]] for n in range(z.halves)]
            full[c * 6 + f] = jnp.concatenate(parts, axis=-1)

    def both(low, high, at):
        to_a[pl.ds(at, low.shape[0])] = jnp.where(even, high, low)
        to_b[pl.ds(at, low.shape[0])] = jnp.where(even, low, high)

    lane = lax.broadcasted_iota(jnp.int32, (8, 128), 1)
    gathers = []
    for parity in range(2):
        base = parity * z.block
        lanes = [jnp.zeros((8, 128), F32) for _ in range(z.lanes // 128)]
        for a in range(3):
            f = 2 * a + parity
            for s in range(0, species):
                tile = mixing[s, 0, slot[f]]
                at = a * z.group + 2 * s
                both(tile[0:2], tile[6:8], base + at)
                edge = tile[:, :128] if parity == 0 else tile[:, width - 128 :]
                shift = (at - (0 if parity == 0 else 126)) % 128
                moved = pltpu.roll(edge, shift, 1) if shift else edge
                k = at // 128
                lanes[k] = jnp.where((lane >> 1) == (at % 128) // 2, moved, lanes[k])
            for at, low_from, col_from in ((z.flux + a, 0, 0), (z.flux + 3 + a, 2, 1)):
                rows = full[low_from * 6 + f]
                both(rows[0:1], rows[7:8], base + at)
                cols = full[col_from * 6 + f]
                edge = cols[:, :128] if parity == 0 else cols[:, width - 128 :]
                shift = (at - (0 if parity == 0 else 127)) % 128
                moved = pltpu.roll(edge, shift, 1) if shift else edge
                k = at // 128
                lanes[k] = jnp.where(lane == at % 128, moved, lanes[k])
        if z.block > z.flux + 6:
            pad = z.block - z.flux - 6
            both(jnp.zeros((pad, width), F32), jnp.zeros((pad, width), F32), base + z.flux + 6)
        if z.group > 2 * species:
            pad = z.group - 2 * species
            for a in range(3):
                both(
                    jnp.zeros((pad, width), F32),
                    jnp.zeros((pad, width), F32),
                    base + a * z.group + 2 * species,
                )
        gathers.append(lanes)
    for k in range(z.lanes // 128):
        even_cols, odd_cols = gathers[0][k], gathers[1][k]
        kept[:, k * 128 : (k + 1) * 128] = jnp.where(first, odd_cols, even_cols)
        spare = jnp.where(first, even_cols, odd_cols)
        at = z.extra + 8 * k
        if width > 128:
            spare = jnp.concatenate([spare] * (width // 128), axis=-1)
        to_a[pl.ds(at, 8)] = spare
        to_b[pl.ds(at, 8)] = spare
        slots_out[0:8, k * 128 : (k + 1) * 128] = odd_cols
        slots_out[8 * (z.tiles - 1) :, k * 128 : (k + 1) * 128] = even_cols

    @pl.when(first | (place == z.tiles - 1))
    def _():
        start = pl.multiple_of(jnp.where(first, z.block, 0), 8)
        rows = to_b[pl.ds(start, z.block)]
        if z.lanes > z.block:
            rows = jnp.concatenate([rows, jnp.zeros((z.lanes - z.block, width), F32)], axis=0)
        slots_out[...] = lax.dot_general(
            reversal(width),
            rows,
            (((1,), (1,)), ((), ())),
            precision=lax.Precision.HIGHEST,
            preferred_element_type=F32,
        )


def step_kernel(
    z, face_slot, mixing, from_a, from_b, arrived, kept, full, out,
    south, north, side, coef, result, copy_sem, out_sem,
):
    place = lax.axis_index("tile")
    slot = slots(face_slot)
    even = lax.rem(place, 2) == 0
    first = place == 0
    last = place == z.tiles - 1
    width, species, block = z.width, z.species, z.block
    blocks = pl.ds(0, 2 * block)

    def halo(source_s, source_n):
        return (
            pltpu.make_async_copy(source_s.at[blocks], south.at[blocks], copy_sem.at[0]),
            pltpu.make_async_copy(source_n.at[blocks], north.at[blocks], copy_sem.at[1]),
        )

    @pl.when(even)
    def _():
        for copy in halo(from_b, from_a):
            copy.start()
        for copy in halo(from_b, from_a):
            copy.wait()

    @pl.when(jnp.logical_not(even))
    def _():
        for copy in halo(from_a, from_b):
            copy.start()
        for copy in halo(from_a, from_b):
            copy.wait()

    lane = lax.broadcasted_iota(jnp.int32, (8, width), 1)
    row = lax.broadcasted_iota(jnp.int32, (8, width), 0)
    lane1 = lax.broadcasted_iota(jnp.int32, (8, 128), 1)

    @pl.when(first | last)
    def _():
        fetch = pltpu.make_async_copy(
            from_b.at[pl.ds(z.extra, z.sent - z.extra)], side.at[pl.ds(0, z.sent - z.extra)], copy_sem.at[2]
        )
        fetch.start()
        fetch.wait()
        pieces = []
        for k in range(z.lanes // 128):
            part = slice(k * 128, (k + 1) * 128)
            spare = side[8 * k : 8 * k + 8, 0:128]
            mine = kept[:, part]
            head = jnp.where(first, mine, spare)
            tail = jnp.where(first, spare, mine)
            pieces.append(jnp.concatenate([head, arrived[8 : 8 * (z.tiles - 1), part], tail], axis=0))
        cols = jnp.concatenate(pieces, axis=1) if len(pieces) > 1 else pieces[0]
        turned = lax.dot_general(
            cols,
            reversal(width),
            (((0,), (0,)), ((), ())),
            precision=lax.Precision.HIGHEST,
            preferred_element_type=F32,
        )[:block]

        @pl.when(first)
        def _():
            south[2 * block : 3 * block] = turned

        @pl.when(last)
        def _():
            north[2 * block : 3 * block] = turned

    south_at = [jnp.where(first, block, 0), jnp.where(first, 2 * block, block)]
    north_at = [jnp.where(last, 2 * block, 0), jnp.where(last, 0, block)]
    south_a = [jnp.where(first, (a + 2) % 3, a) for a in range(3)]
    north_a = [jnp.where(last, (a + 1) % 3, a) for a in range(3)]

    def one(ref, at):
        eight = pl.multiple_of(lax.div(at, 8) * 8, 8)
        rows = ref[pl.ds(eight, 8)]
        return jnp.sum(jnp.where(row == at - eight, rows, 0.0), axis=0, keepdims=True)

    def spread(k, lane_at):
        part = arrived[8 * k : 8 * k + 8, (lane_at // 128) * 128 : (lane_at // 128) * 128 + 128]
        return jnp.sum(jnp.where(lane1 == lane_at % 128, part, 0.0), axis=1, keepdims=True)

    def left(x, ghost, n):
        return pltpu.roll(jnp.where(lane >= width - n, ghost, x), n, 1)

    def right(x, ghost, n):
        return pltpu.roll(jnp.where(lane < n, ghost, x), width - n, 1)

    def below(x, ghost, n):
        return pltpu.roll(jnp.where(row >= 8 - n, ghost, x), n, 0)

    def above(x, ghost, n):
        return pltpu.roll(jnp.where(row < n, ghost, x), 8 - n, 0)

    def upwind(u, total):
        return 0.5 * jnp.abs(u) * (1.0 - jnp.abs(u / (0.5 * total)))

    for f in range(6):
        a, parity = f // 2, f % 2
        dp, fx, fy = full[f], full[6 + f], full[12 + f]
        if parity == 0:
            west = spread(z.tiles - 1, z.flux + (a + 2) % 3)
            east, east_u = full[f + 1], full[6 + f + 1]
        else:
            west = full[f - 1]
            east = spread(0, z.flux + (a + 1) % 3)
            east_u = spread(0, z.flux + 3 + (a + 1) % 3)
        dp_w, dp_e = left(dp, west, 1), right(dp, east, 1)
        u0, u1 = fx, right(fx, east_u, 1)
        dp_s = below(dp, one(south, south_at[parity] + z.flux + south_a[a]), 1)
        dp_n = above(dp, one(north, north_at[parity] + z.flux + north_a[a]), 1)
        v0, v1 = fy, above(fy, one(north, north_at[parity] + z.flux + 3 + north_a[a]), 1)
        inverse = 1.0 / (dp - (u1 - u0) - (v1 - v0))
        center = dp
        for n, (w0, w1, d0, d1) in enumerate(((u0, u1, dp_w, dp_e), (v0, v1, dp_s, dp_n))):
            b0, b1 = upwind(w0, d0 + dp), upwind(w1, dp + d1)
            p0, p1 = w0 * (1.0 / 12.0), w1 * (1.0 / 12.0)
            coef[f, 4 * n] = -p0 * inverse
            coef[f, 4 * n + 1] = (7.0 * p0 + b0 + p1) * inverse
            coef[f, 4 * n + 2] = (-p0 - 7.0 * p1 + b1) * inverse
            coef[f, 4 * n + 3] = p1 * inverse
            center = center + (7.0 * p0 - b0) - (7.0 * p1 + b1)
        coef[f, 8] = center * inverse

    def ghosts(a, s):
        east_at = ((a + 1) % 3) * z.group + 2 * s
        west_at = ((a + 2) % 3) * z.group + 2 * s
        east = arrived[0:8, (east_at // 128) * 128 : (east_at // 128) * 128 + 128]
        west = arrived[8 * (z.tiles - 1) :, (west_at // 128) * 128 : (west_at // 128) * 128 + 128]
        east = pltpu.roll(east, -east_at % 128, 1) if east_at % 128 else east
        west_shift = (126 - west_at) % 128
        west = pltpu.roll(west, west_shift, 1) if west_shift else west
        return jnp.where(lane1 < 2, east, west)

    for a in range(3):
        for s in range(species):
            side[pl.ds((a * species + s) * 8, 8), 0:128] = ghosts(a, s)

    def strip(a, first_s, count, south_rows, north_rows):
        fe, fo = 2 * a, 2 * a + 1
        ce = [coef[fe, n] for n in range(9)]
        co = [coef[fo, n] for n in range(9)]
        for u in range(count):
            s = first_s + u
            qe, qo = mixing[s, 0, slot[fe]], mixing[s, 0, slot[fo]]
            g = side[pl.ds(pl.multiple_of((a * species + s) * 8, 8), 8), 0:128]
            if width > 128:
                g = jnp.concatenate([g] * (width // 128), axis=-1)
            for q, west, east, c, parity, f in ((qe, g, qo, ce, 0, fe), (qo, qe, g, co, 1, fo)):
                sv, nv = south_rows[parity], north_rows[parity]
                sv = pltpu.roll(sv, (6 - 2 * u) % 8, 0) if (6 - 2 * u) % 8 else sv
                nv = pltpu.roll(nv, (-2 * u) % 8, 0) if u else nv
                value = c[8] * q
                value += c[0] * left(q, west, 2)
                value += c[1] * left(q, west, 1)
                value += c[2] * right(q, east, 1)
                value += c[3] * right(q, east, 2)
                value += c[4] * below(q, sv, 2)
                value += c[5] * below(q, sv, 1)
                value += c[6] * above(q, nv, 1)
                value += c[7] * above(q, nv, 2)
                result[s, slot[f]] = value

    def quad(it, count):
        for a in range(3):
            at = [south_at[p] + south_a[a] * z.group + 8 * it for p in range(2)]
            s_rows = [south[pl.ds(pl.multiple_of(x, 8), 8)] for x in at]
            at = [north_at[p] + north_a[a] * z.group + 8 * it for p in range(2)]
            n_rows = [north[pl.ds(pl.multiple_of(x, 8), 8)] for x in at]
            strip(a, 4 * it, count, s_rows, n_rows)
        part = pl.ds(4 * it, count)
        pltpu.make_async_copy(result.at[part], out.at[part, 0], out_sem).start()

    @pl.loop(0, species // 4)
    def _(it):
        quad(it, 4)

    if species % 4:
        quad(species // 4, species % 4)
    pltpu.make_async_copy(result, out.at[:, 0], out_sem).wait()


def local(mixing, layer_mass, mass_east, mass_north, face_slot):
    tiles = lax.axis_size("tile")
    halves = lax.axis_size("spec")
    z = Sizes(mixing, halves, tiles)
    assert z.rows == 8 and mixing.shape[1] == 1
    own = jnp.concatenate([layer_mass, mass_east, mass_north], axis=0)
    if halves == 2:
        other = lax.ppermute(own, "spec", [(0, 1), (1, 0)])
    else:
        other = lax.all_gather(own, "spec", axis=0, tiled=False)
    smem = pl.BlockSpec(memory_space=pltpu.SMEM)
    vmem = pl.BlockSpec(memory_space=pltpu.VMEM)
    hbm = pl.BlockSpec(memory_space=pl.ANY)
    sent = jax.ShapeDtypeStruct((z.sent, z.width), F32)
    to_a, to_b, slots_out, kept, full = pl.pallas_call(
        lambda *refs: pack_kernel(z, *refs),
        out_shape=(
            sent,
            sent,
            jax.ShapeDtypeStruct((8 * tiles, z.lanes), F32),
            jax.ShapeDtypeStruct((8, z.lanes), F32),
            jax.ShapeDtypeStruct((18, 8, z.width), F32),
        ),
        in_specs=[smem, vmem, vmem, vmem],
        out_specs=[vmem] * 5,
        name="pack",
    )(face_slot, mixing, own, other)
    arrived = lax.all_to_all(slots_out, "tile", 0, 0, tiled=True)
    from_a = lax.ppermute(to_a, "tile", [(i, i ^ 1) for i in range(tiles)])
    pairs = [(i, (i + 1) % tiles) if i % 2 else (i, (i - 1) % tiles) for i in range(tiles)]
    from_b = lax.ppermute(to_b, "tile", pairs)
    return pl.pallas_call(
        lambda *refs: step_kernel(z, *refs),
        out_shape=jax.ShapeDtypeStruct(mixing.shape, F32),
        in_specs=[smem, vmem, hbm, hbm, vmem, vmem, vmem],
        out_specs=hbm,
        scratch_shapes=[
            pltpu.VMEM((3 * z.block, z.width), F32),
            pltpu.VMEM((3 * z.block, z.width), F32),
            pltpu.VMEM((z.species * 24, z.width), F32),
            pltpu.VMEM((6, 9, 8, z.width), F32),
            pltpu.VMEM((z.species, 6, 8, z.width), F32),
            pltpu.SemaphoreType.DMA((3,)),
            pltpu.SemaphoreType.DMA,
        ],
        name="step",
    )(face_slot, mixing, from_a, from_b, arrived, kept, full)


def solution(mesh):
    flux = P(None, None, "tile", "spec")
    cells = P("spec", None, None, "tile", None)
    return jax.shard_map(
        local,
        mesh=mesh,
        in_specs=(cells, flux, flux, flux, P()),
        out_specs=cells,
        check_vma=False,
    )
```

```python
import jax
import jax.numpy as jnp
from jax import lax
from jax.experimental import pallas as pl
from jax.experimental.pallas import tpu as pltpu
from jax.sharding import PartitionSpec as P

F32 = jnp.float32
VMEM_LIMIT = 12 << 20


def up(value, unit):
    return -(-value // unit) * unit


class Sizes:
    def __init__(self, mixing, halves, tiles):
        self.species, _, _, self.rows, self.width = mixing.shape
        self.tiles, self.halves = tiles, halves
        self.part = self.width // halves
        self.group = up(2 * self.species, 8)
        self.flux = 3 * self.group
        self.flux2 = self.flux + 8
        self.lanes = up(self.flux2 + 8, 128)
        self.vregs = self.lanes // 128
        self.dp_at = 2 * self.flux
        self.fy_at = self.dp_at + 8
        self.extra = self.fy_at + 8
        self.sent = self.extra + 8 * self.vregs
        self.per = 128 // self.part
        self.own = up(18, self.per) // self.per
        self.chunks = 4


def slots(face_slot):
    return [sum(jnp.where(face_slot[s] == f, s, 0) for s in range(6)) for f in range(6)]


def roll(x, shift, axis):
    shift %= x.shape[axis]
    return pltpu.roll(x, shift, axis) if shift else x


def reverse8(x):
    row = lax.broadcasted_iota(jnp.int32, x.shape, 0)
    x = jnp.where((row & 1) == 0, roll(x, -1, 0), roll(x, 1, 0))
    x = jnp.where((row & 2) == 0, roll(x, -2, 0), roll(x, 2, 0))
    return roll(x, 4, 0)


def pack_kernel(
    z, face_slot, mixing_in, dp_in, fx_in, fy_in, to_a, to_b, out, kept, full, own, order, mixing, fluxes, sems
):
    cuts = [z.species * n // z.chunks for n in range(z.chunks + 1)]
    copies = [
        pltpu.make_async_copy(ref, fluxes.at[c], sems.at[c]) for c, ref in enumerate((dp_in, fx_in, fy_in))
    ]
    for n in range(z.chunks):
        some = pl.ds(cuts[n], cuts[n + 1] - cuts[n])
        copies.append(pltpu.make_async_copy(mixing_in.at[some], mixing.at[some], sems.at[3 + n]))
    for copy in copies:
        copy.start()
    place = lax.axis_index("tile")
    half = lax.axis_index("spec")
    slot = slots(face_slot)
    even = lax.rem(place, 2) == 0
    first, last = place == 0, place == z.tiles - 1
    width, part, species, n_half = z.width, z.part, z.species, z.halves
    places = lax.broadcasted_iota(jnp.int32, (8, 128), 1)
    order[...] = sum(jnp.where(places == f, slot[f], 0) for f in range(6))
    for copy in copies[:3]:
        copy.wait()
    raw = [[fluxes[c, 0, slot[f]] for f in range(6)] for c in range(3)]

    def placed(x):
        return jnp.concatenate([jnp.where(half == n, x, 0.0) for n in range(n_half)], axis=-1)

    for c in range(3):
        for f in range(6):
            full[c * 6 + f] = placed(raw[c][f])
    flat = [raw[c][f] for c in range(3) for f in range(6)]
    for n in range(z.own):
        tiles = flat[n * z.per : (n + 1) * z.per]
        tiles += [tiles[0]] * (z.per - len(tiles))
        own[n] = jnp.concatenate(tiles, axis=-1) if z.per > 1 else tiles[0]

    def both(low, high, at):
        to_a[pl.ds(at, low.shape[0])] = jnp.where(even, high, low)
        to_b[pl.ds(at, low.shape[0])] = jnp.where(even, low, high)

    pad = jnp.zeros((2, part), F32)
    low_dp = jnp.concatenate([x[0:1] for x in raw[0]] + [pad], axis=0)
    high_dp = jnp.concatenate([x[7:8] for x in raw[0]] + [pad], axis=0)
    low_fy = jnp.concatenate([x[0:1] for x in raw[2]] + [pad], axis=0)
    both(placed(low_dp), placed(high_dp), z.dp_at)
    both(placed(low_fy), placed(low_fy), z.fy_at)

    lane = lax.broadcasted_iota(jnp.int32, (8, 128), 1)
    gathers = [[jnp.zeros((8, 128), F32) for _ in range(z.vregs)] for _ in range(2)]
    for parity in range(2):
        for a in range(3):
            f = 2 * a + parity
            if z.group > 2 * species:
                zero = jnp.zeros((z.group - 2 * species, width), F32)
                both(zero, zero, parity * z.flux + a * z.group + 2 * species)
            for c in range(2):
                at = z.flux2 + 3 * c + a
                tile = full[c * 6 + f]
                edge = tile[:, :128] if parity == 0 else tile[:, width - 128 :]
                moved = roll(edge, at - (0 if parity == 0 else 127), 1)
                k = at // 128
                gathers[parity][k] = jnp.where(lane == at % 128, moved, gathers[parity][k])
    for n in range(z.chunks):
        copies[3 + n].wait()
        for s in range(cuts[n], cuts[n + 1]):
            for f in range(6):
                a, parity = f // 2, f % 2
                tile = mixing[s, 0, slot[f]]
                at = a * z.group + 2 * s
                both(tile[0:2], tile[6:8], parity * z.flux + at)
                edge = tile[:, :128] if parity == 0 else tile[:, width - 128 :]
                moved = roll(edge, at - (0 if parity == 0 else 126), 1)
                k = at // 128
                gathers[parity][k] = jnp.where((lane >> 1) == (at % 128) // 2, moved, gathers[parity][k])
    gathers = [[reverse8(x) for x in lanes] for lanes in gathers]
    for k in range(z.vregs):
        even_cols, odd_cols = gathers[0][k], gathers[1][k]
        kept[:, k * 128 : (k + 1) * 128] = jnp.where(first, odd_cols, even_cols)
        spare = jnp.where(first, even_cols, odd_cols)
        spare = jnp.concatenate([spare] * (width // 128), axis=-1) if width > 128 else spare
        to_a[pl.ds(z.extra + 8 * k, 8)] = spare
        to_b[pl.ds(z.extra + 8 * k, 8)] = spare

    ends = ((0, gathers[1]), (z.tiles - 1, gathers[0]))

    @pl.when(first | last)
    def _():
        start = pl.multiple_of(jnp.where(first, z.flux, 0), 8)
        edge_rows = [
            jnp.where(first, raw[c][2 * a + 1][0:1], raw[c][2 * a][7:8]) for c in (0, 2) for a in range(3)
        ]
        rows = [
            to_b[pl.ds(start, z.flux)],
            placed(jnp.concatenate(edge_rows + [pad], axis=0)),
            jnp.zeros((z.lanes - z.flux - 8, width), F32),
        ]
        turned = jnp.concatenate(rows, axis=0).T
        for t in range(z.tiles):
            at = 8 * (z.tiles - 1 - t)
            for n in range(n_half):
                out[t * n_half + n] = turned[at : at + 8]
        for t, cols in ends:
            at = 8 * (z.tiles - 1 - t)
            k = z.flux2 // 128
            here = (lane >= z.flux2 % 128) & (lane < z.flux2 % 128 + 8)
            mixed = jnp.where(here, cols[k], turned[at : at + 8, k * 128 : (k + 1) * 128])
            for n in range(n_half):
                out[t * n_half + n, :, k * 128 : (k + 1) * 128] = mixed

    @pl.when(jnp.logical_not(first | last))
    def _():
        for t, cols in ends:
            for n in range(n_half):
                for k in range(z.vregs):
                    out[t * n_half + n, :, k * 128 : (k + 1) * 128] = cols[k]

    north = lax.rem(place + 1, z.tiles) * n_half
    south = lax.rem(place + z.tiles - 1, z.tiles) * n_half
    for d in range(1, n_half):
        other = lax.rem(half + d, n_half)
        out[north + other, :, 0 : 2 * part] = jnp.concatenate([high_dp, high_dp], axis=-1)
        out[south + other, :, 0 : 2 * part] = jnp.concatenate([low_dp, low_fy], axis=-1)


def step_kernel(
    z, order_in, mixing, from_a, from_b, arrived, kept, full_in, others, out,
    order, south, north, turned, side, coef, result, order_sem, out_sem,
):
    place = lax.axis_index("tile")
    half = lax.axis_index("spec")
    fetch = pltpu.make_async_copy(order_in, order, order_sem)
    fetch.start()
    even = lax.rem(place, 2) == 0
    first = place == 0
    last = place == z.tiles - 1
    width, part, species, n_half = z.width, z.part, z.species, z.halves
    lane = lax.broadcasted_iota(jnp.int32, (8, width), 1)
    row = lax.broadcasted_iota(jnp.int32, (8, width), 0)
    lane1 = lax.broadcasted_iota(jnp.int32, (8, 128), 1)

    halo = z.dp_at
    a_rows, b_rows = from_a[0:halo], from_b[0:halo]
    south[0:halo] = jnp.where(even, b_rows, a_rows)
    north[0:halo] = jnp.where(even, a_rows, b_rows)

    @pl.when(first | last)
    def _():
        holder = jnp.where(first, n_half - 1, 0)
        pieces = []
        for k in range(z.vregs):
            lanes = slice(k * 128, (k + 1) * 128)
            spare = from_b[z.extra + 8 * k : z.extra + 8 * k + 8, 0:128]
            mine = kept[:, lanes]
            parts = []
            for t in reversed(range(z.tiles)):
                if t == 0:
                    x = jnp.where(first, mine, spare)
                elif t == z.tiles - 1:
                    x = jnp.where(first, spare, mine)
                else:
                    x = arrived[t * n_half + half, :, lanes]
                if (k + 1) * 128 > z.flux:
                    x = jnp.where(lane1 + k * 128 < z.flux, x, arrived[t * n_half + holder, :, lanes])
                parts.append(x)
            pieces.append(jnp.concatenate(parts, axis=0).T)
        ghost = jnp.concatenate(pieces, axis=0) if len(pieces) > 1 else pieces[0]

        @pl.when(first)
        def _():
            south[halo : halo + z.flux] = ghost[: z.flux]

        @pl.when(last)
        def _():
            north[halo : halo + z.flux] = ghost[: z.flux]

        turned[...] = ghost[z.flux2 : z.flux2 + 8]

    full = []
    for n in range(18):
        at = (n % z.per) * part
        if n_half == 2:
            x = others[n // z.per][:, at : at + part]
            rest = jnp.concatenate([jnp.where(half == h, 0.0, x) for h in range(2)], axis=-1)
            full.append(full_in[n] + rest)
        else:
            full.append(
                jnp.concatenate([others[h, n // z.per][:, at : at + part] for h in range(n_half)], axis=-1)
            )

    def edge_rows(neighbour, which, mine):
        total = mine
        for n in range(n_half):
            x = arrived[neighbour * n_half + n, :, 0:128]
            x = jnp.concatenate([x] * (width // 128), axis=-1) if width > 128 else x
            x = roll(x, (n - which) * part, 1)
            total = jnp.where((lane >= n * part) & (lane < (n + 1) * part) & (half != n), x, total)
        return total

    below_tile = lax.rem(place + z.tiles - 1, z.tiles)
    above_tile = lax.rem(place + 1, z.tiles)
    a_dp, b_dp = from_a[z.dp_at : z.dp_at + 8], from_b[z.dp_at : z.dp_at + 8]
    a_fy, b_fy = from_a[z.fy_at : z.fy_at + 8], from_b[z.fy_at : z.fy_at + 8]
    dp_south = edge_rows(below_tile, 0, jnp.where(even, b_dp, a_dp))
    dp_north = edge_rows(above_tile, 0, jnp.where(even, a_dp, b_dp))
    fy_north = edge_rows(above_tile, 1, jnp.where(even, a_fy, b_fy))
    gathered = turned[...]

    block = z.flux
    south_at = [jnp.where(first, block, 0), jnp.where(first, 2 * block, block)]
    north_at = [jnp.where(last, 2 * block, 0), jnp.where(last, 0, block)]
    south_a = [jnp.where(first, (a + 2) % 3, a) for a in range(3)]
    north_a = [jnp.where(last, (a + 1) % 3, a) for a in range(3)]

    def come(end, holder):
        tracer = [reverse8(arrived[end * n_half + half, :, k * 128 : (k + 1) * 128]) for k in range(z.vregs)]
        k = z.flux // 128
        return tracer, reverse8(arrived[end * n_half + holder, :, k * 128 : (k + 1) * 128])

    holder = lax.div(width - 8 - 8 * place, part)
    east_cols, east_flux = come(0, holder)
    west_cols, west_flux = come(z.tiles - 1, holder)

    def column(flux, n):
        at = (z.flux + n) % 128
        return flux[:, at : at + 1]

    def left(x, ghost, n):
        return pltpu.roll(jnp.where(lane >= width - n, ghost, x), n, 1)

    def right(x, ghost, n):
        return pltpu.roll(jnp.where(lane < n, ghost, x), width - n, 1)

    def below(x, ghost, n):
        return pltpu.roll(jnp.where(row >= 8 - n, ghost, x), n, 0)

    def above(x, ghost, n):
        return pltpu.roll(jnp.where(row < n, ghost, x), 8 - n, 0)

    def upwind(u, total):
        return 0.5 * jnp.abs(u) * (1.0 - jnp.abs(u / (0.5 * total)))

    for f in range(6):
        a, parity = f // 2, f % 2
        dp, fx, fy = full[f], full[6 + f], full[12 + f]
        if parity == 0:
            west = column(west_flux, (a + 2) % 3)
            east, east_u = full[f + 1], full[6 + f + 1]
            s_end = roll(dp_south, 7 - (f - 1) % 6, 0)
            n_end = [roll(gathered, -((a + 1) % 3) - 3 * c, 0) for c in range(2)]
        else:
            west = full[f - 1]
            east = column(east_flux, (a + 1) % 3)
            east_u = column(east_flux, 3 + (a + 1) % 3)
            s_end = roll(gathered, 7 - (a + 2) % 3, 0)
            n_end = [roll(x, -((f + 1) % 6), 0) for x in (dp_north, fy_north)]
        dp_w, dp_e = left(dp, west, 1), right(dp, east, 1)
        u0, u1 = fx, right(fx, east_u, 1)
        dp_s = below(dp, jnp.where(first, s_end, roll(dp_south, 7 - f, 0)), 1)
        dp_n = above(dp, jnp.where(last, n_end[0], roll(dp_north, -f, 0)), 1)
        v0, v1 = fy, above(fy, jnp.where(last, n_end[1], roll(fy_north, -f, 0)), 1)
        inverse = 1.0 / (dp - (u1 - u0) - (v1 - v0))
        center = dp
        for n, (w0, w1, d0, d1) in enumerate(((u0, u1, dp_w, dp_e), (v0, v1, dp_s, dp_n))):
            b0, b1 = upwind(w0, d0 + dp), upwind(w1, dp + d1)
            p0, p1 = w0 * (1.0 / 12.0), w1 * (1.0 / 12.0)
            coef[f, 4 * n] = -p0 * inverse
            coef[f, 4 * n + 1] = (7.0 * p0 + b0 + p1) * inverse
            coef[f, 4 * n + 2] = (-p0 - 7.0 * p1 + b1) * inverse
            coef[f, 4 * n + 3] = p1 * inverse
            center = center + (7.0 * p0 - b0) - (7.0 * p1 + b1)
        coef[f, 8] = center * inverse

    for a in range(3):
        for s in range(species):
            east_at = ((a + 1) % 3) * z.group + 2 * s
            west_at = ((a + 2) % 3) * z.group + 2 * s
            east = roll(east_cols[east_at // 128], -east_at, 1)
            west = roll(west_cols[west_at // 128], 126 - west_at, 1)
            side[a * species + s] = jnp.where(lane1 < 2, east, west)

    fetch.wait()
    slot = [order[0, f] for f in range(6)]

    def strip(a, first_s, count, south_rows, north_rows):
        fe, fo = 2 * a, 2 * a + 1
        ce = [coef[fe, n] for n in range(9)]
        co = [coef[fo, n] for n in range(9)]
        for u in range(count):
            s = first_s + u
            qe, qo = mixing[s, 0, slot[fe]], mixing[s, 0, slot[fo]]
            g = side[a * species + s]
            g = jnp.concatenate([g] * (width // 128), axis=-1) if width > 128 else g
            for q, west, east, c, parity, f in ((qe, g, qo, ce, 0, fe), (qo, qe, g, co, 1, fo)):
                sv = roll(south_rows[parity], 6 - 2 * u, 0)
                nv = roll(north_rows[parity], -2 * u, 0)
                value = c[8] * q
                value += c[0] * left(q, west, 2)
                value += c[1] * left(q, west, 1)
                value += c[2] * right(q, east, 1)
                value += c[3] * right(q, east, 2)
                value += c[4] * below(q, sv, 2)
                value += c[5] * below(q, sv, 1)
                value += c[6] * above(q, nv, 1)
                value += c[7] * above(q, nv, 2)
                result[s, slot[f]] = value

    def quad(it, count):
        for a in range(3):
            at = [south_at[p] + south_a[a] * z.group + 8 * it for p in range(2)]
            s_rows = [south[pl.ds(pl.multiple_of(x, 8), 8)] for x in at]
            at = [north_at[p] + north_a[a] * z.group + 8 * it for p in range(2)]
            n_rows = [north[pl.ds(pl.multiple_of(x, 8), 8)] for x in at]
            strip(a, 4 * it, count, s_rows, n_rows)
        part = pl.ds(4 * it, count)
        pltpu.make_async_copy(result.at[part], out.at[part, 0], out_sem).start()

    @pl.loop(0, species // 4)
    def _(it):
        quad(it, 4)

    if species % 4:
        quad(species // 4, species % 4)
    pltpu.make_async_copy(result, out.at[:, 0], out_sem).wait()


def local(mixing, layer_mass, mass_east, mass_north, face_slot):
    tiles = lax.axis_size("tile")
    halves = lax.axis_size("spec")
    z = Sizes(mixing, halves, tiles)
    assert z.rows == 8 and mixing.shape[1] == 1 and tiles > 2 and tiles % 2 == 0
    assert z.width == 8 * tiles and z.width % 128 == 0 and 128 % z.part == 0 and 2 * z.part <= z.flux
    smem = pl.BlockSpec(memory_space=pltpu.SMEM)
    vmem = pl.BlockSpec(memory_space=pltpu.VMEM)
    params = pltpu.CompilerParams(vmem_limit_bytes=VMEM_LIMIT)

    def f32(*shape):
        return jax.ShapeDtypeStruct(shape, F32)

    to_a, to_b, messages, kept, full, own, order = pl.pallas_call(
        lambda *refs: pack_kernel(z, *refs),
        out_shape=(
            f32(z.sent, z.width),
            f32(z.sent, z.width),
            f32(tiles * halves, 8, z.lanes),
            f32(8, z.lanes),
            f32(18, 8, z.width),
            f32(z.own, 8, 128),
            jax.ShapeDtypeStruct((8, 128), jnp.int32),
        ),
        in_specs=[smem] + [pl.BlockSpec(memory_space=pltpu.HBM)] * 4,
        out_specs=[vmem] * 7,
        scratch_shapes=[
            pltpu.VMEM(mixing.shape, F32),
            pltpu.VMEM((3,) + layer_mass.shape, F32),
            pltpu.SemaphoreType.DMA((3 + z.chunks,)),
        ],
        name="pack",
    )(face_slot, mixing, layer_mass, mass_east, mass_north)
    arrived = lax.all_to_all(messages, ("tile", "spec"), 0, 0, tiled=True)
    if halves == 2:
        others = lax.ppermute(own, "spec", [(0, 1), (1, 0)])
    else:
        others = lax.all_gather(own, "spec", axis=0, tiled=False)
    from_a = lax.ppermute(to_a, "tile", [(i, i ^ 1) for i in range(tiles)])
    pairs = [(i, (i + 1) % tiles) if i % 2 else (i, (i - 1) % tiles) for i in range(tiles)]
    from_b = lax.ppermute(to_b, "tile", pairs)
    return pl.pallas_call(
        lambda *refs: step_kernel(z, *refs),
        out_shape=f32(*mixing.shape),
        in_specs=[vmem] * 8,
        out_specs=pl.BlockSpec(memory_space=pl.ANY),
        scratch_shapes=[
            pltpu.SMEM((8, 128), jnp.int32),
            pltpu.VMEM((3 * z.flux, z.width), F32),
            pltpu.VMEM((3 * z.flux, z.width), F32),
            pltpu.VMEM((8, z.width), F32),
            pltpu.VMEM((3 * z.species, 8, 128), F32),
            pltpu.VMEM((6, 9, 8, z.width), F32),
            pltpu.VMEM((z.species, 6, 8, z.width), F32),
            pltpu.SemaphoreType.DMA,
            pltpu.SemaphoreType.DMA,
        ],
        compiler_params=params,
        name="step",
    )(order, mixing, from_a, from_b, arrived, kept, full, others)


def solution(mesh):
    flux = P(None, None, "tile", "spec")
    cells = P("spec", None, None, "tile", None)
    return jax.shard_map(
        local,
        mesh=mesh,
        in_specs=(cells, flux, flux, flux, P()),
        out_specs=cells,
        check_vma=False,
    )
```

```python
import jax
import jax.numpy as jnp
from jax import lax
from jax.experimental import pallas as pl
from jax.experimental.pallas import tpu as pltpu
from jax.sharding import PartitionSpec as P

F32 = jnp.float32
VMEM_LIMIT = 12 << 20
CHUNKS = 2
OUT_CHUNKS = 4


def up(value, unit):
    return -(-value // unit) * unit


class Sizes:
    def __init__(self, mixing, halves, tiles):
        self.species, _, _, self.rows, self.width = mixing.shape
        self.tiles, self.halves = tiles, halves
        self.part = self.width // halves
        self.group = up(2 * self.species, 8)
        self.flux = 3 * self.group
        self.flux2 = self.flux + 8
        self.lanes = up(self.flux2 + 8, 128)
        self.vregs = self.lanes // 128
        self.dp_at = 2 * self.flux
        self.fy_at = self.dp_at + 8
        self.extra = self.fy_at + 8
        self.sent = self.extra + 8 * self.vregs
        self.per = 128 // self.part
        self.own = up(18, self.per) // self.per
        self.pieces = 21
        self.shared = up(self.pieces, self.per) // self.per


def slots(face_slot):
    return [sum(jnp.where(face_slot[s] == f, s, 0) for s in range(6)) for f in range(6)]


def roll(x, shift, axis):
    shift %= x.shape[axis]
    return pltpu.roll(x, shift, axis) if shift else x


def reverse8(x):
    row = lax.broadcasted_iota(jnp.int32, x.shape, 0)
    x = jnp.where((row & 1) == 0, roll(x, -1, 0), roll(x, 1, 0))
    x = jnp.where((row & 2) == 0, roll(x, -2, 0), roll(x, 2, 0))
    return roll(x, 4, 0)


def upwind(u, total):
    return 0.5 * jnp.abs(u) * (1.0 - jnp.abs(u / (0.5 * total)))


def wide(x, width):
    return jnp.concatenate([x] * (width // 128), axis=-1) if width > 128 else x


def side_by_side(tiles, per):
    tiles = tiles + [tiles[0]] * (per - len(tiles))
    return jnp.concatenate(tiles, axis=-1) if per > 1 else tiles[0]


def pack_kernel(
    z, slot_in, mixing_in, dp_in, fx_in, fy_in,
    to_a, to_b, out, edges, own, order, face_slot, mixing, fluxes, sems,
):
    cuts = [z.species * n // CHUNKS for n in range(CHUNKS + 1)]
    copies = [pltpu.make_async_copy(slot_in, face_slot, sems.at[0])]
    for c, ref in enumerate((dp_in, fx_in, fy_in)):
        copies.append(pltpu.make_async_copy(ref, fluxes.at[c], sems.at[1 + c]))
    for n in range(CHUNKS):
        some = pl.ds(cuts[n], cuts[n + 1] - cuts[n])
        copies.append(pltpu.make_async_copy(mixing_in.at[some], mixing.at[some], sems.at[4 + n]))
    for copy in copies:
        copy.start()
    place = lax.axis_index("tile")
    half = lax.axis_index("spec")
    copies[0].wait()
    slot = slots(face_slot)
    even = lax.rem(place, 2) == 0
    first, last = place == 0, place == z.tiles - 1
    width, part, species, n_half = z.width, z.part, z.species, z.halves
    lane = lax.broadcasted_iota(jnp.int32, (8, 128), 1)
    order[...] = sum(jnp.where(lane == f, slot[f], 0) for f in range(6))
    for copy in copies[1:4]:
        copy.wait()
    raw = [[fluxes[c, 0, slot[f]] for f in range(6)] for c in range(3)]
    flat = [raw[c][f] for c in range(3) for f in range(6)]
    for n in range(z.own):
        own[n] = side_by_side(flat[n * z.per : (n + 1) * z.per], z.per)

    def both(low, high, at):
        to_a[pl.ds(at, low.shape[0])] = jnp.where(even, high, low)
        to_b[pl.ds(at, low.shape[0])] = jnp.where(even, low, high)

    def padded(x):
        return jnp.concatenate([x, jnp.zeros((8, width - part), F32)], axis=-1) if width > part else x

    pad = jnp.zeros((2, part), F32)
    low_dp = jnp.concatenate([x[0:1] for x in raw[0]] + [pad], axis=0)
    high_dp = jnp.concatenate([x[7:8] for x in raw[0]] + [pad], axis=0)
    low_fy = padded(jnp.concatenate([x[0:1] for x in raw[2]] + [pad], axis=0))
    both(padded(low_dp), padded(high_dp), z.dp_at)
    both(low_fy, low_fy, z.fy_at)

    columns = [[jnp.zeros((8, 128), F32) for _ in range(z.vregs)] for _ in range(2)]
    for parity in range(2):
        for a in range(3):
            f = 2 * a + parity
            if z.group > 2 * species:
                zero = jnp.zeros((z.group - 2 * species, width), F32)
                both(zero, zero, parity * z.flux + a * z.group + 2 * species)
            for c in range(2):
                at = z.flux2 + 3 * c + a
                edge = side_by_side([raw[c][f]] * z.per, z.per)
                moved = roll(edge, at - (0 if parity == 0 else 127), 1)
                k = at // 128
                columns[parity][k] = jnp.where(lane == at % 128, moved, columns[parity][k])
    for n in range(CHUNKS):
        copies[4 + n].wait()
        for s in range(cuts[n], cuts[n + 1]):
            for f in range(6):
                a, parity = f // 2, f % 2
                tile = mixing[s, 0, slot[f]]
                at = a * z.group + 2 * s
                both(tile[0:2], tile[6:8], parity * z.flux + at)
                edge = tile[:, :128] if parity == 0 else tile[:, width - 128 :]
                moved = roll(edge, at - (0 if parity == 0 else 126), 1)
                k = at // 128
                columns[parity][k] = jnp.where((lane >> 1) == (at % 128) // 2, moved, columns[parity][k])
    turned = [[reverse8(x) for x in lanes] for lanes in columns]
    for k in range(z.vregs):
        for parity in range(2):
            edges[parity, :, k * 128 : (k + 1) * 128] = columns[parity][k]
        spare = wide(jnp.where(first, turned[0][k], turned[1][k]), width)
        to_a[pl.ds(z.extra + 8 * k, 8)] = spare
        to_b[pl.ds(z.extra + 8 * k, 8)] = spare

    ends = ((0, turned[1]), (z.tiles - 1, turned[0]))

    @pl.when(first | last)
    def _():
        rows, dps, fys = [], [], []
        for a in range(3):
            for_odd, for_even = (a + 1) % 3, (a + 2) % 3
            start = jnp.where(first, z.flux + for_odd * z.group, for_even * z.group)
            rows.append(to_b[pl.ds(pl.multiple_of(start, 8), z.group)])
            for c, values in ((0, dps), (2, fys)):
                values.append(jnp.where(first, raw[c][2 * for_odd + 1][0:1], raw[c][2 * for_even][7:8]))
        flux = jnp.concatenate(dps + fys + [pad], axis=0)
        flux = jnp.concatenate([jnp.where(half == n, flux, 0.0) for n in range(n_half)], axis=-1)
        rows += [flux, jnp.zeros((z.lanes - z.flux - 8, width), F32)]
        messages = jnp.concatenate(rows, axis=0).T
        for t in range(z.tiles):
            at = 8 * (z.tiles - 1 - t)
            for n in range(n_half):
                out[t * n_half + n] = messages[at : at + 8]
        for t, cols in ends:
            at = 8 * (z.tiles - 1 - t)
            k = z.flux2 // 128
            here = (lane >= z.flux2 % 128) & (lane < z.flux2 % 128 + 8)
            mixed = jnp.where(here, cols[k], messages[at : at + 8, k * 128 : (k + 1) * 128])
            for n in range(n_half):
                out[t * n_half + n, :, k * 128 : (k + 1) * 128] = mixed

    @pl.when(jnp.logical_not(first | last))
    def _():
        for t, cols in ends:
            for n in range(n_half):
                for k in range(z.vregs):
                    out[t * n_half + n, :, k * 128 : (k + 1) * 128] = cols[k]


def share_kernel(z, own, from_a, from_b, out):
    even = lax.rem(lax.axis_index("tile"), 2) == 0
    part = z.part
    dp_a, dp_b = from_a[z.dp_at : z.dp_at + 8, :part], from_b[z.dp_at : z.dp_at + 8, :part]
    fy_a, fy_b = from_a[z.fy_at : z.fy_at + 8, :part], from_b[z.fy_at : z.fy_at + 8, :part]
    halo = [jnp.where(even, dp_b, dp_a), jnp.where(even, dp_a, dp_b), jnp.where(even, fy_a, fy_b)]
    flat = [own[n // z.per][:, (n % z.per) * part : (n % z.per + 1) * part] for n in range(18)] + halo
    for n in range(z.shared):
        out[n] = side_by_side(flat[n * z.per : (n + 1) * z.per], z.per)


def interior_kernel(
    z, order_in, mixing, from_a, from_b, mine, others, partial, ends, aux,
    order, south, north, coef, order_sem,
):
    fetch = pltpu.make_async_copy(order_in, order, order_sem)
    fetch.start()
    place = lax.axis_index("tile")
    half = lax.axis_index("spec")
    even = lax.rem(place, 2) == 0
    first, last = place == 0, place == z.tiles - 1
    width, part, species = z.width, z.part, z.species
    lane = lax.broadcasted_iota(jnp.int32, (8, width), 1)
    row = lax.broadcasted_iota(jnp.int32, (8, width), 0)
    lane1 = lax.broadcasted_iota(jnp.int32, (8, 128), 1)

    a_rows, b_rows = from_a[0 : z.dp_at], from_b[0 : z.dp_at]
    south[...] = jnp.where(even, b_rows, a_rows)
    north[...] = jnp.where(even, a_rows, b_rows)

    full = []
    for n in range(z.pieces):
        cut = slice((n % z.per) * part, (n % z.per + 1) * part)
        if z.halves == 2:
            x, y = mine[n // z.per][:, cut], others[n // z.per][:, cut]
            parts = [jnp.where(half == 0, x, y), jnp.where(half == 0, y, x)]
        else:
            parts = [others[h, n // z.per][:, cut] for h in range(z.halves)]
        full.append(jnp.concatenate(parts, axis=-1))
    dp_south, dp_north, fy_north = full[18:]

    def left(x, ghost, n):
        return pltpu.roll(jnp.where(lane >= width - n, ghost, x), n, 1)

    def right(x, ghost, n):
        return pltpu.roll(jnp.where(lane < n, ghost, x), width - n, 1)

    def below(x, ghost, n):
        return pltpu.roll(jnp.where(row >= 8 - n, ghost, x), n, 0)

    def above(x, ghost, n):
        return pltpu.roll(jnp.where(row < n, ghost, x), 8 - n, 0)

    for f in range(6):
        parity = f % 2
        dp, fx, fy = full[f], full[6 + f], full[12 + f]
        if parity == 0:
            west, east, east_u = dp, full[f + 1], full[6 + f + 1]
            s_end, n_end, v_end = roll(dp_south, 7 - (f - 1) % 6, 0), dp, 0.0
            known = jnp.logical_not(last & (row == 7))
        else:
            west, east, east_u = full[f - 1], dp, 0.0
            s_end, n_end, v_end = dp, roll(dp_north, -((f + 1) % 6), 0), roll(fy_north, -((f + 1) % 6), 0)
            known = lane < width - 1
        dp_w, dp_e = left(dp, west, 1), right(dp, east, 1)
        u0, u1 = fx, right(fx, east_u, 1)
        dp_s = below(dp, jnp.where(first, s_end, roll(dp_south, 7 - f, 0)), 1)
        dp_n = above(dp, jnp.where(last, n_end, roll(dp_north, -f, 0)), 1)
        v0, v1 = fy, above(fy, jnp.where(last, v_end, roll(fy_north, -f, 0)), 1)
        new = dp - (u1 - u0) - (v1 - v0)
        inverse = jnp.where(known, 1.0 / jnp.where(known, new, 1.0), 1.0)
        for n, x in enumerate((fx, dp, inverse, new, v0, v1)):
            aux[f, n] = x
        center = dp
        for n, (w0, w1, d0, d1) in enumerate(((u0, u1, dp_w, dp_e), (v0, v1, dp_s, dp_n))):
            b0, b1 = upwind(w0, d0 + dp), upwind(w1, dp + d1)
            if n == 0 and parity == 0:
                b0 = jnp.where(lane == 0, 0.0, b0)
            if n == 1 and parity == 1:
                b0 = jnp.where(first & (row == 0), 0.0, b0)
            p0, p1 = w0 * (1.0 / 12.0), w1 * (1.0 / 12.0)
            coef[f, 4 * n] = -p0 * inverse
            coef[f, 4 * n + 1] = (7.0 * p0 + b0 + p1) * inverse
            coef[f, 4 * n + 2] = (-p0 - 7.0 * p1 + b1) * inverse
            coef[f, 4 * n + 3] = p1 * inverse
            center = center + (7.0 * p0 - b0) - (7.0 * p1 + b1)
        coef[f, 8] = center * inverse

    block = z.flux
    south_at, north_at = jnp.where(first, block, 0), jnp.where(last, 0, block)
    fetch.wait()
    slot = [order[0, f] for f in range(6)]

    def quad(it, count):
        for a in range(3):
            a_s, a_n = jnp.where(first, (a + 2) % 3, a), jnp.where(last, (a + 1) % 3, a)

            def ghosts(ref, at, ref_a):
                return ref[pl.ds(pl.multiple_of(at + ref_a * z.group + 8 * it, 8), 8)]

            south_rows = [ghosts(south, south_at, a_s), jnp.where(first, 0.0, ghosts(south, block, a))]
            north_rows = [jnp.where(last, 0.0, ghosts(north, 0, a)), ghosts(north, north_at, a_n)]
            fe, fo = 2 * a, 2 * a + 1
            ce = [coef[fe, n] for n in range(9)]
            co = [coef[fo, n] for n in range(9)]
            for u in range(count):
                s = 4 * it + u
                qe, qo = mixing[s, 0, slot[fe]], mixing[s, 0, slot[fo]]
                for q, west, east, c, parity, f in ((qe, 0.0, qo, ce, 0, fe), (qo, qe, 0.0, co, 1, fo)):
                    sv = roll(south_rows[parity], 6 - 2 * u, 0)
                    nv = roll(north_rows[parity], -2 * u, 0)
                    value = c[8] * q
                    value += c[0] * left(q, west, 2)
                    value += c[1] * left(q, west, 1)
                    value += c[2] * right(q, east, 1)
                    value += c[3] * right(q, east, 2)
                    value += c[4] * below(q, sv, 2)
                    value += c[5] * below(q, sv, 1)
                    value += c[6] * above(q, nv, 1)
                    value += c[7] * above(q, nv, 2)
                    partial[s, f] = value

    @pl.loop(0, species // 4)
    def _(it):
        quad(it, 4)

    if species % 4:
        quad(species // 4, species % 4)

    lanes = [[jnp.zeros((8, 128), F32) for _ in range(z.vregs)] for _ in range(2)]
    for s in range(species):
        for f in range(6):
            a, parity = f // 2, f % 2
            at = a * z.group + 2 * s
            cut = slice(0, 128) if parity == 0 else slice(width - 128, width)
            moved = roll(partial[s, f, :, cut], at - (0 if parity == 0 else 126), 1)
            k = at // 128
            lanes[parity][k] = jnp.where((lane1 >> 1) == (at % 128) // 2, moved, lanes[parity][k])
    for parity in range(2):
        for k in range(z.vregs):
            ends[parity, :, k * 128 : (k + 1) * 128] = lanes[parity][k]


def finish_kernel(
    z, order_in, mixing, from_b, partial, ends, aux, edges, arrived, out,
    order, turned, fixed, result, order_sem, out_sem,
):
    fetch = pltpu.make_async_copy(order_in, order, order_sem)
    fetch.start()
    place = lax.axis_index("tile")
    half = lax.axis_index("spec")
    first, last = place == 0, place == z.tiles - 1
    width, part, species, n_half = z.width, z.part, z.species, z.halves
    lane = lax.broadcasted_iota(jnp.int32, (8, width), 1)
    row = lax.broadcasted_iota(jnp.int32, (8, width), 0)
    lane1 = lax.broadcasted_iota(jnp.int32, (8, 128), 1)
    twelfth = 1.0 / 12.0
    holder = lax.div(width - 8 - 8 * place, part)

    def column(x, at):
        return x[:, at : at + 1]

    def spread(values, k):
        at = lane1 + k * 128
        return jnp.where(at < z.group, values[0], jnp.where(at < 2 * z.group, values[1], values[2]))

    last_column = []
    odd_end = (lane1 & 1) == 1
    for parity in range(2):
        end = z.tiles - 1 if parity == 0 else 0
        flux = reverse8(arrived[end * n_half + holder, :, (z.flux // 128) * 128 : (z.flux // 128 + 1) * 128])
        mul = []
        for a in range(3):
            f = 2 * a + parity
            fx, dp, inverse, new = (aux[f, n] for n in range(4))
            ghost_dp = column(flux, z.flux % 128 + a)
            if parity == 0:
                u0, p1 = column(fx, 0), column(fx, 1) * twelfth
                p0, b0 = u0 * twelfth, upwind(u0, ghost_dp + column(dp, 0))
                i0, i1 = column(inverse, 0), column(inverse, 1)
                mul.append((-p0 * i0, -p1 * i1, (7.0 * p0 + b0 + p1) * i0, -b0 * i0))
            else:
                u1 = column(flux, z.flux % 128 + 3 + a)
                p1, b1 = u1 * twelfth, upwind(u1, column(dp, width - 1) + ghost_dp)
                p0 = column(fx, width - 1) * twelfth
                i1 = 1.0 / (column(new, width - 1) - u1)
                last_column.append(i1)
                mul.append(
                    (p0 * column(inverse, width - 2), p1 * i1, (b1 - 7.0 * p1 - p0) * i1, -(7.0 * p1 + b1) * i1, p1 * i1, i1)
                )
        for k in range(z.vregs):
            cut = slice(k * 128, (k + 1) * 128)
            g = reverse8(arrived[end * n_half + half, :, cut])
            own, q = ends[parity, :, cut], edges[parity, :, cut]
            m = [spread([mul[a][n] for a in range(3)], k) for n in range(len(mul[0]))]
            if parity == 0:
                value = own + jnp.where(odd_end, m[1], m[0]) * g
                value += jnp.where(odd_end, 0.0, m[2] * roll(g, -1, 1) + m[3] * q)
            else:
                value = own * jnp.where(odd_end, m[5], 1.0) + jnp.where(odd_end, m[1], m[0]) * g
                value += jnp.where(odd_end, m[2] * roll(g, 1, 1) + m[3] * q + m[4] * roll(q, 1, 1), 0.0)
            fixed[parity, :, cut] = value

    cuts = [species * n // OUT_CHUNKS for n in range(OUT_CHUNKS + 1)]

    def store(n, special):
        for f in range(6):
            a, parity = f // 2, f % 2
            extra = special(a, parity) if special else None
            for s in range(cuts[n], cuts[n + 1]):
                at = a * z.group + 2 * s
                value = partial[s, f]
                end = fixed[parity, :, (at // 128) * 128 : (at // 128 + 1) * 128]
                end = wide(roll(end, -at if parity == 0 else 126 - at, 1), width)
                value = jnp.where(lane < 2 if parity == 0 else lane >= width - 2, end, value)
                if extra is not None:
                    value = extra(value, s, f)
                result[f, s] = value

    def send(n):
        some = pl.ds(cuts[n], cuts[n + 1] - cuts[n])
        for f in range(6):
            pltpu.make_async_copy(result.at[f, some], out.at[some, 0, order[0, f]], out_sem).start()

    def everything(special=None):
        for n in range(OUT_CHUNKS):
            store(n, special)
            send(n)

    def gather():
        holder = jnp.where(first, n_half - 1, 0)
        pieces = []
        for k in range(z.vregs):
            cut = slice(k * 128, (k + 1) * 128)
            spare = from_b[z.extra + 8 * k : z.extra + 8 * k + 8, 0:128]
            mine = reverse8(jnp.where(first, edges[1, :, cut], edges[0, :, cut]))
            parts = []
            for t in reversed(range(z.tiles)):
                if t == 0:
                    x = jnp.where(first, mine, spare)
                elif t == z.tiles - 1:
                    x = jnp.where(first, spare, mine)
                else:
                    x = arrived[t * n_half + half, :, cut]
                if (k + 1) * 128 > z.flux:
                    x = jnp.where(lane1 + k * 128 < z.flux, x, arrived[t * n_half + holder, :, cut])
                parts.append(x)
            pieces.append(jnp.concatenate(parts, axis=0).T)
        turned[...] = jnp.concatenate(pieces, axis=0) if len(pieces) > 1 else pieces[0]
        return turned[z.flux2 : z.flux2 + 8]

    fetch.wait()

    @pl.when(first)
    def _():
        flux = gather()

        def special(a, parity):
            if parity == 0:
                return None
            f, source = 2 * a + 1, (a + 2) % 3
            dp, inverse, v0, v1 = aux[f, 1], aux[f, 2], aux[f, 4], aux[f, 5]
            inverse = jnp.where(lane == width - 1, last_column[a], inverse)
            ghost_dp = flux[source : source + 1]
            p0, p1, b0 = v0 * twelfth, v1 * twelfth, upwind(v0, ghost_dp + dp)
            zero = jnp.zeros_like(dp)
            on0, on1 = row == 0, row < 2
            two = jnp.where(on1, -p0 * inverse, zero)
            one = jnp.where(on0, (7.0 * p0 + b0 + p1) * inverse, zero)
            none = jnp.where(on0, -b0 * inverse, zero)

            def extra(value, s, f):
                rows = turned[source * z.group + 8 * (s // 4) : source * z.group + 8 * (s // 4) + 8]
                u = s % 4
                q = mixing[s, 0, order[0, f]]
                return value + two * roll(rows, -2 * u, 0) + one * roll(rows, -2 * u - 1, 0) + none * q

            return extra

        everything(special)

    @pl.when(last)
    def _():
        flux = gather()

        def special(a, parity):
            if parity == 1:
                return None
            f, source = 2 * a, (a + 1) % 3
            dp, inverse, new, v0 = (aux[f, n] for n in (1, 2, 3, 4))
            ghost_dp, v1 = flux[source : source + 1], flux[3 + source : 4 + source]
            on7, on6 = row == 7, row >= 6
            inverse = jnp.where(on7, 1.0 / jnp.where(on7, new - v1, 1.0), inverse)
            zero = jnp.zeros_like(dp)
            p0, p1, b1 = v0 * twelfth, v1 * twelfth, upwind(v1, dp + ghost_dp)
            two = jnp.where(on7, p1 * inverse, jnp.where(on6, roll(p0, -1, 0) * inverse, zero))
            one = jnp.where(on7, (b1 - 7.0 * p1 - p0) * inverse, zero)
            none = jnp.where(on7, -(7.0 * p1 + b1) * inverse, zero)
            back = jnp.where(on7, p1 * inverse, zero)
            scale = jnp.where(on7, inverse, 1.0)

            def extra(value, s, f):
                rows = turned[source * z.group + 8 * (s // 4) : source * z.group + 8 * (s // 4) + 8]
                u = s % 4
                q = mixing[s, 0, order[0, f]]
                value = value * scale + two * roll(rows, 6 - 2 * u, 0) + one * roll(rows, 7 - 2 * u, 0)
                return value + none * q + back * roll(q, 1, 0)

            return extra

        everything(special)

    @pl.when(jnp.logical_not(first | last))
    def _():
        everything()

    for f in range(6):
        pltpu.make_async_copy(result.at[f], out.at[:, 0, order[0, f]], out_sem).wait()


def local(mixing, layer_mass, mass_east, mass_north, face_slot):
    tiles = lax.axis_size("tile")
    halves = lax.axis_size("spec")
    z = Sizes(mixing, halves, tiles)
    assert z.rows == 8 and mixing.shape[1] == 1 and tiles > 2 and tiles % 2 == 0
    assert z.width == 8 * tiles and z.width % 128 == 0 and 128 % z.part == 0
    vmem = pl.BlockSpec(memory_space=pltpu.VMEM)
    hbm = pl.BlockSpec(memory_space=pl.ANY)
    params = pltpu.CompilerParams(vmem_limit_bytes=VMEM_LIMIT)
    cells = (z.species, 6, 8, z.width)

    def f32(*shape):
        return jax.ShapeDtypeStruct(shape, F32)

    to_a, to_b, messages, edges, own, order = pl.pallas_call(
        lambda *refs: pack_kernel(z, *refs),
        out_shape=(
            f32(z.sent, z.width),
            f32(z.sent, z.width),
            f32(tiles * halves, 8, z.lanes),
            f32(2, 8, z.lanes),
            f32(z.own, 8, 128),
            jax.ShapeDtypeStruct((8, 128), jnp.int32),
        ),
        in_specs=[hbm] * 5,
        out_specs=[vmem] * 6,
        scratch_shapes=[
            pltpu.SMEM((6,), jnp.int32),
            pltpu.VMEM(mixing.shape, F32),
            pltpu.VMEM((3,) + layer_mass.shape, F32),
            pltpu.SemaphoreType.DMA((4 + CHUNKS,)),
        ],
        name="pack",
    )(face_slot, mixing, layer_mass, mass_east, mass_north)
    arrived = lax.all_to_all(messages, ("tile", "spec"), 0, 0, tiled=True)
    from_a = lax.ppermute(to_a, "tile", [(i, i ^ 1) for i in range(tiles)])
    pairs = [(i, (i + 1) % tiles) if i % 2 else (i, (i - 1) % tiles) for i in range(tiles)]
    from_b = lax.ppermute(to_b, "tile", pairs)
    mine = pl.pallas_call(
        lambda *refs: share_kernel(z, *refs),
        out_shape=f32(z.shared, 8, 128),
        in_specs=[vmem] * 3,
        out_specs=vmem,
        compiler_params=params,
        cost_estimate=pl.CostEstimate(flops=23 * 10**9, bytes_accessed=0, transcendentals=0),
        name="share",
    )(own, from_a, from_b)
    if halves == 2:
        others = lax.ppermute(mine, "spec", [(0, 1), (1, 0)])
    else:
        others = lax.all_gather(mine, "spec", axis=0, tiled=False)
    partial, ends, aux = pl.pallas_call(
        lambda *refs: interior_kernel(z, *refs),
        out_shape=(f32(*cells), f32(2, 8, z.lanes), f32(6, 6, 8, z.width)),
        in_specs=[vmem] * 6,
        out_specs=[vmem] * 3,
        scratch_shapes=[
            pltpu.SMEM((8, 128), jnp.int32),
            pltpu.VMEM((2 * z.flux, z.width), F32),
            pltpu.VMEM((2 * z.flux, z.width), F32),
            pltpu.VMEM((6, 9, 8, z.width), F32),
            pltpu.SemaphoreType.DMA,
        ],
        compiler_params=params,
        name="interior",
    )(order, mixing, from_a, from_b, mine, others)
    return pl.pallas_call(
        lambda *refs: finish_kernel(z, *refs),
        out_shape=f32(*mixing.shape),
        in_specs=[vmem] * 8,
        out_specs=hbm,
        scratch_shapes=[
            pltpu.SMEM((8, 128), jnp.int32),
            pltpu.VMEM((z.lanes, z.width), F32),
            pltpu.VMEM((2, 8, z.lanes), F32),
            pltpu.VMEM((6, z.species, 8, z.width), F32),
            pltpu.SemaphoreType.DMA,
            pltpu.SemaphoreType.DMA,
        ],
        compiler_params=params,
        name="finish",
    )(order, mixing, from_b, partial, ends, aux, edges, arrived)


def solution(mesh):
    flux = P(None, None, "tile", "spec")
    cells = P("spec", None, None, "tile", None)
    return jax.shard_map(
        local,
        mesh=mesh,
        in_specs=(cells, flux, flux, flux, P()),
        out_specs=cells,
        check_vma=False,
    )
```

```python
import jax
import jax.numpy as jnp
from jax import lax
from jax.experimental import pallas as pl
from jax.experimental.pallas import tpu as pltpu
from jax.sharding import PartitionSpec as P

F32 = jnp.float32
VMEM_LIMIT = 12 << 20
CHUNKS = 2
OUT_CHUNKS = 4


def up(value, unit):
    return -(-value // unit) * unit


class Sizes:
    def __init__(self, mixing, halves, tiles):
        self.species, _, _, self.rows, self.width = mixing.shape
        self.tiles, self.halves = tiles, halves
        self.part = self.width // halves
        self.group = up(2 * self.species, 8)
        self.flux = 3 * self.group
        self.flux2 = self.flux + 8
        self.lanes = up(self.flux2 + 8, 128)
        self.vregs = self.lanes // 128
        self.dp_at = 2 * self.flux
        self.fy_at = self.dp_at + 8
        self.extra = self.fy_at + 8
        self.sent = self.extra + 8 * self.vregs
        self.per = 128 // self.part
        self.own = up(18, self.per) // self.per
        self.pieces = 21
        self.shared = up(self.pieces, self.per) // self.per


def slots(face_slot):
    return [sum(jnp.where(face_slot[s] == f, s, 0) for s in range(6)) for f in range(6)]


def roll(x, shift, axis):
    shift %= x.shape[axis]
    return pltpu.roll(x, shift, axis) if shift else x


def reverse8(x):
    row = lax.broadcasted_iota(jnp.int32, x.shape, 0)
    x = jnp.where((row & 1) == 0, roll(x, -1, 0), roll(x, 1, 0))
    x = jnp.where((row & 2) == 0, roll(x, -2, 0), roll(x, 2, 0))
    return roll(x, 4, 0)


def upwind(u, total):
    return 0.5 * jnp.abs(u) * (1.0 - jnp.abs(u / (0.5 * total)))


def wide(x, width):
    return jnp.concatenate([x] * (width // 128), axis=-1) if width > 128 else x


def side_by_side(tiles, per):
    tiles = tiles + [tiles[0]] * (per - len(tiles))
    return jnp.concatenate(tiles, axis=-1) if per > 1 else tiles[0]


def pack_kernel(
    z, slot_in, mixing_in, dp_in, fx_in, fy_in,
    to_a_out, to_b_out, out_out, edges_out, own_out, order_out,
    to_a, to_b, out, edges, own, order, face_slot, mixing, fluxes, sems, out_sems,
):
    cuts = [z.species * n // CHUNKS for n in range(CHUNKS + 1)]
    copies = [pltpu.make_async_copy(slot_in, face_slot, sems.at[0])]
    for c, ref in enumerate((dp_in, fx_in, fy_in)):
        copies.append(pltpu.make_async_copy(ref, fluxes.at[c], sems.at[1 + c]))
    for n in range(CHUNKS):
        some = pl.ds(cuts[n], cuts[n + 1] - cuts[n])
        copies.append(pltpu.make_async_copy(mixing_in.at[some], mixing.at[some], sems.at[4 + n]))
    for copy in copies:
        copy.start()
    place = lax.axis_index("tile")
    half = lax.axis_index("spec")
    copies[0].wait()
    slot = slots(face_slot)
    even = lax.rem(place, 2) == 0
    first, last = place == 0, place == z.tiles - 1
    width, part, species, n_half = z.width, z.part, z.species, z.halves
    lane = lax.broadcasted_iota(jnp.int32, (8, 128), 1)
    order[...] = sum(jnp.where(lane == f, slot[f], 0) for f in range(6))
    results = [
        pltpu.make_async_copy(x, y, out_sems.at[n])
        for n, (x, y) in enumerate(
            ((to_a, to_a_out), (to_b, to_b_out), (edges, edges_out), (own, own_out), (order, order_out))
        )
    ]
    results[4].start()
    for copy in copies[1:4]:
        copy.wait()
    raw = [[fluxes[c, 0, slot[f]] for f in range(6)] for c in range(3)]
    flat = [raw[c][f] for c in range(3) for f in range(6)]
    for n in range(z.own):
        own[n] = side_by_side(flat[n * z.per : (n + 1) * z.per], z.per)
    results[3].start()

    def both(low, high, at):
        to_a[pl.ds(at, low.shape[0])] = jnp.where(even, high, low)
        to_b[pl.ds(at, low.shape[0])] = jnp.where(even, low, high)

    def padded(x):
        return jnp.concatenate([x, jnp.zeros((8, width - part), F32)], axis=-1) if width > part else x

    pad = jnp.zeros((2, part), F32)
    low_dp = jnp.concatenate([x[0:1] for x in raw[0]] + [pad], axis=0)
    high_dp = jnp.concatenate([x[7:8] for x in raw[0]] + [pad], axis=0)
    low_fy = padded(jnp.concatenate([x[0:1] for x in raw[2]] + [pad], axis=0))
    both(padded(low_dp), padded(high_dp), z.dp_at)
    both(low_fy, low_fy, z.fy_at)

    columns = [[jnp.zeros((8, 128), F32) for _ in range(z.vregs)] for _ in range(2)]
    for parity in range(2):
        for a in range(3):
            f = 2 * a + parity
            if z.group > 2 * species:
                zero = jnp.zeros((z.group - 2 * species, width), F32)
                both(zero, zero, parity * z.flux + a * z.group + 2 * species)
            for c in range(2):
                at = z.flux2 + 3 * c + a
                edge = side_by_side([raw[c][f]] * z.per, z.per)
                moved = roll(edge, at - (0 if parity == 0 else 127), 1)
                k = at // 128
                columns[parity][k] = jnp.where(lane == at % 128, moved, columns[parity][k])
    for n in range(CHUNKS):
        copies[4 + n].wait()
        for s in range(cuts[n], cuts[n + 1]):
            for f in range(6):
                a, parity = f // 2, f % 2
                tile = mixing[s, 0, slot[f]]
                at = a * z.group + 2 * s
                both(tile[0:2], tile[6:8], parity * z.flux + at)
                edge = tile[:, :128] if parity == 0 else tile[:, width - 128 :]
                moved = roll(edge, at - (0 if parity == 0 else 126), 1)
                k = at // 128
                columns[parity][k] = jnp.where((lane >> 1) == (at % 128) // 2, moved, columns[parity][k])
    turned = [[reverse8(x) for x in lanes] for lanes in columns]
    for k in range(z.vregs):
        for parity in range(2):
            edges[parity, :, k * 128 : (k + 1) * 128] = columns[parity][k]
        spare = wide(jnp.where(first, turned[0][k], turned[1][k]), width)
        to_a[pl.ds(z.extra + 8 * k, 8)] = spare
        to_b[pl.ds(z.extra + 8 * k, 8)] = spare
    for n in range(3):
        results[n].start()

    ends = ((0, turned[1]), (z.tiles - 1, turned[0]))

    @pl.when(first | last)
    def _():
        rows, dps, fys = [], [], []
        for a in range(3):
            for_odd, for_even = (a + 1) % 3, (a + 2) % 3
            start = jnp.where(first, z.flux + for_odd * z.group, for_even * z.group)
            rows.append(to_b[pl.ds(pl.multiple_of(start, 8), z.group)])
            for c, values in ((0, dps), (2, fys)):
                values.append(jnp.where(first, raw[c][2 * for_odd + 1][0:1], raw[c][2 * for_even][7:8]))
        flux = jnp.concatenate(dps + fys + [pad], axis=0)
        flux = jnp.concatenate([jnp.where(half == n, flux, 0.0) for n in range(n_half)], axis=-1)
        rows += [flux, jnp.zeros((z.lanes - z.flux - 8, width), F32)]
        messages = jnp.concatenate(rows, axis=0).T
        for t in range(z.tiles):
            at = 8 * (z.tiles - 1 - t)
            for n in range(n_half):
                out[t * n_half + n] = messages[at : at + 8]
        for t, cols in ends:
            at = 8 * (z.tiles - 1 - t)
            k = z.flux2 // 128
            here = (lane >= z.flux2 % 128) & (lane < z.flux2 % 128 + 8)
            mixed = jnp.where(here, cols[k], messages[at : at + 8, k * 128 : (k + 1) * 128])
            for n in range(n_half):
                out[t * n_half + n, :, k * 128 : (k + 1) * 128] = mixed
        copy = pltpu.make_async_copy(out, out_out, out_sems.at[5])
        copy.start()
        copy.wait()

    @pl.when(jnp.logical_not(first | last))
    def _():
        for t, cols in ends:
            for n in range(n_half):
                for k in range(z.vregs):
                    out[t * n_half + n, :, k * 128 : (k + 1) * 128] = cols[k]
        copies = []
        for t, _ in ends:
            some = pl.ds(t * n_half, n_half)
            copies.append(pltpu.make_async_copy(out.at[some], out_out.at[some], out_sems.at[5 + (t > 0)]))
        for copy in copies:
            copy.start()
        for copy in copies:
            copy.wait()

    for copy in results:
        copy.wait()


def share_kernel(z, own, from_a, from_b, out):
    even = lax.rem(lax.axis_index("tile"), 2) == 0
    part = z.part
    dp_a, dp_b = from_a[z.dp_at : z.dp_at + 8, :part], from_b[z.dp_at : z.dp_at + 8, :part]
    fy_a, fy_b = from_a[z.fy_at : z.fy_at + 8, :part], from_b[z.fy_at : z.fy_at + 8, :part]
    halo = [jnp.where(even, dp_b, dp_a), jnp.where(even, dp_a, dp_b), jnp.where(even, fy_a, fy_b)]
    flat = [own[n // z.per][:, (n % z.per) * part : (n % z.per + 1) * part] for n in range(18)] + halo
    for n in range(z.shared):
        out[n] = side_by_side(flat[n * z.per : (n + 1) * z.per], z.per)


def interior_kernel(
    z, order_in, mixing, from_a, from_b, mine, others, partial, ends, aux,
    order, south, north, coef, order_sem,
):
    fetch = pltpu.make_async_copy(order_in, order, order_sem)
    fetch.start()
    place = lax.axis_index("tile")
    half = lax.axis_index("spec")
    even = lax.rem(place, 2) == 0
    first, last = place == 0, place == z.tiles - 1
    width, part, species = z.width, z.part, z.species
    lane = lax.broadcasted_iota(jnp.int32, (8, width), 1)
    row = lax.broadcasted_iota(jnp.int32, (8, width), 0)
    lane1 = lax.broadcasted_iota(jnp.int32, (8, 128), 1)

    a_rows, b_rows = from_a[0 : z.dp_at], from_b[0 : z.dp_at]
    south[...] = jnp.where(even, b_rows, a_rows)
    north[...] = jnp.where(even, a_rows, b_rows)

    full = []
    for n in range(z.pieces):
        cut = slice((n % z.per) * part, (n % z.per + 1) * part)
        if z.halves == 2:
            x, y = mine[n // z.per][:, cut], others[n // z.per][:, cut]
            parts = [jnp.where(half == 0, x, y), jnp.where(half == 0, y, x)]
        else:
            parts = [others[h, n // z.per][:, cut] for h in range(z.halves)]
        full.append(jnp.concatenate(parts, axis=-1))
    dp_south, dp_north, fy_north = full[18:]

    def left(x, ghost, n):
        return pltpu.roll(jnp.where(lane >= width - n, ghost, x), n, 1)

    def right(x, ghost, n):
        return pltpu.roll(jnp.where(lane < n, ghost, x), width - n, 1)

    def below(x, ghost, n):
        return pltpu.roll(jnp.where(row >= 8 - n, ghost, x), n, 0)

    def above(x, ghost, n):
        return pltpu.roll(jnp.where(row < n, ghost, x), 8 - n, 0)

    for f in range(6):
        parity = f % 2
        dp, fx, fy = full[f], full[6 + f], full[12 + f]
        if parity == 0:
            west, east, east_u = dp, full[f + 1], full[6 + f + 1]
            s_end, n_end, v_end = roll(dp_south, 7 - (f - 1) % 6, 0), dp, 0.0
            known = jnp.logical_not(last & (row == 7))
        else:
            west, east, east_u = full[f - 1], dp, 0.0
            s_end, n_end, v_end = dp, roll(dp_north, -((f + 1) % 6), 0), roll(fy_north, -((f + 1) % 6), 0)
            known = lane < width - 1
        dp_w, dp_e = left(dp, west, 1), right(dp, east, 1)
        u0, u1 = fx, right(fx, east_u, 1)
        dp_s = below(dp, jnp.where(first, s_end, roll(dp_south, 7 - f, 0)), 1)
        dp_n = above(dp, jnp.where(last, n_end, roll(dp_north, -f, 0)), 1)
        v0, v1 = fy, above(fy, jnp.where(last, v_end, roll(fy_north, -f, 0)), 1)
        new = dp - (u1 - u0) - (v1 - v0)
        inverse = jnp.where(known, 1.0 / jnp.where(known, new, 1.0), 1.0)
        for n, x in enumerate((fx, dp, inverse, new, v0, v1)):
            aux[f, n] = x
        center = dp
        for n, (w0, w1, d0, d1) in enumerate(((u0, u1, dp_w, dp_e), (v0, v1, dp_s, dp_n))):
            b0, b1 = upwind(w0, d0 + dp), upwind(w1, dp + d1)
            if n == 0 and parity == 0:
                b0 = jnp.where(lane == 0, 0.0, b0)
            if n == 1 and parity == 1:
                b0 = jnp.where(first & (row == 0), 0.0, b0)
            p0, p1 = w0 * (1.0 / 12.0), w1 * (1.0 / 12.0)
            coef[f, 4 * n] = -p0 * inverse
            coef[f, 4 * n + 1] = (7.0 * p0 + b0 + p1) * inverse
            coef[f, 4 * n + 2] = (-p0 - 7.0 * p1 + b1) * inverse
            coef[f, 4 * n + 3] = p1 * inverse
            center = center + (7.0 * p0 - b0) - (7.0 * p1 + b1)
        coef[f, 8] = center * inverse

    block = z.flux
    south_at, north_at = jnp.where(first, block, 0), jnp.where(last, 0, block)
    fetch.wait()
    slot = [order[0, f] for f in range(6)]

    def quad(it, count):
        for a in range(3):
            a_s, a_n = jnp.where(first, (a + 2) % 3, a), jnp.where(last, (a + 1) % 3, a)

            def ghosts(ref, at, ref_a):
                return ref[pl.ds(pl.multiple_of(at + ref_a * z.group + 8 * it, 8), 8)]

            south_rows = [ghosts(south, south_at, a_s), jnp.where(first, 0.0, ghosts(south, block, a))]
            north_rows = [jnp.where(last, 0.0, ghosts(north, 0, a)), ghosts(north, north_at, a_n)]
            fe, fo = 2 * a, 2 * a + 1
            ce = [coef[fe, n] for n in range(9)]
            co = [coef[fo, n] for n in range(9)]
            for u in range(count):
                s = 4 * it + u
                qe, qo = mixing[s, 0, slot[fe]], mixing[s, 0, slot[fo]]
                for q, west, east, c, parity, f in ((qe, 0.0, qo, ce, 0, fe), (qo, qe, 0.0, co, 1, fo)):
                    sv = roll(south_rows[parity], 6 - 2 * u, 0)
                    nv = roll(north_rows[parity], -2 * u, 0)
                    value = c[8] * q
                    value += c[0] * left(q, west, 2)
                    value += c[1] * left(q, west, 1)
                    value += c[2] * right(q, east, 1)
                    value += c[3] * right(q, east, 2)
                    value += c[4] * below(q, sv, 2)
                    value += c[5] * below(q, sv, 1)
                    value += c[6] * above(q, nv, 1)
                    value += c[7] * above(q, nv, 2)
                    partial[s, f] = value

    @pl.loop(0, species // 4)
    def _(it):
        quad(it, 4)

    if species % 4:
        quad(species // 4, species % 4)

    lanes = [[jnp.zeros((8, 128), F32) for _ in range(z.vregs)] for _ in range(2)]
    for s in range(species):
        for f in range(6):
            a, parity = f // 2, f % 2
            at = a * z.group + 2 * s
            cut = slice(0, 128) if parity == 0 else slice(width - 128, width)
            moved = roll(partial[s, f, :, cut], at - (0 if parity == 0 else 126), 1)
            k = at // 128
            lanes[parity][k] = jnp.where((lane1 >> 1) == (at % 128) // 2, moved, lanes[parity][k])
    for parity in range(2):
        for k in range(z.vregs):
            ends[parity, :, k * 128 : (k + 1) * 128] = lanes[parity][k]


def finish_kernel(
    z, order_in, mixing, from_b, partial, ends, aux, edges, arrived, out,
    turned, fixed, result, out_sem,
):
    place = lax.axis_index("tile")
    half = lax.axis_index("spec")
    first, last = place == 0, place == z.tiles - 1
    width, part, species, n_half = z.width, z.part, z.species, z.halves
    lane = lax.broadcasted_iota(jnp.int32, (8, width), 1)
    row = lax.broadcasted_iota(jnp.int32, (8, width), 0)
    lane1 = lax.broadcasted_iota(jnp.int32, (8, 128), 1)
    twelfth = 1.0 / 12.0
    holder = lax.div(width - 8 - 8 * place, part)
    places = order_in[0:1].astype(F32)
    slot = [jnp.sum(jnp.where(lane1[0:1] == f, places, 0.0)).astype(jnp.int32) for f in range(6)]

    def column(x, at):
        return x[:, at : at + 1]

    def spread(values, k):
        at = lane1 + k * 128
        return jnp.where(at < z.group, values[0], jnp.where(at < 2 * z.group, values[1], values[2]))

    last_column = []
    odd_end = (lane1 & 1) == 1
    for parity in range(2):
        end = z.tiles - 1 if parity == 0 else 0
        flux = reverse8(arrived[end * n_half + holder, :, (z.flux // 128) * 128 : (z.flux // 128 + 1) * 128])
        mul = []
        for a in range(3):
            f = 2 * a + parity
            fx, dp, inverse, new = (aux[f, n] for n in range(4))
            ghost_dp = column(flux, z.flux % 128 + a)
            if parity == 0:
                u0, p1 = column(fx, 0), column(fx, 1) * twelfth
                p0, b0 = u0 * twelfth, upwind(u0, ghost_dp + column(dp, 0))
                i0, i1 = column(inverse, 0), column(inverse, 1)
                mul.append((-p0 * i0, -p1 * i1, (7.0 * p0 + b0 + p1) * i0, -b0 * i0))
            else:
                u1 = column(flux, z.flux % 128 + 3 + a)
                p1, b1 = u1 * twelfth, upwind(u1, column(dp, width - 1) + ghost_dp)
                p0 = column(fx, width - 1) * twelfth
                i1 = 1.0 / (column(new, width - 1) - u1)
                last_column.append(i1)
                mul.append(
                    (p0 * column(inverse, width - 2), p1 * i1, (b1 - 7.0 * p1 - p0) * i1, -(7.0 * p1 + b1) * i1, p1 * i1, i1)
                )
        for k in range(z.vregs):
            cut = slice(k * 128, (k + 1) * 128)
            g = reverse8(arrived[end * n_half + half, :, cut])
            own, q = ends[parity, :, cut], edges[parity, :, cut]
            m = [spread([mul[a][n] for a in range(3)], k) for n in range(len(mul[0]))]
            if parity == 0:
                value = own + jnp.where(odd_end, m[1], m[0]) * g
                value += jnp.where(odd_end, 0.0, m[2] * roll(g, -1, 1) + m[3] * q)
            else:
                value = own * jnp.where(odd_end, m[5], 1.0) + jnp.where(odd_end, m[1], m[0]) * g
                value += jnp.where(odd_end, m[2] * roll(g, 1, 1) + m[3] * q + m[4] * roll(q, 1, 1), 0.0)
            fixed[parity, :, cut] = value

    cuts = [species * n // OUT_CHUNKS for n in range(OUT_CHUNKS + 1)]

    def store(n, special):
        for f in range(6):
            a, parity = f // 2, f % 2
            extra = special(a, parity) if special else None
            for s in range(cuts[n], cuts[n + 1]):
                at = a * z.group + 2 * s
                value = partial[s, f]
                end = fixed[parity, :, (at // 128) * 128 : (at // 128 + 1) * 128]
                end = wide(roll(end, -at if parity == 0 else 126 - at, 1), width)
                value = jnp.where(lane < 2 if parity == 0 else lane >= width - 2, end, value)
                if extra is not None:
                    value = extra(value, s, f)
                result[f, s] = value

    def send(n):
        some = pl.ds(cuts[n], cuts[n + 1] - cuts[n])
        for f in range(6):
            pltpu.make_async_copy(result.at[f, some], out.at[some, 0, slot[f]], out_sem).start()

    def everything(special=None):
        for n in range(OUT_CHUNKS):
            store(n, special)
            send(n)

    def gather():
        holder = jnp.where(first, n_half - 1, 0)
        pieces = []
        for k in range(z.vregs):
            cut = slice(k * 128, (k + 1) * 128)
            spare = from_b[z.extra + 8 * k : z.extra + 8 * k + 8, 0:128]
            mine = reverse8(jnp.where(first, edges[1, :, cut], edges[0, :, cut]))
            parts = []
            for t in reversed(range(z.tiles)):
                if t == 0:
                    x = jnp.where(first, mine, spare)
                elif t == z.tiles - 1:
                    x = jnp.where(first, spare, mine)
                else:
                    x = arrived[t * n_half + half, :, cut]
                if (k + 1) * 128 > z.flux:
                    x = jnp.where(lane1 + k * 128 < z.flux, x, arrived[t * n_half + holder, :, cut])
                parts.append(x)
            pieces.append(jnp.concatenate(parts, axis=0).T)
        turned[...] = jnp.concatenate(pieces, axis=0) if len(pieces) > 1 else pieces[0]
        return turned[z.flux2 : z.flux2 + 8]

    @pl.when(first)
    def _():
        flux = gather()

        def special(a, parity):
            if parity == 0:
                return None
            f, source = 2 * a + 1, (a + 2) % 3
            dp, inverse, v0, v1 = aux[f, 1], aux[f, 2], aux[f, 4], aux[f, 5]
            inverse = jnp.where(lane == width - 1, last_column[a], inverse)
            ghost_dp = flux[source : source + 1]
            p0, p1, b0 = v0 * twelfth, v1 * twelfth, upwind(v0, ghost_dp + dp)
            zero = jnp.zeros_like(dp)
            on0, on1 = row == 0, row < 2
            two = jnp.where(on1, -p0 * inverse, zero)
            one = jnp.where(on0, (7.0 * p0 + b0 + p1) * inverse, zero)
            none = jnp.where(on0, -b0 * inverse, zero)

            def extra(value, s, f):
                rows = turned[source * z.group + 8 * (s // 4) : source * z.group + 8 * (s // 4) + 8]
                u = s % 4
                q = mixing[s, 0, slot[f]]
                return value + two * roll(rows, -2 * u, 0) + one * roll(rows, -2 * u - 1, 0) + none * q

            return extra

        everything(special)

    @pl.when(last)
    def _():
        flux = gather()

        def special(a, parity):
            if parity == 1:
                return None
            f, source = 2 * a, (a + 1) % 3
            dp, inverse, new, v0 = (aux[f, n] for n in (1, 2, 3, 4))
            ghost_dp, v1 = flux[source : source + 1], flux[3 + source : 4 + source]
            on7, on6 = row == 7, row >= 6
            inverse = jnp.where(on7, 1.0 / jnp.where(on7, new - v1, 1.0), inverse)
            zero = jnp.zeros_like(dp)
            p0, p1, b1 = v0 * twelfth, v1 * twelfth, upwind(v1, dp + ghost_dp)
            two = jnp.where(on7, p1 * inverse, jnp.where(on6, roll(p0, -1, 0) * inverse, zero))
            one = jnp.where(on7, (b1 - 7.0 * p1 - p0) * inverse, zero)
            none = jnp.where(on7, -(7.0 * p1 + b1) * inverse, zero)
            back = jnp.where(on7, p1 * inverse, zero)
            scale = jnp.where(on7, inverse, 1.0)

            def extra(value, s, f):
                rows = turned[source * z.group + 8 * (s // 4) : source * z.group + 8 * (s // 4) + 8]
                u = s % 4
                q = mixing[s, 0, slot[f]]
                value = value * scale + two * roll(rows, 6 - 2 * u, 0) + one * roll(rows, 7 - 2 * u, 0)
                return value + none * q + back * roll(q, 1, 0)

            return extra

        everything(special)

    @pl.when(jnp.logical_not(first | last))
    def _():
        everything()

    for f in range(6):
        pltpu.make_async_copy(result.at[f], out.at[:, 0, slot[f]], out_sem).wait()


def local(mixing, layer_mass, mass_east, mass_north, face_slot):
    tiles = lax.axis_size("tile")
    halves = lax.axis_size("spec")
    z = Sizes(mixing, halves, tiles)
    assert z.rows == 8 and mixing.shape[1] == 1 and tiles > 2 and tiles % 2 == 0
    assert z.width == 8 * tiles and z.width % 128 == 0 and 128 % z.part == 0
    vmem = pl.BlockSpec(memory_space=pltpu.VMEM)
    hbm = pl.BlockSpec(memory_space=pl.ANY)
    params = pltpu.CompilerParams(vmem_limit_bytes=VMEM_LIMIT)
    cells = (z.species, 6, 8, z.width)

    def f32(*shape):
        return jax.ShapeDtypeStruct(shape, F32)

    packed = (
        f32(z.sent, z.width),
        f32(z.sent, z.width),
        f32(tiles * halves, 8, z.lanes),
        f32(2, 8, z.lanes),
        f32(z.own, 8, 128),
        jax.ShapeDtypeStruct((8, 128), jnp.int32),
    )
    to_a, to_b, messages, edges, own, order = pl.pallas_call(
        lambda *refs: pack_kernel(z, *refs),
        out_shape=packed,
        in_specs=[hbm] * 5,
        out_specs=[hbm] * 6,
        scratch_shapes=[pltpu.VMEM(x.shape, x.dtype) for x in packed]
        + [
            pltpu.SMEM((6,), jnp.int32),
            pltpu.VMEM(mixing.shape, F32),
            pltpu.VMEM((3,) + layer_mass.shape, F32),
            pltpu.SemaphoreType.DMA((4 + CHUNKS,)),
            pltpu.SemaphoreType.DMA((7,)),
        ],
        name="pack",
    )(face_slot, mixing, layer_mass, mass_east, mass_north)
    arrived = lax.all_to_all(messages, ("tile", "spec"), 0, 0, tiled=True)
    from_a = lax.ppermute(to_a, "tile", [(i, i ^ 1) for i in range(tiles)])
    pairs = [(i, (i + 1) % tiles) if i % 2 else (i, (i - 1) % tiles) for i in range(tiles)]
    from_b = lax.ppermute(to_b, "tile", pairs)
    mine = pl.pallas_call(
        lambda *refs: share_kernel(z, *refs),
        out_shape=f32(z.shared, 8, 128),
        in_specs=[vmem] * 3,
        out_specs=vmem,
        compiler_params=params,
        cost_estimate=pl.CostEstimate(flops=23 * 10**9, bytes_accessed=0, transcendentals=0),
        name="share",
    )(own, from_a, from_b)
    if halves == 2:
        others = lax.ppermute(mine, "spec", [(0, 1), (1, 0)])
    else:
        others = lax.all_gather(mine, "spec", axis=0, tiled=False)
    partial, ends, aux = pl.pallas_call(
        lambda *refs: interior_kernel(z, *refs),
        out_shape=(f32(*cells), f32(2, 8, z.lanes), f32(6, 6, 8, z.width)),
        in_specs=[vmem] * 6,
        out_specs=[vmem] * 3,
        scratch_shapes=[
            pltpu.SMEM((8, 128), jnp.int32),
            pltpu.VMEM((2 * z.flux, z.width), F32),
            pltpu.VMEM((2 * z.flux, z.width), F32),
            pltpu.VMEM((6, 9, 8, z.width), F32),
            pltpu.SemaphoreType.DMA,
        ],
        compiler_params=params,
        name="interior",
    )(order, mixing, from_a, from_b, mine, others)
    return pl.pallas_call(
        lambda *refs: finish_kernel(z, *refs),
        out_shape=f32(*mixing.shape),
        in_specs=[vmem] * 8,
        out_specs=hbm,
        scratch_shapes=[
            pltpu.VMEM((z.lanes, z.width), F32),
            pltpu.VMEM((2, 8, z.lanes), F32),
            pltpu.VMEM((6, z.species, 8, z.width), F32),
            pltpu.SemaphoreType.DMA,
        ],
        compiler_params=params,
        name="finish",
    )(order, mixing, from_b, partial, ends, aux, edges, arrived)


def solution(mesh):
    flux = P(None, None, "tile", "spec")
    cells = P("spec", None, None, "tile", None)
    return jax.shard_map(
        local,
        mesh=mesh,
        in_specs=(cells, flux, flux, flux, P()),
        out_specs=cells,
        check_vma=False,
    )
```

```python
import jax
import jax.numpy as jnp
from jax import lax
from jax.experimental import pallas as pl
from jax.experimental.pallas import tpu as pltpu
from jax.sharding import PartitionSpec as P

F32 = jnp.float32
VMEM_LIMIT = 12 << 20
CHUNKS = 2
OUT_CHUNKS = 4


def up(value, unit):
    return -(-value // unit) * unit


class Sizes:
    def __init__(self, mixing, halves, tiles):
        self.species, _, _, self.rows, self.width = mixing.shape
        self.tiles, self.halves = tiles, halves
        self.part = self.width // halves
        self.group = up(2 * self.species, 8)
        self.flux = 3 * self.group
        self.flux2 = self.flux + 8
        self.lanes = up(self.flux2 + 8, 128)
        self.vregs = self.lanes // 128
        self.dp_at = 2 * self.flux
        self.fy_at = self.dp_at + 8
        self.extra = self.fy_at + 8
        self.sent = self.extra + 8 * self.vregs
        self.per = 128 // self.part
        self.own = up(18, self.per) // self.per
        self.pieces = 21
        self.shared = up(self.pieces, self.per) // self.per


def slots(face_slot):
    return [sum(jnp.where(face_slot[s] == f, s, 0) for s in range(6)) for f in range(6)]


def roll(x, shift, axis):
    shift %= x.shape[axis]
    return pltpu.roll(x, shift, axis) if shift else x


def reverse8(x):
    row = lax.broadcasted_iota(jnp.int32, x.shape, 0)
    x = jnp.where((row & 1) == 0, roll(x, -1, 0), roll(x, 1, 0))
    x = jnp.where((row & 2) == 0, roll(x, -2, 0), roll(x, 2, 0))
    return roll(x, 4, 0)


def upwind(u, total):
    return 0.5 * jnp.abs(u) * (1.0 - jnp.abs(u / (0.5 * total)))


def wide(x, width):
    return jnp.concatenate([x] * (width // 128), axis=-1) if width > 128 else x


def side_by_side(tiles, per):
    tiles = tiles + [tiles[0]] * (per - len(tiles))
    return jnp.concatenate(tiles, axis=-1) if per > 1 else tiles[0]


def pack_kernel(
    z, slot_in, mixing_in, dp_in, fx_in, fy_in,
    to_a_out, to_b_out, out_out, edges_out, own_out, order_out,
    to_a, to_b, out, edges, own, order, face_slot, mixing, fluxes, sems, out_sems,
):
    cuts = [z.species * n // CHUNKS for n in range(CHUNKS + 1)]
    copies = [pltpu.make_async_copy(slot_in, face_slot, sems.at[0])]
    for c, ref in enumerate((dp_in, fx_in, fy_in)):
        copies.append(pltpu.make_async_copy(ref, fluxes.at[c], sems.at[1 + c]))
    for n in range(CHUNKS):
        some = pl.ds(cuts[n], cuts[n + 1] - cuts[n])
        copies.append(pltpu.make_async_copy(mixing_in.at[some], mixing.at[some], sems.at[4 + n]))
    for copy in copies:
        copy.start()
    place = lax.axis_index("tile")
    half = lax.axis_index("spec")
    copies[0].wait()
    slot = slots(face_slot)
    even = lax.rem(place, 2) == 0
    first, last = place == 0, place == z.tiles - 1
    width, part, species, n_half = z.width, z.part, z.species, z.halves
    lane = lax.broadcasted_iota(jnp.int32, (8, 128), 1)
    order[...] = sum(jnp.where(lane == f, slot[f], 0) for f in range(6))
    results = [
        pltpu.make_async_copy(x, y, out_sems.at[n])
        for n, (x, y) in enumerate(
            ((to_a, to_a_out), (to_b, to_b_out), (edges, edges_out), (own, own_out), (order, order_out))
        )
    ]
    results[4].start()
    for copy in copies[1:4]:
        copy.wait()
    raw = [[fluxes[c, 0, slot[f]] for f in range(6)] for c in range(3)]
    flat = [raw[c][f] for c in range(3) for f in range(6)]
    for n in range(z.own):
        own[n] = side_by_side(flat[n * z.per : (n + 1) * z.per], z.per)
    results[3].start()

    def both(low, high, at):
        to_a[pl.ds(at, low.shape[0])] = jnp.where(even, high, low)
        to_b[pl.ds(at, low.shape[0])] = jnp.where(even, low, high)

    def padded(x):
        return jnp.concatenate([x, jnp.zeros((8, width - part), F32)], axis=-1) if width > part else x

    pad = jnp.zeros((2, part), F32)
    low_dp = jnp.concatenate([x[0:1] for x in raw[0]] + [pad], axis=0)
    high_dp = jnp.concatenate([x[7:8] for x in raw[0]] + [pad], axis=0)
    low_fy = padded(jnp.concatenate([x[0:1] for x in raw[2]] + [pad], axis=0))
    both(padded(low_dp), padded(high_dp), z.dp_at)
    both(low_fy, low_fy, z.fy_at)

    columns = [[jnp.zeros((8, 128), F32) for _ in range(z.vregs)] for _ in range(2)]
    for parity in range(2):
        for a in range(3):
            f = 2 * a + parity
            if z.group > 2 * species:
                zero = jnp.zeros((z.group - 2 * species, width), F32)
                both(zero, zero, parity * z.flux + a * z.group + 2 * species)
            for c in range(2):
                at = z.flux2 + 3 * c + a
                edge = side_by_side([raw[c][f]] * z.per, z.per)
                moved = roll(edge, at - (0 if parity == 0 else 127), 1)
                k = at // 128
                columns[parity][k] = jnp.where(lane == at % 128, moved, columns[parity][k])
    for n in range(CHUNKS):
        copies[4 + n].wait()
        for s in range(cuts[n], cuts[n + 1]):
            for f in range(6):
                a, parity = f // 2, f % 2
                tile = mixing[s, 0, slot[f]]
                at = a * z.group + 2 * s
                both(tile[0:2], tile[6:8], parity * z.flux + at)
                edge = tile[:, :128] if parity == 0 else tile[:, width - 128 :]
                moved = roll(edge, at - (0 if parity == 0 else 126), 1)
                k = at // 128
                columns[parity][k] = jnp.where((lane >> 1) == (at % 128) // 2, moved, columns[parity][k])
    turned = [[reverse8(x) for x in lanes] for lanes in columns]
    for k in range(z.vregs):
        for parity in range(2):
            edges[parity, :, k * 128 : (k + 1) * 128] = columns[parity][k]
        spare = wide(jnp.where(first, turned[0][k], turned[1][k]), width)
        to_a[pl.ds(z.extra + 8 * k, 8)] = spare
        to_b[pl.ds(z.extra + 8 * k, 8)] = spare
    for n in range(3):
        results[n].start()

    ends = ((0, turned[1]), (z.tiles - 1, turned[0]))

    @pl.when(first | last)
    def _():
        rows, dps, fys = [], [], []
        for a in range(3):
            for_odd, for_even = (a + 1) % 3, (a + 2) % 3
            start = jnp.where(first, z.flux + for_odd * z.group, for_even * z.group)
            rows.append(to_b[pl.ds(pl.multiple_of(start, 8), z.group)])
            for c, values in ((0, dps), (2, fys)):
                values.append(jnp.where(first, raw[c][2 * for_odd + 1][0:1], raw[c][2 * for_even][7:8]))
        flux = jnp.concatenate(dps + fys + [pad], axis=0)
        flux = jnp.concatenate([jnp.where(half == n, flux, 0.0) for n in range(n_half)], axis=-1)
        rows += [flux, jnp.zeros((z.lanes - z.flux - 8, width), F32)]
        messages = jnp.concatenate(rows, axis=0).T
        for t in range(z.tiles):
            at = 8 * (z.tiles - 1 - t)
            for n in range(n_half):
                out[n, t] = messages[at : at + 8]
        for t, cols in ends:
            at = 8 * (z.tiles - 1 - t)
            k = z.flux2 // 128
            here = (lane >= z.flux2 % 128) & (lane < z.flux2 % 128 + 8)
            mixed = jnp.where(here, cols[k], messages[at : at + 8, k * 128 : (k + 1) * 128])
            for n in range(n_half):
                out[n, t, :, k * 128 : (k + 1) * 128] = mixed
        copy = pltpu.make_async_copy(out, out_out, out_sems.at[5])
        copy.start()
        copy.wait()

    @pl.when(jnp.logical_not(first | last))
    def _():
        for t, cols in ends:
            for n in range(n_half):
                for k in range(z.vregs):
                    out[n, t, :, k * 128 : (k + 1) * 128] = cols[k]
        copies = []
        for t, _ in ends:
            copies.append(pltpu.make_async_copy(out.at[:, t], out_out.at[:, t], out_sems.at[5 + (t > 0)]))
        for copy in copies:
            copy.start()
        for copy in copies:
            copy.wait()

    for copy in results:
        copy.wait()


def share_kernel(z, own, from_a, from_b, out):
    even = lax.rem(lax.axis_index("tile"), 2) == 0
    part = z.part
    dp_a, dp_b = from_a[z.dp_at : z.dp_at + 8, :part], from_b[z.dp_at : z.dp_at + 8, :part]
    fy_a, fy_b = from_a[z.fy_at : z.fy_at + 8, :part], from_b[z.fy_at : z.fy_at + 8, :part]
    halo = [jnp.where(even, dp_b, dp_a), jnp.where(even, dp_a, dp_b), jnp.where(even, fy_a, fy_b)]
    flat = [own[n // z.per][:, (n % z.per) * part : (n % z.per + 1) * part] for n in range(18)] + halo
    for n in range(z.shared):
        out[n] = side_by_side(flat[n * z.per : (n + 1) * z.per], z.per)


def interior_kernel(
    z, order_in, mixing, from_a, from_b, mine, others, partial, ends, aux,
    order, south, north, coef, order_sem,
):
    fetch = pltpu.make_async_copy(order_in, order, order_sem)
    fetch.start()
    place = lax.axis_index("tile")
    half = lax.axis_index("spec")
    even = lax.rem(place, 2) == 0
    first, last = place == 0, place == z.tiles - 1
    width, part, species = z.width, z.part, z.species
    lane = lax.broadcasted_iota(jnp.int32, (8, width), 1)
    row = lax.broadcasted_iota(jnp.int32, (8, width), 0)
    lane1 = lax.broadcasted_iota(jnp.int32, (8, 128), 1)

    a_rows, b_rows = from_a[0 : z.dp_at], from_b[0 : z.dp_at]
    south[...] = jnp.where(even, b_rows, a_rows)
    north[...] = jnp.where(even, a_rows, b_rows)

    full = []
    for n in range(z.pieces):
        cut = slice((n % z.per) * part, (n % z.per + 1) * part)
        if z.halves == 2:
            x, y = mine[n // z.per][:, cut], others[n // z.per][:, cut]
            parts = [jnp.where(half == 0, x, y), jnp.where(half == 0, y, x)]
        else:
            parts = [others[h, n // z.per][:, cut] for h in range(z.halves)]
        full.append(jnp.concatenate(parts, axis=-1))
    dp_south, dp_north, fy_north = full[18:]

    def left(x, ghost, n):
        return pltpu.roll(jnp.where(lane >= width - n, ghost, x), n, 1)

    def right(x, ghost, n):
        return pltpu.roll(jnp.where(lane < n, ghost, x), width - n, 1)

    def below(x, ghost, n):
        return pltpu.roll(jnp.where(row >= 8 - n, ghost, x), n, 0)

    def above(x, ghost, n):
        return pltpu.roll(jnp.where(row < n, ghost, x), 8 - n, 0)

    for f in range(6):
        parity = f % 2
        dp, fx, fy = full[f], full[6 + f], full[12 + f]
        if parity == 0:
            west, east, east_u = dp, full[f + 1], full[6 + f + 1]
            s_end, n_end, v_end = roll(dp_south, 7 - (f - 1) % 6, 0), dp, 0.0
            known = jnp.logical_not(last & (row == 7))
        else:
            west, east, east_u = full[f - 1], dp, 0.0
            s_end, n_end, v_end = dp, roll(dp_north, -((f + 1) % 6), 0), roll(fy_north, -((f + 1) % 6), 0)
            known = lane < width - 1
        dp_w, dp_e = left(dp, west, 1), right(dp, east, 1)
        u0, u1 = fx, right(fx, east_u, 1)
        dp_s = below(dp, jnp.where(first, s_end, roll(dp_south, 7 - f, 0)), 1)
        dp_n = above(dp, jnp.where(last, n_end, roll(dp_north, -f, 0)), 1)
        v0, v1 = fy, above(fy, jnp.where(last, v_end, roll(fy_north, -f, 0)), 1)
        new = dp - (u1 - u0) - (v1 - v0)
        inverse = jnp.where(known, 1.0 / jnp.where(known, new, 1.0), 1.0)
        for n, x in enumerate((fx, dp, inverse, new, v0, v1)):
            aux[f, n] = x
        center = dp
        for n, (w0, w1, d0, d1) in enumerate(((u0, u1, dp_w, dp_e), (v0, v1, dp_s, dp_n))):
            b0, b1 = upwind(w0, d0 + dp), upwind(w1, dp + d1)
            if n == 0 and parity == 0:
                b0 = jnp.where(lane == 0, 0.0, b0)
            if n == 1 and parity == 1:
                b0 = jnp.where(first & (row == 0), 0.0, b0)
            p0, p1 = w0 * (1.0 / 12.0), w1 * (1.0 / 12.0)
            coef[f, 4 * n] = -p0 * inverse
            coef[f, 4 * n + 1] = (7.0 * p0 + b0 + p1) * inverse
            coef[f, 4 * n + 2] = (-p0 - 7.0 * p1 + b1) * inverse
            coef[f, 4 * n + 3] = p1 * inverse
            center = center + (7.0 * p0 - b0) - (7.0 * p1 + b1)
        coef[f, 8] = center * inverse

    block = z.flux
    south_at, north_at = jnp.where(first, block, 0), jnp.where(last, 0, block)
    fetch.wait()
    slot = [order[0, f] for f in range(6)]

    def quad(it, count):
        for a in range(3):
            a_s, a_n = jnp.where(first, (a + 2) % 3, a), jnp.where(last, (a + 1) % 3, a)

            def ghosts(ref, at, ref_a):
                return ref[pl.ds(pl.multiple_of(at + ref_a * z.group + 8 * it, 8), 8)]

            south_rows = [ghosts(south, south_at, a_s), jnp.where(first, 0.0, ghosts(south, block, a))]
            north_rows = [jnp.where(last, 0.0, ghosts(north, 0, a)), ghosts(north, north_at, a_n)]
            fe, fo = 2 * a, 2 * a + 1
            ce = [coef[fe, n] for n in range(9)]
            co = [coef[fo, n] for n in range(9)]
            for u in range(count):
                s = 4 * it + u
                qe, qo = mixing[s, 0, slot[fe]], mixing[s, 0, slot[fo]]
                for q, west, east, c, parity, f in ((qe, 0.0, qo, ce, 0, fe), (qo, qe, 0.0, co, 1, fo)):
                    sv = roll(south_rows[parity], 6 - 2 * u, 0)
                    nv = roll(north_rows[parity], -2 * u, 0)
                    value = c[8] * q
                    value += c[0] * left(q, west, 2)
                    value += c[1] * left(q, west, 1)
                    value += c[2] * right(q, east, 1)
                    value += c[3] * right(q, east, 2)
                    value += c[4] * below(q, sv, 2)
                    value += c[5] * below(q, sv, 1)
                    value += c[6] * above(q, nv, 1)
                    value += c[7] * above(q, nv, 2)
                    partial[s, f] = value

    @pl.loop(0, species // 4)
    def _(it):
        quad(it, 4)

    if species % 4:
        quad(species // 4, species % 4)

    lanes = [[jnp.zeros((8, 128), F32) for _ in range(z.vregs)] for _ in range(2)]
    for s in range(species):
        for f in range(6):
            a, parity = f // 2, f % 2
            at = a * z.group + 2 * s
            cut = slice(0, 128) if parity == 0 else slice(width - 128, width)
            moved = roll(partial[s, f, :, cut], at - (0 if parity == 0 else 126), 1)
            k = at // 128
            lanes[parity][k] = jnp.where((lane1 >> 1) == (at % 128) // 2, moved, lanes[parity][k])
    for parity in range(2):
        for k in range(z.vregs):
            ends[parity, :, k * 128 : (k + 1) * 128] = lanes[parity][k]


def finish_kernel(
    z, order_in, mixing, from_b, partial, ends, aux, edges, arrived, out,
    turned, fixed, result, out_sem,
):
    place = lax.axis_index("tile")
    half = lax.axis_index("spec")
    first, last = place == 0, place == z.tiles - 1
    width, part, species, n_half = z.width, z.part, z.species, z.halves
    lane = lax.broadcasted_iota(jnp.int32, (8, width), 1)
    row = lax.broadcasted_iota(jnp.int32, (8, width), 0)
    lane1 = lax.broadcasted_iota(jnp.int32, (8, 128), 1)
    twelfth = 1.0 / 12.0
    holder = lax.div(width - 8 - 8 * place, part)
    places = order_in[0:1].astype(F32)
    slot = [jnp.sum(jnp.where(lane1[0:1] == f, places, 0.0)).astype(jnp.int32) for f in range(6)]

    def column(x, at):
        return x[:, at : at + 1]

    def spread(values, k):
        at = lane1 + k * 128
        return jnp.where(at < z.group, values[0], jnp.where(at < 2 * z.group, values[1], values[2]))

    last_column = []
    odd_end = (lane1 & 1) == 1
    for parity in range(2):
        end = z.tiles - 1 if parity == 0 else 0
        flux = reverse8(arrived[holder, end, :, (z.flux // 128) * 128 : (z.flux // 128 + 1) * 128])
        mul = []
        for a in range(3):
            f = 2 * a + parity
            fx, dp, inverse, new = (aux[f, n] for n in range(4))
            ghost_dp = column(flux, z.flux % 128 + a)
            if parity == 0:
                u0, p1 = column(fx, 0), column(fx, 1) * twelfth
                p0, b0 = u0 * twelfth, upwind(u0, ghost_dp + column(dp, 0))
                i0, i1 = column(inverse, 0), column(inverse, 1)
                mul.append((-p0 * i0, -p1 * i1, (7.0 * p0 + b0 + p1) * i0, -b0 * i0))
            else:
                u1 = column(flux, z.flux % 128 + 3 + a)
                p1, b1 = u1 * twelfth, upwind(u1, column(dp, width - 1) + ghost_dp)
                p0 = column(fx, width - 1) * twelfth
                i1 = 1.0 / (column(new, width - 1) - u1)
                last_column.append(i1)
                mul.append(
                    (p0 * column(inverse, width - 2), p1 * i1, (b1 - 7.0 * p1 - p0) * i1, -(7.0 * p1 + b1) * i1, p1 * i1, i1)
                )
        for k in range(z.vregs):
            cut = slice(k * 128, (k + 1) * 128)
            g = reverse8(arrived[half, end, :, cut])
            own, q = ends[parity, :, cut], edges[parity, :, cut]
            m = [spread([mul[a][n] for a in range(3)], k) for n in range(len(mul[0]))]
            if parity == 0:
                value = own + jnp.where(odd_end, m[1], m[0]) * g
                value += jnp.where(odd_end, 0.0, m[2] * roll(g, -1, 1) + m[3] * q)
            else:
                value = own * jnp.where(odd_end, m[5], 1.0) + jnp.where(odd_end, m[1], m[0]) * g
                value += jnp.where(odd_end, m[2] * roll(g, 1, 1) + m[3] * q + m[4] * roll(q, 1, 1), 0.0)
            fixed[parity, :, cut] = value

    cuts = [species * n // OUT_CHUNKS for n in range(OUT_CHUNKS + 1)]

    def store(n, special):
        for f in range(6):
            a, parity = f // 2, f % 2
            extra = special(a, parity) if special else None
            for s in range(cuts[n], cuts[n + 1]):
                at = a * z.group + 2 * s
                value = partial[s, f]
                end = fixed[parity, :, (at // 128) * 128 : (at // 128 + 1) * 128]
                end = wide(roll(end, -at if parity == 0 else 126 - at, 1), width)
                value = jnp.where(lane < 2 if parity == 0 else lane >= width - 2, end, value)
                if extra is not None:
                    value = extra(value, s, f)
                result[f, s] = value

    def send(n):
        some = pl.ds(cuts[n], cuts[n + 1] - cuts[n])
        for f in range(6):
            pltpu.make_async_copy(result.at[f, some], out.at[some, 0, slot[f]], out_sem).start()

    def everything(special=None):
        for n in range(OUT_CHUNKS):
            store(n, special)
            send(n)

    def gather():
        holder = jnp.where(first, n_half - 1, 0)
        pieces = []
        for k in range(z.vregs):
            cut = slice(k * 128, (k + 1) * 128)
            spare = from_b[z.extra + 8 * k : z.extra + 8 * k + 8, 0:128]
            mine = reverse8(jnp.where(first, edges[1, :, cut], edges[0, :, cut]))
            parts = []
            for t in reversed(range(z.tiles)):
                if t == 0:
                    x = jnp.where(first, mine, spare)
                elif t == z.tiles - 1:
                    x = jnp.where(first, spare, mine)
                else:
                    x = arrived[half, t, :, cut]
                if (k + 1) * 128 > z.flux:
                    x = jnp.where(lane1 + k * 128 < z.flux, x, arrived[holder, t, :, cut])
                parts.append(x)
            pieces.append(jnp.concatenate(parts, axis=0).T)
        turned[...] = jnp.concatenate(pieces, axis=0) if len(pieces) > 1 else pieces[0]
        return turned[z.flux2 : z.flux2 + 8]

    @pl.when(first)
    def _():
        flux = gather()

        def special(a, parity):
            if parity == 0:
                return None
            f, source = 2 * a + 1, (a + 2) % 3
            dp, inverse, v0, v1 = aux[f, 1], aux[f, 2], aux[f, 4], aux[f, 5]
            inverse = jnp.where(lane == width - 1, last_column[a], inverse)
            ghost_dp = flux[source : source + 1]
            p0, p1, b0 = v0 * twelfth, v1 * twelfth, upwind(v0, ghost_dp + dp)
            zero = jnp.zeros_like(dp)
            on0, on1 = row == 0, row < 2
            two = jnp.where(on1, -p0 * inverse, zero)
            one = jnp.where(on0, (7.0 * p0 + b0 + p1) * inverse, zero)
            none = jnp.where(on0, -b0 * inverse, zero)

            def extra(value, s, f):
                rows = turned[source * z.group + 8 * (s // 4) : source * z.group + 8 * (s // 4) + 8]
                u = s % 4
                q = mixing[s, 0, slot[f]]
                return value + two * roll(rows, -2 * u, 0) + one * roll(rows, -2 * u - 1, 0) + none * q

            return extra

        everything(special)

    @pl.when(last)
    def _():
        flux = gather()

        def special(a, parity):
            if parity == 1:
                return None
            f, source = 2 * a, (a + 1) % 3
            dp, inverse, new, v0 = (aux[f, n] for n in (1, 2, 3, 4))
            ghost_dp, v1 = flux[source : source + 1], flux[3 + source : 4 + source]
            on7, on6 = row == 7, row >= 6
            inverse = jnp.where(on7, 1.0 / jnp.where(on7, new - v1, 1.0), inverse)
            zero = jnp.zeros_like(dp)
            p0, p1, b1 = v0 * twelfth, v1 * twelfth, upwind(v1, dp + ghost_dp)
            two = jnp.where(on7, p1 * inverse, jnp.where(on6, roll(p0, -1, 0) * inverse, zero))
            one = jnp.where(on7, (b1 - 7.0 * p1 - p0) * inverse, zero)
            none = jnp.where(on7, -(7.0 * p1 + b1) * inverse, zero)
            back = jnp.where(on7, p1 * inverse, zero)
            scale = jnp.where(on7, inverse, 1.0)

            def extra(value, s, f):
                rows = turned[source * z.group + 8 * (s // 4) : source * z.group + 8 * (s // 4) + 8]
                u = s % 4
                q = mixing[s, 0, slot[f]]
                value = value * scale + two * roll(rows, 6 - 2 * u, 0) + one * roll(rows, 7 - 2 * u, 0)
                return value + none * q + back * roll(q, 1, 0)

            return extra

        everything(special)

    @pl.when(jnp.logical_not(first | last))
    def _():
        everything()

    for f in range(6):
        pltpu.make_async_copy(result.at[f], out.at[:, 0, slot[f]], out_sem).wait()


def local(mixing, layer_mass, mass_east, mass_north, face_slot):
    tiles = lax.axis_size("tile")
    halves = lax.axis_size("spec")
    z = Sizes(mixing, halves, tiles)
    assert z.rows == 8 and mixing.shape[1] == 1 and tiles > 2 and tiles % 2 == 0
    assert z.width == 8 * tiles and z.width % 128 == 0 and 128 % z.part == 0
    vmem = pl.BlockSpec(memory_space=pltpu.VMEM)
    hbm = pl.BlockSpec(memory_space=pl.ANY)
    params = pltpu.CompilerParams(vmem_limit_bytes=VMEM_LIMIT)
    cells = (z.species, 6, 8, z.width)

    def f32(*shape):
        return jax.ShapeDtypeStruct(shape, F32)

    packed = (
        f32(z.sent, z.width),
        f32(z.sent, z.width),
        f32(halves, tiles, 8, z.lanes),
        f32(2, 8, z.lanes),
        f32(z.own, 8, 128),
        jax.ShapeDtypeStruct((8, 128), jnp.int32),
    )
    to_a, to_b, messages, edges, own, order = pl.pallas_call(
        lambda *refs: pack_kernel(z, *refs),
        out_shape=packed,
        in_specs=[hbm] * 5,
        out_specs=[hbm] * 6,
        scratch_shapes=[pltpu.VMEM(x.shape, x.dtype) for x in packed]
        + [
            pltpu.SMEM((6,), jnp.int32),
            pltpu.VMEM(mixing.shape, F32),
            pltpu.VMEM((3,) + layer_mass.shape, F32),
            pltpu.SemaphoreType.DMA((4 + CHUNKS,)),
            pltpu.SemaphoreType.DMA((7,)),
        ],
        name="pack",
    )(face_slot, mixing, layer_mass, mass_east, mass_north)
    arrived = lax.all_to_all(
        messages.reshape(halves * tiles, 8, z.lanes), ("spec", "tile"), 0, 0, tiled=True
    ).reshape(messages.shape)
    from_a = lax.ppermute(to_a, "tile", [(i, i ^ 1) for i in range(tiles)])
    pairs = [(i, (i + 1) % tiles) if i % 2 else (i, (i - 1) % tiles) for i in range(tiles)]
    from_b = lax.ppermute(to_b, "tile", pairs)
    mine = pl.pallas_call(
        lambda *refs: share_kernel(z, *refs),
        out_shape=f32(z.shared, 8, 128),
        in_specs=[vmem] * 3,
        out_specs=vmem,
        compiler_params=params,
        cost_estimate=pl.CostEstimate(flops=23 * 10**9, bytes_accessed=0, transcendentals=0),
        name="share",
    )(own, from_a, from_b)
    if halves == 2:
        others = lax.ppermute(mine, "spec", [(0, 1), (1, 0)])
    else:
        others = lax.all_gather(mine, "spec", axis=0, tiled=False)
    partial, ends, aux = pl.pallas_call(
        lambda *refs: interior_kernel(z, *refs),
        out_shape=(f32(*cells), f32(2, 8, z.lanes), f32(6, 6, 8, z.width)),
        in_specs=[vmem] * 6,
        out_specs=[vmem] * 3,
        scratch_shapes=[
            pltpu.SMEM((8, 128), jnp.int32),
            pltpu.VMEM((2 * z.flux, z.width), F32),
            pltpu.VMEM((2 * z.flux, z.width), F32),
            pltpu.VMEM((6, 9, 8, z.width), F32),
            pltpu.SemaphoreType.DMA,
        ],
        compiler_params=params,
        name="interior",
    )(order, mixing, from_a, from_b, mine, others)
    return pl.pallas_call(
        lambda *refs: finish_kernel(z, *refs),
        out_shape=f32(*mixing.shape),
        in_specs=[vmem] * 8,
        out_specs=hbm,
        scratch_shapes=[
            pltpu.VMEM((z.lanes, z.width), F32),
            pltpu.VMEM((2, 8, z.lanes), F32),
            pltpu.VMEM((6, z.species, 8, z.width), F32),
            pltpu.SemaphoreType.DMA,
        ],
        compiler_params=params,
        name="finish",
    )(order, mixing, from_b, partial, ends, aux, edges, arrived)


def solution(mesh):
    flux = P(None, None, "tile", "spec")
    cells = P("spec", None, None, "tile", None)
    return jax.shard_map(
        local,
        mesh=mesh,
        in_specs=(cells, flux, flux, flux, P()),
        out_specs=cells,
        check_vma=False,
    )
```

```python
import jax
import jax.numpy as jnp
from jax import lax
from jax.experimental import pallas as pl
from jax.experimental.pallas import tpu as pltpu
from jax.sharding import PartitionSpec as P

F32 = jnp.float32
VMEM_LIMIT = 12 << 20
CHUNKS = 2
OUT_CHUNKS = 4
ORDERS = {(16, 2): (
    19, 30, 2, 3, 17, 10, 15, 6, 20, 22, 16, 9, 25, 1, 5, 7,
    12, 31, 28, 0, 14, 27, 21, 8, 11, 26, 18, 13, 4, 29, 24, 23,
)}


def up(value, unit):
    return -(-value // unit) * unit


class Sizes:
    def __init__(self, mixing, halves, tiles):
        self.species, _, _, self.rows, self.width = mixing.shape
        self.tiles, self.halves = tiles, halves
        self.part = self.width // halves
        self.group = up(2 * self.species, 8)
        self.flux = 3 * self.group
        self.flux2 = self.flux + 8
        self.lanes = up(self.flux2 + 8, 128)
        self.vregs = self.lanes // 128
        self.dp_at = 2 * self.flux
        self.fy_at = self.dp_at + 8
        self.extra = self.fy_at + 8
        self.sent = self.extra + 8 * self.vregs
        self.per = 128 // self.part
        self.own = up(18, self.per) // self.per
        self.pieces = 21
        self.shared = up(self.pieces, self.per) // self.per
        natural = tuple(t * halves + n for n in range(halves) for t in range(tiles))
        self.order = ORDERS.get((tiles, halves), natural)
        ranks = {device: rank for rank, device in enumerate(self.order)}
        self.rank = [[ranks[t * halves + n] for n in range(halves)] for t in range(tiles)]


def slots(face_slot):
    return [sum(jnp.where(face_slot[s] == f, s, 0) for s in range(6)) for f in range(6)]


def roll(x, shift, axis):
    shift %= x.shape[axis]
    return pltpu.roll(x, shift, axis) if shift else x


def reverse8(x):
    row = lax.broadcasted_iota(jnp.int32, x.shape, 0)
    x = jnp.where((row & 1) == 0, roll(x, -1, 0), roll(x, 1, 0))
    x = jnp.where((row & 2) == 0, roll(x, -2, 0), roll(x, 2, 0))
    return roll(x, 4, 0)


def upwind(u, total):
    return 0.5 * jnp.abs(u) * (1.0 - jnp.abs(u / (0.5 * total)))


def wide(x, width):
    return jnp.concatenate([x] * (width // 128), axis=-1) if width > 128 else x


def side_by_side(tiles, per):
    tiles = tiles + [tiles[0]] * (per - len(tiles))
    return jnp.concatenate(tiles, axis=-1) if per > 1 else tiles[0]


def pack_kernel(
    z, slot_in, mixing_in, dp_in, fx_in, fy_in,
    to_a_out, to_b_out, out_out, edges_out, own_out, order_out,
    to_a, to_b, out, edges, own, order, face_slot, mixing, fluxes, sems, out_sems,
):
    cuts = [z.species * n // CHUNKS for n in range(CHUNKS + 1)]
    copies = [pltpu.make_async_copy(slot_in, face_slot, sems.at[0])]
    for c, ref in enumerate((dp_in, fx_in, fy_in)):
        copies.append(pltpu.make_async_copy(ref, fluxes.at[c], sems.at[1 + c]))
    for n in range(CHUNKS):
        some = pl.ds(cuts[n], cuts[n + 1] - cuts[n])
        copies.append(pltpu.make_async_copy(mixing_in.at[some], mixing.at[some], sems.at[4 + n]))
    for copy in copies:
        copy.start()
    place = lax.axis_index("tile")
    half = lax.axis_index("spec")
    copies[0].wait()
    slot = slots(face_slot)
    even = lax.rem(place, 2) == 0
    first, last = place == 0, place == z.tiles - 1
    width, part, species, n_half = z.width, z.part, z.species, z.halves
    lane = lax.broadcasted_iota(jnp.int32, (8, 128), 1)
    order[...] = sum(jnp.where(lane == f, slot[f], 0) for f in range(6))
    results = [
        pltpu.make_async_copy(x, y, out_sems.at[n])
        for n, (x, y) in enumerate(
            ((to_a, to_a_out), (to_b, to_b_out), (edges, edges_out), (own, own_out), (order, order_out))
        )
    ]
    results[4].start()
    for copy in copies[1:4]:
        copy.wait()
    raw = [[fluxes[c, 0, slot[f]] for f in range(6)] for c in range(3)]
    flat = [raw[c][f] for c in range(3) for f in range(6)]
    for n in range(z.own):
        own[n] = side_by_side(flat[n * z.per : (n + 1) * z.per], z.per)
    results[3].start()

    def both(low, high, at):
        to_a[pl.ds(at, low.shape[0])] = jnp.where(even, high, low)
        to_b[pl.ds(at, low.shape[0])] = jnp.where(even, low, high)

    def padded(x):
        return jnp.concatenate([x, jnp.zeros((8, width - part), F32)], axis=-1) if width > part else x

    pad = jnp.zeros((2, part), F32)
    low_dp = jnp.concatenate([x[0:1] for x in raw[0]] + [pad], axis=0)
    high_dp = jnp.concatenate([x[7:8] for x in raw[0]] + [pad], axis=0)
    low_fy = padded(jnp.concatenate([x[0:1] for x in raw[2]] + [pad], axis=0))
    both(padded(low_dp), padded(high_dp), z.dp_at)
    both(low_fy, low_fy, z.fy_at)

    columns = [[jnp.zeros((8, 128), F32) for _ in range(z.vregs)] for _ in range(2)]
    for parity in range(2):
        for a in range(3):
            f = 2 * a + parity
            if z.group > 2 * species:
                zero = jnp.zeros((z.group - 2 * species, width), F32)
                both(zero, zero, parity * z.flux + a * z.group + 2 * species)
            for c in range(2):
                at = z.flux2 + 3 * c + a
                edge = side_by_side([raw[c][f]] * z.per, z.per)
                moved = roll(edge, at - (0 if parity == 0 else 127), 1)
                k = at // 128
                columns[parity][k] = jnp.where(lane == at % 128, moved, columns[parity][k])
    for n in range(CHUNKS):
        copies[4 + n].wait()
        for s in range(cuts[n], cuts[n + 1]):
            for f in range(6):
                a, parity = f // 2, f % 2
                tile = mixing[s, 0, slot[f]]
                at = a * z.group + 2 * s
                both(tile[0:2], tile[6:8], parity * z.flux + at)
                edge = tile[:, :128] if parity == 0 else tile[:, width - 128 :]
                moved = roll(edge, at - (0 if parity == 0 else 126), 1)
                k = at // 128
                columns[parity][k] = jnp.where((lane >> 1) == (at % 128) // 2, moved, columns[parity][k])
    turned = [[reverse8(x) for x in lanes] for lanes in columns]
    for k in range(z.vregs):
        for parity in range(2):
            edges[parity, :, k * 128 : (k + 1) * 128] = columns[parity][k]
        spare = wide(jnp.where(first, turned[0][k], turned[1][k]), width)
        to_a[pl.ds(z.extra + 8 * k, 8)] = spare
        to_b[pl.ds(z.extra + 8 * k, 8)] = spare
    for n in range(3):
        results[n].start()

    ends = ((0, turned[1]), (z.tiles - 1, turned[0]))

    @pl.when(first | last)
    def _():
        rows, dps, fys = [], [], []
        for a in range(3):
            for_odd, for_even = (a + 1) % 3, (a + 2) % 3
            start = jnp.where(first, z.flux + for_odd * z.group, for_even * z.group)
            rows.append(to_b[pl.ds(pl.multiple_of(start, 8), z.group)])
            for c, values in ((0, dps), (2, fys)):
                values.append(jnp.where(first, raw[c][2 * for_odd + 1][0:1], raw[c][2 * for_even][7:8]))
        flux = jnp.concatenate(dps + fys + [pad], axis=0)
        flux = jnp.concatenate([jnp.where(half == n, flux, 0.0) for n in range(n_half)], axis=-1)
        rows += [flux, jnp.zeros((z.lanes - z.flux - 8, width), F32)]
        messages = jnp.concatenate(rows, axis=0).T
        for t in range(z.tiles):
            at = 8 * (z.tiles - 1 - t)
            for n in range(n_half):
                out[z.rank[t][n]] = messages[at : at + 8]
        for t, cols in ends:
            at = 8 * (z.tiles - 1 - t)
            k = z.flux2 // 128
            here = (lane >= z.flux2 % 128) & (lane < z.flux2 % 128 + 8)
            mixed = jnp.where(here, cols[k], messages[at : at + 8, k * 128 : (k + 1) * 128])
            for n in range(n_half):
                out[z.rank[t][n], :, k * 128 : (k + 1) * 128] = mixed
        copy = pltpu.make_async_copy(out, out_out, out_sems.at[5])
        copy.start()
        copy.wait()

    @pl.when(jnp.logical_not(first | last))
    def _():
        for t, cols in ends:
            for n in range(n_half):
                for k in range(z.vregs):
                    out[z.rank[t][n], :, k * 128 : (k + 1) * 128] = cols[k]
        copies = []
        for e, (t, _) in enumerate(ends):
            for n in range(n_half):
                at = z.rank[t][n]
                copies.append(pltpu.make_async_copy(out.at[at], out_out.at[at], out_sems.at[5 + e * n_half + n]))
        for copy in copies:
            copy.start()
        for copy in copies:
            copy.wait()

    for copy in results:
        copy.wait()


def share_kernel(z, own, from_a, from_b, out):
    even = lax.rem(lax.axis_index("tile"), 2) == 0
    part = z.part
    dp_a, dp_b = from_a[z.dp_at : z.dp_at + 8, :part], from_b[z.dp_at : z.dp_at + 8, :part]
    fy_a, fy_b = from_a[z.fy_at : z.fy_at + 8, :part], from_b[z.fy_at : z.fy_at + 8, :part]
    halo = [jnp.where(even, dp_b, dp_a), jnp.where(even, dp_a, dp_b), jnp.where(even, fy_a, fy_b)]
    flat = [own[n // z.per][:, (n % z.per) * part : (n % z.per + 1) * part] for n in range(18)] + halo
    for n in range(z.shared):
        out[n] = side_by_side(flat[n * z.per : (n + 1) * z.per], z.per)


def interior_kernel(
    z, order_in, mixing, from_a, from_b, mine, others, partial, ends, aux,
    order, south, north, coef, order_sem,
):
    fetch = pltpu.make_async_copy(order_in, order, order_sem)
    fetch.start()
    place = lax.axis_index("tile")
    half = lax.axis_index("spec")
    even = lax.rem(place, 2) == 0
    first, last = place == 0, place == z.tiles - 1
    width, part, species = z.width, z.part, z.species
    lane = lax.broadcasted_iota(jnp.int32, (8, width), 1)
    row = lax.broadcasted_iota(jnp.int32, (8, width), 0)
    lane1 = lax.broadcasted_iota(jnp.int32, (8, 128), 1)

    a_rows, b_rows = from_a[0 : z.dp_at], from_b[0 : z.dp_at]
    south[...] = jnp.where(even, b_rows, a_rows)
    north[...] = jnp.where(even, a_rows, b_rows)

    full = []
    for n in range(z.pieces):
        cut = slice((n % z.per) * part, (n % z.per + 1) * part)
        if z.halves == 2:
            x, y = mine[n // z.per][:, cut], others[n // z.per][:, cut]
            parts = [jnp.where(half == 0, x, y), jnp.where(half == 0, y, x)]
        else:
            parts = [others[h, n // z.per][:, cut] for h in range(z.halves)]
        full.append(jnp.concatenate(parts, axis=-1))
    dp_south, dp_north, fy_north = full[18:]

    def left(x, ghost, n):
        return pltpu.roll(jnp.where(lane >= width - n, ghost, x), n, 1)

    def right(x, ghost, n):
        return pltpu.roll(jnp.where(lane < n, ghost, x), width - n, 1)

    def below(x, ghost, n):
        return pltpu.roll(jnp.where(row >= 8 - n, ghost, x), n, 0)

    def above(x, ghost, n):
        return pltpu.roll(jnp.where(row < n, ghost, x), 8 - n, 0)

    for f in range(6):
        parity = f % 2
        dp, fx, fy = full[f], full[6 + f], full[12 + f]
        if parity == 0:
            west, east, east_u = dp, full[f + 1], full[6 + f + 1]
            s_end, n_end, v_end = roll(dp_south, 7 - (f - 1) % 6, 0), dp, 0.0
            known = jnp.logical_not(last & (row == 7))
        else:
            west, east, east_u = full[f - 1], dp, 0.0
            s_end, n_end, v_end = dp, roll(dp_north, -((f + 1) % 6), 0), roll(fy_north, -((f + 1) % 6), 0)
            known = lane < width - 1
        dp_w, dp_e = left(dp, west, 1), right(dp, east, 1)
        u0, u1 = fx, right(fx, east_u, 1)
        dp_s = below(dp, jnp.where(first, s_end, roll(dp_south, 7 - f, 0)), 1)
        dp_n = above(dp, jnp.where(last, n_end, roll(dp_north, -f, 0)), 1)
        v0, v1 = fy, above(fy, jnp.where(last, v_end, roll(fy_north, -f, 0)), 1)
        new = dp - (u1 - u0) - (v1 - v0)
        inverse = jnp.where(known, 1.0 / jnp.where(known, new, 1.0), 1.0)
        for n, x in enumerate((fx, dp, inverse, new, v0, v1)):
            aux[f, n] = x
        center = dp
        for n, (w0, w1, d0, d1) in enumerate(((u0, u1, dp_w, dp_e), (v0, v1, dp_s, dp_n))):
            b0, b1 = upwind(w0, d0 + dp), upwind(w1, dp + d1)
            if n == 0 and parity == 0:
                b0 = jnp.where(lane == 0, 0.0, b0)
            if n == 1 and parity == 1:
                b0 = jnp.where(first & (row == 0), 0.0, b0)
            p0, p1 = w0 * (1.0 / 12.0), w1 * (1.0 / 12.0)
            coef[f, 4 * n] = -p0 * inverse
            coef[f, 4 * n + 1] = (7.0 * p0 + b0 + p1) * inverse
            coef[f, 4 * n + 2] = (-p0 - 7.0 * p1 + b1) * inverse
            coef[f, 4 * n + 3] = p1 * inverse
            center = center + (7.0 * p0 - b0) - (7.0 * p1 + b1)
        coef[f, 8] = center * inverse

    block = z.flux
    south_at, north_at = jnp.where(first, block, 0), jnp.where(last, 0, block)
    fetch.wait()
    slot = [order[0, f] for f in range(6)]

    def quad(it, count):
        for a in range(3):
            a_s, a_n = jnp.where(first, (a + 2) % 3, a), jnp.where(last, (a + 1) % 3, a)

            def ghosts(ref, at, ref_a):
                return ref[pl.ds(pl.multiple_of(at + ref_a * z.group + 8 * it, 8), 8)]

            south_rows = [ghosts(south, south_at, a_s), jnp.where(first, 0.0, ghosts(south, block, a))]
            north_rows = [jnp.where(last, 0.0, ghosts(north, 0, a)), ghosts(north, north_at, a_n)]
            fe, fo = 2 * a, 2 * a + 1
            ce = [coef[fe, n] for n in range(9)]
            co = [coef[fo, n] for n in range(9)]
            for u in range(count):
                s = 4 * it + u
                qe, qo = mixing[s, 0, slot[fe]], mixing[s, 0, slot[fo]]
                for q, west, east, c, parity, f in ((qe, 0.0, qo, ce, 0, fe), (qo, qe, 0.0, co, 1, fo)):
                    sv = roll(south_rows[parity], 6 - 2 * u, 0)
                    nv = roll(north_rows[parity], -2 * u, 0)
                    value = c[8] * q
                    value += c[0] * left(q, west, 2)
                    value += c[1] * left(q, west, 1)
                    value += c[2] * right(q, east, 1)
                    value += c[3] * right(q, east, 2)
                    value += c[4] * below(q, sv, 2)
                    value += c[5] * below(q, sv, 1)
                    value += c[6] * above(q, nv, 1)
                    value += c[7] * above(q, nv, 2)
                    partial[s, f] = value

    @pl.loop(0, species // 4)
    def _(it):
        quad(it, 4)

    if species % 4:
        quad(species // 4, species % 4)

    lanes = [[jnp.zeros((8, 128), F32) for _ in range(z.vregs)] for _ in range(2)]
    for s in range(species):
        for f in range(6):
            a, parity = f // 2, f % 2
            at = a * z.group + 2 * s
            cut = slice(0, 128) if parity == 0 else slice(width - 128, width)
            moved = roll(partial[s, f, :, cut], at - (0 if parity == 0 else 126), 1)
            k = at // 128
            lanes[parity][k] = jnp.where((lane1 >> 1) == (at % 128) // 2, moved, lanes[parity][k])
    for parity in range(2):
        for k in range(z.vregs):
            ends[parity, :, k * 128 : (k + 1) * 128] = lanes[parity][k]


def finish_kernel(
    z, order_in, mixing, from_b, partial, ends, aux, edges, arrived, out,
    turned, fixed, result, out_sem,
):
    place = lax.axis_index("tile")
    half = lax.axis_index("spec")
    first, last = place == 0, place == z.tiles - 1
    width, part, species, n_half = z.width, z.part, z.species, z.halves
    lane = lax.broadcasted_iota(jnp.int32, (8, width), 1)
    row = lax.broadcasted_iota(jnp.int32, (8, width), 0)
    lane1 = lax.broadcasted_iota(jnp.int32, (8, 128), 1)
    twelfth = 1.0 / 12.0
    holder = lax.div(width - 8 - 8 * place, part)

    def message(n, t, cut):
        rank = sum(jnp.where(n == h, z.rank[t][h], 0) for h in range(n_half))
        return arrived[rank, :, cut]

    places = order_in[0:1].astype(F32)
    slot = [jnp.sum(jnp.where(lane1[0:1] == f, places, 0.0)).astype(jnp.int32) for f in range(6)]

    def column(x, at):
        return x[:, at : at + 1]

    def spread(values, k):
        at = lane1 + k * 128
        return jnp.where(at < z.group, values[0], jnp.where(at < 2 * z.group, values[1], values[2]))

    last_column = []
    odd_end = (lane1 & 1) == 1
    for parity in range(2):
        end = z.tiles - 1 if parity == 0 else 0
        flux = reverse8(message(holder, end, slice((z.flux // 128) * 128, (z.flux // 128 + 1) * 128)))
        mul = []
        for a in range(3):
            f = 2 * a + parity
            fx, dp, inverse, new = (aux[f, n] for n in range(4))
            ghost_dp = column(flux, z.flux % 128 + a)
            if parity == 0:
                u0, p1 = column(fx, 0), column(fx, 1) * twelfth
                p0, b0 = u0 * twelfth, upwind(u0, ghost_dp + column(dp, 0))
                i0, i1 = column(inverse, 0), column(inverse, 1)
                mul.append((-p0 * i0, -p1 * i1, (7.0 * p0 + b0 + p1) * i0, -b0 * i0))
            else:
                u1 = column(flux, z.flux % 128 + 3 + a)
                p1, b1 = u1 * twelfth, upwind(u1, column(dp, width - 1) + ghost_dp)
                p0 = column(fx, width - 1) * twelfth
                i1 = 1.0 / (column(new, width - 1) - u1)
                last_column.append(i1)
                mul.append(
                    (p0 * column(inverse, width - 2), p1 * i1, (b1 - 7.0 * p1 - p0) * i1, -(7.0 * p1 + b1) * i1, p1 * i1, i1)
                )
        for k in range(z.vregs):
            cut = slice(k * 128, (k + 1) * 128)
            g = reverse8(message(half, end, cut))
            own, q = ends[parity, :, cut], edges[parity, :, cut]
            m = [spread([mul[a][n] for a in range(3)], k) for n in range(len(mul[0]))]
            if parity == 0:
                value = own + jnp.where(odd_end, m[1], m[0]) * g
                value += jnp.where(odd_end, 0.0, m[2] * roll(g, -1, 1) + m[3] * q)
            else:
                value = own * jnp.where(odd_end, m[5], 1.0) + jnp.where(odd_end, m[1], m[0]) * g
                value += jnp.where(odd_end, m[2] * roll(g, 1, 1) + m[3] * q + m[4] * roll(q, 1, 1), 0.0)
            fixed[parity, :, cut] = value

    cuts = [species * n // OUT_CHUNKS for n in range(OUT_CHUNKS + 1)]

    def store(n, special):
        for f in range(6):
            a, parity = f // 2, f % 2
            extra = special(a, parity) if special else None
            for s in range(cuts[n], cuts[n + 1]):
                at = a * z.group + 2 * s
                value = partial[s, f]
                end = fixed[parity, :, (at // 128) * 128 : (at // 128 + 1) * 128]
                end = wide(roll(end, -at if parity == 0 else 126 - at, 1), width)
                value = jnp.where(lane < 2 if parity == 0 else lane >= width - 2, end, value)
                if extra is not None:
                    value = extra(value, s, f)
                result[f, s] = value

    def send(n):
        some = pl.ds(cuts[n], cuts[n + 1] - cuts[n])
        for f in range(6):
            pltpu.make_async_copy(result.at[f, some], out.at[some, 0, slot[f]], out_sem).start()

    def everything(special=None):
        for n in range(OUT_CHUNKS):
            store(n, special)
            send(n)

    def gather():
        holder = jnp.where(first, n_half - 1, 0)
        pieces = []
        for k in range(z.vregs):
            cut = slice(k * 128, (k + 1) * 128)
            spare = from_b[z.extra + 8 * k : z.extra + 8 * k + 8, 0:128]
            mine = reverse8(jnp.where(first, edges[1, :, cut], edges[0, :, cut]))
            parts = []
            for t in reversed(range(z.tiles)):
                if t == 0:
                    x = jnp.where(first, mine, spare)
                elif t == z.tiles - 1:
                    x = jnp.where(first, spare, mine)
                else:
                    x = message(half, t, cut)
                if (k + 1) * 128 > z.flux:
                    x = jnp.where(lane1 + k * 128 < z.flux, x, message(holder, t, cut))
                parts.append(x)
            pieces.append(jnp.concatenate(parts, axis=0).T)
        turned[...] = jnp.concatenate(pieces, axis=0) if len(pieces) > 1 else pieces[0]
        return turned[z.flux2 : z.flux2 + 8]

    @pl.when(first)
    def _():
        flux = gather()

        def special(a, parity):
            if parity == 0:
                return None
            f, source = 2 * a + 1, (a + 2) % 3
            dp, inverse, v0, v1 = aux[f, 1], aux[f, 2], aux[f, 4], aux[f, 5]
            inverse = jnp.where(lane == width - 1, last_column[a], inverse)
            ghost_dp = flux[source : source + 1]
            p0, p1, b0 = v0 * twelfth, v1 * twelfth, upwind(v0, ghost_dp + dp)
            zero = jnp.zeros_like(dp)
            on0, on1 = row == 0, row < 2
            two = jnp.where(on1, -p0 * inverse, zero)
            one = jnp.where(on0, (7.0 * p0 + b0 + p1) * inverse, zero)
            none = jnp.where(on0, -b0 * inverse, zero)

            def extra(value, s, f):
                rows = turned[source * z.group + 8 * (s // 4) : source * z.group + 8 * (s // 4) + 8]
                u = s % 4
                q = mixing[s, 0, slot[f]]
                return value + two * roll(rows, -2 * u, 0) + one * roll(rows, -2 * u - 1, 0) + none * q

            return extra

        everything(special)

    @pl.when(last)
    def _():
        flux = gather()

        def special(a, parity):
            if parity == 1:
                return None
            f, source = 2 * a, (a + 1) % 3
            dp, inverse, new, v0 = (aux[f, n] for n in (1, 2, 3, 4))
            ghost_dp, v1 = flux[source : source + 1], flux[3 + source : 4 + source]
            on7, on6 = row == 7, row >= 6
            inverse = jnp.where(on7, 1.0 / jnp.where(on7, new - v1, 1.0), inverse)
            zero = jnp.zeros_like(dp)
            p0, p1, b1 = v0 * twelfth, v1 * twelfth, upwind(v1, dp + ghost_dp)
            two = jnp.where(on7, p1 * inverse, jnp.where(on6, roll(p0, -1, 0) * inverse, zero))
            one = jnp.where(on7, (b1 - 7.0 * p1 - p0) * inverse, zero)
            none = jnp.where(on7, -(7.0 * p1 + b1) * inverse, zero)
            back = jnp.where(on7, p1 * inverse, zero)
            scale = jnp.where(on7, inverse, 1.0)

            def extra(value, s, f):
                rows = turned[source * z.group + 8 * (s // 4) : source * z.group + 8 * (s // 4) + 8]
                u = s % 4
                q = mixing[s, 0, slot[f]]
                value = value * scale + two * roll(rows, 6 - 2 * u, 0) + one * roll(rows, 7 - 2 * u, 0)
                return value + none * q + back * roll(q, 1, 0)

            return extra

        everything(special)

    @pl.when(jnp.logical_not(first | last))
    def _():
        everything()

    for f in range(6):
        pltpu.make_async_copy(result.at[f], out.at[:, 0, slot[f]], out_sem).wait()


def local(mixing, layer_mass, mass_east, mass_north, face_slot):
    tiles = lax.axis_size("tile")
    halves = lax.axis_size("spec")
    z = Sizes(mixing, halves, tiles)
    assert z.rows == 8 and mixing.shape[1] == 1 and tiles > 2 and tiles % 2 == 0
    assert z.width == 8 * tiles and z.width % 128 == 0 and 128 % z.part == 0
    vmem = pl.BlockSpec(memory_space=pltpu.VMEM)
    hbm = pl.BlockSpec(memory_space=pl.ANY)
    params = pltpu.CompilerParams(vmem_limit_bytes=VMEM_LIMIT)
    cells = (z.species, 6, 8, z.width)

    def f32(*shape):
        return jax.ShapeDtypeStruct(shape, F32)

    packed = (
        f32(z.sent, z.width),
        f32(z.sent, z.width),
        f32(halves * tiles, 8, z.lanes),
        f32(2, 8, z.lanes),
        f32(z.own, 8, 128),
        jax.ShapeDtypeStruct((8, 128), jnp.int32),
    )
    to_a, to_b, messages, edges, own, order = pl.pallas_call(
        lambda *refs: pack_kernel(z, *refs),
        out_shape=packed,
        in_specs=[hbm] * 5,
        out_specs=[hbm] * 6,
        scratch_shapes=[pltpu.VMEM(x.shape, x.dtype) for x in packed]
        + [
            pltpu.SMEM((6,), jnp.int32),
            pltpu.VMEM(mixing.shape, F32),
            pltpu.VMEM((3,) + layer_mass.shape, F32),
            pltpu.SemaphoreType.DMA((4 + CHUNKS,)),
            pltpu.SemaphoreType.DMA((5 + 2 * halves,)),
        ],
        name="pack",
    )(face_slot, mixing, layer_mass, mass_east, mass_north)
    arrived = lax.all_to_all(
        messages, ("tile", "spec"), 0, 0, axis_index_groups=[list(z.order)], tiled=True
    )
    from_a = lax.ppermute(to_a, "tile", [(i, i ^ 1) for i in range(tiles)])
    pairs = [(i, (i + 1) % tiles) if i % 2 else (i, (i - 1) % tiles) for i in range(tiles)]
    from_b = lax.ppermute(to_b, "tile", pairs)
    mine = pl.pallas_call(
        lambda *refs: share_kernel(z, *refs),
        out_shape=f32(z.shared, 8, 128),
        in_specs=[vmem] * 3,
        out_specs=vmem,
        compiler_params=params,
        cost_estimate=pl.CostEstimate(flops=23 * 10**9, bytes_accessed=0, transcendentals=0),
        name="share",
    )(own, from_a, from_b)
    if halves == 2:
        others = lax.ppermute(mine, "spec", [(0, 1), (1, 0)])
    else:
        others = lax.all_gather(mine, "spec", axis=0, tiled=False)
    partial, ends, aux = pl.pallas_call(
        lambda *refs: interior_kernel(z, *refs),
        out_shape=(f32(*cells), f32(2, 8, z.lanes), f32(6, 6, 8, z.width)),
        in_specs=[vmem] * 6,
        out_specs=[vmem] * 3,
        scratch_shapes=[
            pltpu.SMEM((8, 128), jnp.int32),
            pltpu.VMEM((2 * z.flux, z.width), F32),
            pltpu.VMEM((2 * z.flux, z.width), F32),
            pltpu.VMEM((6, 9, 8, z.width), F32),
            pltpu.SemaphoreType.DMA,
        ],
        compiler_params=params,
        name="interior",
    )(order, mixing, from_a, from_b, mine, others)
    return pl.pallas_call(
        lambda *refs: finish_kernel(z, *refs),
        out_shape=f32(*mixing.shape),
        in_specs=[vmem] * 8,
        out_specs=hbm,
        scratch_shapes=[
            pltpu.VMEM((z.lanes, z.width), F32),
            pltpu.VMEM((2, 8, z.lanes), F32),
            pltpu.VMEM((6, z.species, 8, z.width), F32),
            pltpu.SemaphoreType.DMA,
        ],
        compiler_params=params,
        name="finish",
    )(order, mixing, from_b, partial, ends, aux, edges, arrived)


def solution(mesh):
    flux = P(None, None, "tile", "spec")
    cells = P("spec", None, None, "tile", None)
    return jax.shard_map(
        local,
        mesh=mesh,
        in_specs=(cells, flux, flux, flux, P()),
        out_specs=cells,
        check_vma=False,
    )
```

```python
import jax
import jax.numpy as jnp
from jax import lax
from jax.experimental import pallas as pl
from jax.experimental.pallas import tpu as pltpu
from jax.sharding import PartitionSpec as P

F32 = jnp.float32
VMEM_LIMIT = 12 << 20
CHUNKS = 2
OUT_CHUNKS = 4
ORDERS = {(16, 2): (
    19, 30, 2, 3, 17, 10, 15, 6, 20, 22, 16, 9, 25, 1, 5, 7,
    12, 31, 28, 0, 14, 27, 21, 8, 11, 26, 18, 13, 4, 29, 24, 23,
)}


def up(value, unit):
    return -(-value // unit) * unit


class Sizes:
    def __init__(self, mixing, halves, tiles):
        self.species, _, _, self.rows, self.width = mixing.shape
        self.tiles, self.halves = tiles, halves
        self.part = self.width // halves
        self.group = up(2 * self.species, 8)
        self.flux = 3 * self.group
        self.flux2 = self.flux + 8
        self.lanes = up(self.flux2 + 8, 128)
        self.vregs = self.lanes // 128
        self.dp_at = 2 * self.flux
        self.fy_at = self.dp_at + 8
        self.extra = self.fy_at + 8
        self.sent = self.extra + 8 * self.vregs
        self.per = 128 // self.part
        self.own = up(18, self.per) // self.per
        self.pieces = 21
        self.shared = up(self.pieces, self.per) // self.per
        natural = tuple(t * halves + n for n in range(halves) for t in range(tiles))
        self.order = ORDERS.get((tiles, halves), natural)
        ranks = {device: rank for rank, device in enumerate(self.order)}
        self.rank = [[ranks[t * halves + n] for n in range(halves)] for t in range(tiles)]


def slots(face_slot):
    return [sum(jnp.where(face_slot[s] == f, s, 0) for s in range(6)) for f in range(6)]


def roll(x, shift, axis):
    shift %= x.shape[axis]
    return pltpu.roll(x, shift, axis) if shift else x


def reverse8(x):
    row = lax.broadcasted_iota(jnp.int32, x.shape, 0)
    x = jnp.where((row & 1) == 0, roll(x, -1, 0), roll(x, 1, 0))
    x = jnp.where((row & 2) == 0, roll(x, -2, 0), roll(x, 2, 0))
    return roll(x, 4, 0)


def upwind(u, total):
    return 0.5 * jnp.abs(u) * (1.0 - jnp.abs(u / (0.5 * total)))


def column(x, at):
    return x[:, at : at + 1]


def spread(z, values, k):
    at = lax.broadcasted_iota(jnp.int32, (8, 128), 1) + k * 128
    return jnp.where(at < z.group, values[0], jnp.where(at < 2 * z.group, values[1], values[2]))


def wide(x, width):
    return jnp.concatenate([x] * (width // 128), axis=-1) if width > 128 else x


def side_by_side(tiles, per):
    tiles = tiles + [tiles[0]] * (per - len(tiles))
    return jnp.concatenate(tiles, axis=-1) if per > 1 else tiles[0]


def pack_kernel(
    z, slot_in, mixing_in, dp_in, fx_in, fy_in,
    to_a_out, to_b_out, out_out, edges_out, own_out, order_out,
    to_a, to_b, out, edges, own, order, face_slot, mixing, fluxes, sems, out_sems,
):
    cuts = [z.species * n // CHUNKS for n in range(CHUNKS + 1)]
    copies = [pltpu.make_async_copy(slot_in, face_slot, sems.at[0])]
    for c, ref in enumerate((dp_in, fx_in, fy_in)):
        copies.append(pltpu.make_async_copy(ref, fluxes.at[c], sems.at[1 + c]))
    for n in range(CHUNKS):
        some = pl.ds(cuts[n], cuts[n + 1] - cuts[n])
        copies.append(pltpu.make_async_copy(mixing_in.at[some], mixing.at[some], sems.at[4 + n]))
    for copy in copies:
        copy.start()
    place = lax.axis_index("tile")
    half = lax.axis_index("spec")
    copies[0].wait()
    slot = slots(face_slot)
    even = lax.rem(place, 2) == 0
    first, last = place == 0, place == z.tiles - 1
    width, part, species, n_half = z.width, z.part, z.species, z.halves
    lane = lax.broadcasted_iota(jnp.int32, (8, 128), 1)
    order[...] = sum(jnp.where(lane == f, slot[f], 0) for f in range(6))
    results = [
        pltpu.make_async_copy(x, y, out_sems.at[n])
        for n, (x, y) in enumerate(
            ((to_a, to_a_out), (to_b, to_b_out), (edges, edges_out), (own, own_out), (order, order_out))
        )
    ]
    results[4].start()
    for copy in copies[1:4]:
        copy.wait()
    raw = [[fluxes[c, 0, slot[f]] for f in range(6)] for c in range(3)]
    flat = [raw[c][f] for c in range(3) for f in range(6)]
    for n in range(z.own):
        own[n] = side_by_side(flat[n * z.per : (n + 1) * z.per], z.per)
    results[3].start()

    def both(low, high, at):
        to_a[pl.ds(at, low.shape[0])] = jnp.where(even, high, low)
        to_b[pl.ds(at, low.shape[0])] = jnp.where(even, low, high)

    def padded(x):
        return jnp.concatenate([x, jnp.zeros((8, width - part), F32)], axis=-1) if width > part else x

    pad = jnp.zeros((2, part), F32)
    low_dp = jnp.concatenate([x[0:1] for x in raw[0]] + [pad], axis=0)
    high_dp = jnp.concatenate([x[7:8] for x in raw[0]] + [pad], axis=0)
    low_fy = padded(jnp.concatenate([x[0:1] for x in raw[2]] + [pad], axis=0))
    both(padded(low_dp), padded(high_dp), z.dp_at)
    both(low_fy, low_fy, z.fy_at)

    columns = [[jnp.zeros((8, 128), F32) for _ in range(z.vregs)] for _ in range(2)]
    for parity in range(2):
        for a in range(3):
            f = 2 * a + parity
            if z.group > 2 * species:
                zero = jnp.zeros((z.group - 2 * species, width), F32)
                both(zero, zero, parity * z.flux + a * z.group + 2 * species)
            for c in range(2):
                at = z.flux2 + 3 * c + a
                edge = side_by_side([raw[c][f]] * z.per, z.per)
                moved = roll(edge, at - (0 if parity == 0 else 127), 1)
                k = at // 128
                columns[parity][k] = jnp.where(lane == at % 128, moved, columns[parity][k])
    for n in range(CHUNKS):
        copies[4 + n].wait()
        for s in range(cuts[n], cuts[n + 1]):
            for f in range(6):
                a, parity = f // 2, f % 2
                tile = mixing[s, 0, slot[f]]
                at = a * z.group + 2 * s
                both(tile[0:2], tile[6:8], parity * z.flux + at)
                edge = tile[:, :128] if parity == 0 else tile[:, width - 128 :]
                moved = roll(edge, at - (0 if parity == 0 else 126), 1)
                k = at // 128
                columns[parity][k] = jnp.where((lane >> 1) == (at % 128) // 2, moved, columns[parity][k])
    turned = [[reverse8(x) for x in lanes] for lanes in columns]
    for k in range(z.vregs):
        for parity in range(2):
            edges[parity, :, k * 128 : (k + 1) * 128] = columns[parity][k]
        spare = wide(jnp.where(first, turned[0][k], turned[1][k]), width)
        to_a[pl.ds(z.extra + 8 * k, 8)] = spare
        to_b[pl.ds(z.extra + 8 * k, 8)] = spare
    for n in range(3):
        results[n].start()

    ends = ((0, turned[1]), (z.tiles - 1, turned[0]))

    @pl.when(first | last)
    def _():
        rows, dps, fys = [], [], []
        for a in range(3):
            for_odd, for_even = (a + 1) % 3, (a + 2) % 3
            start = jnp.where(first, z.flux + for_odd * z.group, for_even * z.group)
            rows.append(to_b[pl.ds(pl.multiple_of(start, 8), z.group)])
            for c, values in ((0, dps), (2, fys)):
                values.append(jnp.where(first, raw[c][2 * for_odd + 1][0:1], raw[c][2 * for_even][7:8]))
        flux = jnp.concatenate(dps + fys + [pad], axis=0)
        flux = jnp.concatenate([jnp.where(half == n, flux, 0.0) for n in range(n_half)], axis=-1)
        rows += [flux, jnp.zeros((z.lanes - z.flux - 8, width), F32)]
        messages = jnp.concatenate(rows, axis=0).T
        for t in range(z.tiles):
            at = 8 * (z.tiles - 1 - t)
            for n in range(n_half):
                out[z.rank[t][n]] = messages[at : at + 8]
        for t, cols in ends:
            at = 8 * (z.tiles - 1 - t)
            k = z.flux2 // 128
            here = (lane >= z.flux2 % 128) & (lane < z.flux2 % 128 + 8)
            mixed = jnp.where(here, cols[k], messages[at : at + 8, k * 128 : (k + 1) * 128])
            for n in range(n_half):
                out[z.rank[t][n], :, k * 128 : (k + 1) * 128] = mixed
        copy = pltpu.make_async_copy(out, out_out, out_sems.at[5])
        copy.start()
        copy.wait()

    @pl.when(jnp.logical_not(first | last))
    def _():
        for t, cols in ends:
            for n in range(n_half):
                for k in range(z.vregs):
                    out[z.rank[t][n], :, k * 128 : (k + 1) * 128] = cols[k]
        copies = []
        for e, (t, _) in enumerate(ends):
            for n in range(n_half):
                at = z.rank[t][n]
                copies.append(pltpu.make_async_copy(out.at[at], out_out.at[at], out_sems.at[5 + e * n_half + n]))
        for copy in copies:
            copy.start()
        for copy in copies:
            copy.wait()

    for copy in results:
        copy.wait()


def share_kernel(z, own, from_a, from_b, out):
    even = lax.rem(lax.axis_index("tile"), 2) == 0
    part = z.part
    dp_a, dp_b = from_a[z.dp_at : z.dp_at + 8, :part], from_b[z.dp_at : z.dp_at + 8, :part]
    fy_a, fy_b = from_a[z.fy_at : z.fy_at + 8, :part], from_b[z.fy_at : z.fy_at + 8, :part]
    halo = [jnp.where(even, dp_b, dp_a), jnp.where(even, dp_a, dp_b), jnp.where(even, fy_a, fy_b)]
    flat = [own[n // z.per][:, (n % z.per) * part : (n % z.per + 1) * part] for n in range(18)] + halo
    for n in range(z.shared):
        out[n] = side_by_side(flat[n * z.per : (n + 1) * z.per], z.per)


def interior_kernel(
    z, order_in, mixing, from_a, from_b, mine, others, partial, ends, aux, early,
    order, south, north, coef, order_sem,
):
    fetch = pltpu.make_async_copy(order_in, order, order_sem)
    fetch.start()
    place = lax.axis_index("tile")
    half = lax.axis_index("spec")
    even = lax.rem(place, 2) == 0
    first, last = place == 0, place == z.tiles - 1
    width, part, species = z.width, z.part, z.species
    lane = lax.broadcasted_iota(jnp.int32, (8, width), 1)
    row = lax.broadcasted_iota(jnp.int32, (8, width), 0)
    lane1 = lax.broadcasted_iota(jnp.int32, (8, 128), 1)

    a_rows, b_rows = from_a[0 : z.dp_at], from_b[0 : z.dp_at]
    south[...] = jnp.where(even, b_rows, a_rows)
    north[...] = jnp.where(even, a_rows, b_rows)

    full = []
    for n in range(z.pieces):
        cut = slice((n % z.per) * part, (n % z.per + 1) * part)
        if z.halves == 2:
            x, y = mine[n // z.per][:, cut], others[n // z.per][:, cut]
            parts = [jnp.where(half == 0, x, y), jnp.where(half == 0, y, x)]
        else:
            parts = [others[h, n // z.per][:, cut] for h in range(z.halves)]
        full.append(jnp.concatenate(parts, axis=-1))
    dp_south, dp_north, fy_north = full[18:]

    def left(x, ghost, n):
        return pltpu.roll(jnp.where(lane >= width - n, ghost, x), n, 1)

    def right(x, ghost, n):
        return pltpu.roll(jnp.where(lane < n, ghost, x), width - n, 1)

    def below(x, ghost, n):
        return pltpu.roll(jnp.where(row >= 8 - n, ghost, x), n, 0)

    def above(x, ghost, n):
        return pltpu.roll(jnp.where(row < n, ghost, x), 8 - n, 0)

    for f in range(6):
        parity = f % 2
        dp, fx, fy = full[f], full[6 + f], full[12 + f]
        if parity == 0:
            west, east, east_u = dp, full[f + 1], full[6 + f + 1]
            s_end, n_end, v_end = roll(dp_south, 7 - (f - 1) % 6, 0), dp, 0.0
            known = jnp.logical_not(last & (row == 7))
        else:
            west, east, east_u = full[f - 1], dp, 0.0
            s_end, n_end, v_end = dp, roll(dp_north, -((f + 1) % 6), 0), roll(fy_north, -((f + 1) % 6), 0)
            known = lane < width - 1
        dp_w, dp_e = left(dp, west, 1), right(dp, east, 1)
        u0, u1 = fx, right(fx, east_u, 1)
        dp_s = below(dp, jnp.where(first, s_end, roll(dp_south, 7 - f, 0)), 1)
        dp_n = above(dp, jnp.where(last, n_end, roll(dp_north, -f, 0)), 1)
        v0, v1 = fy, above(fy, jnp.where(last, v_end, roll(fy_north, -f, 0)), 1)
        new = dp - (u1 - u0) - (v1 - v0)
        inverse = jnp.where(known, 1.0 / jnp.where(known, new, 1.0), 1.0)
        for n, x in enumerate((fx, dp, inverse, new, v0, v1)):
            aux[f, n] = x
        center = dp
        for n, (w0, w1, d0, d1) in enumerate(((u0, u1, dp_w, dp_e), (v0, v1, dp_s, dp_n))):
            b0, b1 = upwind(w0, d0 + dp), upwind(w1, dp + d1)
            if n == 0 and parity == 0:
                b0 = jnp.where(lane == 0, 0.0, b0)
            if n == 1 and parity == 1:
                b0 = jnp.where(first & (row == 0), 0.0, b0)
            p0, p1 = w0 * (1.0 / 12.0), w1 * (1.0 / 12.0)
            coef[f, 4 * n] = -p0 * inverse
            coef[f, 4 * n + 1] = (7.0 * p0 + b0 + p1) * inverse
            coef[f, 4 * n + 2] = (-p0 - 7.0 * p1 + b1) * inverse
            coef[f, 4 * n + 3] = p1 * inverse
            center = center + (7.0 * p0 - b0) - (7.0 * p1 + b1)
        coef[f, 8] = center * inverse

    block = z.flux
    south_at, north_at = jnp.where(first, block, 0), jnp.where(last, 0, block)
    fetch.wait()
    slot = [order[0, f] for f in range(6)]

    def quad(it, count):
        for a in range(3):
            a_s, a_n = jnp.where(first, (a + 2) % 3, a), jnp.where(last, (a + 1) % 3, a)

            def ghosts(ref, at, ref_a):
                return ref[pl.ds(pl.multiple_of(at + ref_a * z.group + 8 * it, 8), 8)]

            south_rows = [ghosts(south, south_at, a_s), jnp.where(first, 0.0, ghosts(south, block, a))]
            north_rows = [jnp.where(last, 0.0, ghosts(north, 0, a)), ghosts(north, north_at, a_n)]
            fe, fo = 2 * a, 2 * a + 1
            ce = [coef[fe, n] for n in range(9)]
            co = [coef[fo, n] for n in range(9)]
            for u in range(count):
                s = 4 * it + u
                qe, qo = mixing[s, 0, slot[fe]], mixing[s, 0, slot[fo]]
                for q, west, east, c, parity, f in ((qe, 0.0, qo, ce, 0, fe), (qo, qe, 0.0, co, 1, fo)):
                    sv = roll(south_rows[parity], 6 - 2 * u, 0)
                    nv = roll(north_rows[parity], -2 * u, 0)
                    value = c[8] * q
                    value += c[0] * left(q, west, 2)
                    value += c[1] * left(q, west, 1)
                    value += c[2] * right(q, east, 1)
                    value += c[3] * right(q, east, 2)
                    value += c[4] * below(q, sv, 2)
                    value += c[5] * below(q, sv, 1)
                    value += c[6] * above(q, nv, 1)
                    value += c[7] * above(q, nv, 2)
                    partial[s, f] = value

    @pl.loop(0, species // 4)
    def _(it):
        quad(it, 4)

    if species % 4:
        quad(species // 4, species % 4)

    for parity in range(2):
        values = []
        for a in range(3):
            f = 2 * a + parity
            fx, dp, inverse, new = (aux[f, n] for n in range(4))
            if parity == 0:
                u0, p0, p1 = column(fx, 0), column(fx, 0) * (1.0 / 12.0), column(fx, 1) * (1.0 / 12.0)
                i0, i1 = column(inverse, 0), column(inverse, 1)
                values.append((u0, column(dp, 0), i0, -p0 * i0, (7.0 * p0 + p1) * i0, -p1 * i1))
            else:
                p0 = column(fx, width - 1) * (1.0 / 12.0)
                i0 = column(inverse, width - 2)
                values.append((column(dp, width - 1), column(new, width - 1), p0, p0 * i0, i0))
        for k in range(z.vregs):
            x = [spread(z, [v[n] for v in values], k) for n in range(len(values[0]))]
            if parity == 0:
                x[3] = jnp.where((lane1 & 1) == 1, x[5], x[3])
            for n in range(5):
                early[parity, n, :, k * 128 : (k + 1) * 128] = x[n]

    lanes = [[jnp.zeros((8, 128), F32) for _ in range(z.vregs)] for _ in range(2)]
    for s in range(species):
        for f in range(6):
            a, parity = f // 2, f % 2
            at = a * z.group + 2 * s
            cut = slice(0, 128) if parity == 0 else slice(width - 128, width)
            moved = roll(partial[s, f, :, cut], at - (0 if parity == 0 else 126), 1)
            k = at // 128
            lanes[parity][k] = jnp.where((lane1 >> 1) == (at % 128) // 2, moved, lanes[parity][k])
    for parity in range(2):
        for k in range(z.vregs):
            ends[parity, :, k * 128 : (k + 1) * 128] = lanes[parity][k]


def finish_kernel(
    z, order_in, mixing, from_b, partial, ends, aux, early, edges, arrived, out,
    turned, fixed, result, out_sem,
):
    place = lax.axis_index("tile")
    half = lax.axis_index("spec")
    first, last = place == 0, place == z.tiles - 1
    width, part, species, n_half = z.width, z.part, z.species, z.halves
    lane = lax.broadcasted_iota(jnp.int32, (8, width), 1)
    row = lax.broadcasted_iota(jnp.int32, (8, width), 0)
    lane1 = lax.broadcasted_iota(jnp.int32, (8, 128), 1)
    twelfth = 1.0 / 12.0
    holder = lax.div(width - 8 - 8 * place, part)

    def message(n, t, cut):
        rank = sum(jnp.where(n == h, z.rank[t][h], 0) for h in range(n_half))
        return arrived[rank, :, cut]

    places = order_in[0:1].astype(F32)
    slot = [jnp.sum(jnp.where(lane1[0:1] == f, places, 0.0)).astype(jnp.int32) for f in range(6)]

    east_flow = []
    odd_end = (lane1 & 1) == 1
    for parity in range(2):
        end = z.tiles - 1 if parity == 0 else 0
        flux = reverse8(message(holder, end, slice((z.flux // 128) * 128, (z.flux // 128 + 1) * 128)))
        ghost_dp = [column(flux, z.flux % 128 + a) for a in range(3)]
        if parity == 1:
            east_flow = [column(flux, z.flux % 128 + 3 + a) for a in range(3)]
        for k in range(z.vregs):
            cut = slice(k * 128, (k + 1) * 128)
            g = reverse8(message(half, end, cut))
            own, q = ends[parity, :, cut], edges[parity, :, cut]
            m = [early[parity, n, :, cut] for n in range(5)]
            ghost = spread(z, ghost_dp, k)
            if parity == 0:
                b = upwind(m[0], ghost + m[1]) * m[2]
                value = own + m[3] * g + jnp.where(odd_end, 0.0, (m[4] + b) * roll(g, -1, 1) - b * q)
            else:
                u = spread(z, east_flow, k)
                p, b = u * twelfth, upwind(u, m[0] + ghost)
                last_cell = own + p * (g + roll(q, 1, 1)) + (b - 7.0 * p - m[2]) * roll(g, 1, 1) - (7.0 * p + b) * q
                value = jnp.where(odd_end, last_cell / (m[1] - u), own + m[3] * g)
            fixed[parity, :, cut] = value

    cuts = [species * n // OUT_CHUNKS for n in range(OUT_CHUNKS + 1)]

    def store(n, special):
        for f in range(6):
            a, parity = f // 2, f % 2
            extra = special(a, parity) if special else None
            for s in range(cuts[n], cuts[n + 1]):
                at = a * z.group + 2 * s
                value = partial[s, f]
                end = fixed[parity, :, (at // 128) * 128 : (at // 128 + 1) * 128]
                end = wide(roll(end, -at if parity == 0 else 126 - at, 1), width)
                value = jnp.where(lane < 2 if parity == 0 else lane >= width - 2, end, value)
                if extra is not None:
                    value = extra(value, s, f)
                result[f, s] = value

    def send(n):
        some = pl.ds(cuts[n], cuts[n + 1] - cuts[n])
        for f in range(6):
            pltpu.make_async_copy(result.at[f, some], out.at[some, 0, slot[f]], out_sem).start()

    def everything(special=None):
        for n in range(OUT_CHUNKS):
            store(n, special)
            send(n)

    def gather():
        holder = jnp.where(first, n_half - 1, 0)
        pieces = []
        for k in range(z.vregs):
            cut = slice(k * 128, (k + 1) * 128)
            spare = from_b[z.extra + 8 * k : z.extra + 8 * k + 8, 0:128]
            mine = reverse8(jnp.where(first, edges[1, :, cut], edges[0, :, cut]))
            parts = []
            for t in reversed(range(z.tiles)):
                if t == 0:
                    x = jnp.where(first, mine, spare)
                elif t == z.tiles - 1:
                    x = jnp.where(first, spare, mine)
                else:
                    x = message(half, t, cut)
                if (k + 1) * 128 > z.flux:
                    x = jnp.where(lane1 + k * 128 < z.flux, x, message(holder, t, cut))
                parts.append(x)
            pieces.append(jnp.concatenate(parts, axis=0).T)
        turned[...] = jnp.concatenate(pieces, axis=0) if len(pieces) > 1 else pieces[0]
        return turned[z.flux2 : z.flux2 + 8]

    @pl.when(first)
    def _():
        flux = gather()

        def special(a, parity):
            if parity == 0:
                return None
            f, source = 2 * a + 1, (a + 2) % 3
            dp, inverse, new, v0, v1 = (aux[f, n] for n in range(1, 6))
            east = lane == width - 1
            inverse = jnp.where(east, 1.0 / jnp.where(east, new - east_flow[a], 1.0), inverse)
            ghost_dp = flux[source : source + 1]
            p0, p1, b0 = v0 * twelfth, v1 * twelfth, upwind(v0, ghost_dp + dp)
            zero = jnp.zeros_like(dp)
            on0, on1 = row == 0, row < 2
            two = jnp.where(on1, -p0 * inverse, zero)
            one = jnp.where(on0, (7.0 * p0 + b0 + p1) * inverse, zero)
            none = jnp.where(on0, -b0 * inverse, zero)

            def extra(value, s, f):
                rows = turned[source * z.group + 8 * (s // 4) : source * z.group + 8 * (s // 4) + 8]
                u = s % 4
                q = mixing[s, 0, slot[f]]
                return value + two * roll(rows, -2 * u, 0) + one * roll(rows, -2 * u - 1, 0) + none * q

            return extra

        everything(special)

    @pl.when(last)
    def _():
        flux = gather()

        def special(a, parity):
            if parity == 1:
                return None
            f, source = 2 * a, (a + 1) % 3
            dp, inverse, new, v0 = (aux[f, n] for n in (1, 2, 3, 4))
            ghost_dp, v1 = flux[source : source + 1], flux[3 + source : 4 + source]
            on7, on6 = row == 7, row >= 6
            inverse = jnp.where(on7, 1.0 / jnp.where(on7, new - v1, 1.0), inverse)
            zero = jnp.zeros_like(dp)
            p0, p1, b1 = v0 * twelfth, v1 * twelfth, upwind(v1, dp + ghost_dp)
            two = jnp.where(on7, p1 * inverse, jnp.where(on6, roll(p0, -1, 0) * inverse, zero))
            one = jnp.where(on7, (b1 - 7.0 * p1 - p0) * inverse, zero)
            none = jnp.where(on7, -(7.0 * p1 + b1) * inverse, zero)
            back = jnp.where(on7, p1 * inverse, zero)
            scale = jnp.where(on7, inverse, 1.0)

            def extra(value, s, f):
                rows = turned[source * z.group + 8 * (s // 4) : source * z.group + 8 * (s // 4) + 8]
                u = s % 4
                q = mixing[s, 0, slot[f]]
                value = value * scale + two * roll(rows, 6 - 2 * u, 0) + one * roll(rows, 7 - 2 * u, 0)
                return value + none * q + back * roll(q, 1, 0)

            return extra

        everything(special)

    @pl.when(jnp.logical_not(first | last))
    def _():
        everything()

    for f in range(6):
        pltpu.make_async_copy(result.at[f], out.at[:, 0, slot[f]], out_sem).wait()


def local(mixing, layer_mass, mass_east, mass_north, face_slot):
    tiles = lax.axis_size("tile")
    halves = lax.axis_size("spec")
    z = Sizes(mixing, halves, tiles)
    assert z.rows == 8 and mixing.shape[1] == 1 and tiles > 2 and tiles % 2 == 0
    assert z.width == 8 * tiles and z.width % 128 == 0 and 128 % z.part == 0
    vmem = pl.BlockSpec(memory_space=pltpu.VMEM)
    hbm = pl.BlockSpec(memory_space=pl.ANY)
    params = pltpu.CompilerParams(vmem_limit_bytes=VMEM_LIMIT)
    cells = (z.species, 6, 8, z.width)

    def f32(*shape):
        return jax.ShapeDtypeStruct(shape, F32)

    packed = (
        f32(z.sent, z.width),
        f32(z.sent, z.width),
        f32(halves * tiles, 8, z.lanes),
        f32(2, 8, z.lanes),
        f32(z.own, 8, 128),
        jax.ShapeDtypeStruct((8, 128), jnp.int32),
    )
    to_a, to_b, messages, edges, own, order = pl.pallas_call(
        lambda *refs: pack_kernel(z, *refs),
        out_shape=packed,
        in_specs=[hbm] * 5,
        out_specs=[hbm] * 6,
        scratch_shapes=[pltpu.VMEM(x.shape, x.dtype) for x in packed]
        + [
            pltpu.SMEM((6,), jnp.int32),
            pltpu.VMEM(mixing.shape, F32),
            pltpu.VMEM((3,) + layer_mass.shape, F32),
            pltpu.SemaphoreType.DMA((4 + CHUNKS,)),
            pltpu.SemaphoreType.DMA((5 + 2 * halves,)),
        ],
        name="pack",
    )(face_slot, mixing, layer_mass, mass_east, mass_north)
    arrived = lax.all_to_all(
        messages, ("tile", "spec"), 0, 0, axis_index_groups=[list(z.order)], tiled=True
    )
    from_a = lax.ppermute(to_a, "tile", [(i, i ^ 1) for i in range(tiles)])
    pairs = [(i, (i + 1) % tiles) if i % 2 else (i, (i - 1) % tiles) for i in range(tiles)]
    from_b = lax.ppermute(to_b, "tile", pairs)
    mine = pl.pallas_call(
        lambda *refs: share_kernel(z, *refs),
        out_shape=f32(z.shared, 8, 128),
        in_specs=[vmem] * 3,
        out_specs=vmem,
        compiler_params=params,
        cost_estimate=pl.CostEstimate(flops=23 * 10**9, bytes_accessed=0, transcendentals=0),
        name="share",
    )(own, from_a, from_b)
    if halves == 2:
        others = lax.ppermute(mine, "spec", [(0, 1), (1, 0)])
    else:
        others = lax.all_gather(mine, "spec", axis=0, tiled=False)
    partial, ends, aux, early = pl.pallas_call(
        lambda *refs: interior_kernel(z, *refs),
        out_shape=(f32(*cells), f32(2, 8, z.lanes), f32(6, 6, 8, z.width), f32(2, 5, 8, z.lanes)),
        in_specs=[vmem] * 6,
        out_specs=[vmem] * 4,
        scratch_shapes=[
            pltpu.SMEM((8, 128), jnp.int32),
            pltpu.VMEM((2 * z.flux, z.width), F32),
            pltpu.VMEM((2 * z.flux, z.width), F32),
            pltpu.VMEM((6, 9, 8, z.width), F32),
            pltpu.SemaphoreType.DMA,
        ],
        compiler_params=params,
        name="interior",
    )(order, mixing, from_a, from_b, mine, others)
    return pl.pallas_call(
        lambda *refs: finish_kernel(z, *refs),
        out_shape=f32(*mixing.shape),
        in_specs=[vmem] * 9,
        out_specs=hbm,
        scratch_shapes=[
            pltpu.VMEM((z.lanes, z.width), F32),
            pltpu.VMEM((2, 8, z.lanes), F32),
            pltpu.VMEM((6, z.species, 8, z.width), F32),
            pltpu.SemaphoreType.DMA,
        ],
        compiler_params=params,
        name="finish",
    )(order, mixing, from_b, partial, ends, aux, early, edges, arrived)


def solution(mesh):
    flux = P(None, None, "tile", "spec")
    cells = P("spec", None, None, "tile", None)
    return jax.shard_map(
        local,
        mesh=mesh,
        in_specs=(cells, flux, flux, flux, P()),
        out_specs=cells,
        check_vma=False,
    )
```

```python
import jax
import jax.numpy as jnp
from jax import lax
from jax.experimental import pallas as pl
from jax.experimental.pallas import tpu as pltpu
from jax.sharding import PartitionSpec as P

F32 = jnp.float32
VMEM_LIMIT = 12 << 20
CHUNKS = 2
OUT_CHUNKS = 6
ORDERS = {(16, 2): (
    19, 30, 2, 7, 17, 10, 26, 18, 20, 22, 16, 9, 25, 1, 5, 3,
    12, 31, 28, 0, 14, 27, 21, 8, 11, 15, 6, 13, 4, 29, 24, 23,
)}


def up(value, unit):
    return -(-value // unit) * unit


class Sizes:
    def __init__(self, mixing, halves, tiles):
        self.species, _, _, self.rows, self.width = mixing.shape
        self.tiles, self.halves = tiles, halves
        self.part = self.width // halves
        self.group = up(2 * self.species, 8)
        self.flux = 3 * self.group
        self.flux2 = self.flux + 8
        self.lanes = up(self.flux2 + 8, 128)
        self.vregs = self.lanes // 128
        self.dp_at = 2 * self.flux
        self.fy_at = self.dp_at + 8
        self.extra = self.fy_at + 8
        self.sent = self.extra + 8 * self.vregs
        self.per = 128 // self.part
        self.own = up(18, self.per) // self.per
        self.pieces = 21
        self.shared = up(self.pieces, self.per) // self.per
        natural = tuple(t * halves + n for n in range(halves) for t in range(tiles))
        self.order = ORDERS.get((tiles, halves), natural)
        ranks = {device: rank for rank, device in enumerate(self.order)}
        self.rank = [[ranks[t * halves + n] for n in range(halves)] for t in range(tiles)]


def slots(face_slot):
    return [sum(jnp.where(face_slot[s] == f, s, 0) for s in range(6)) for f in range(6)]


def roll(x, shift, axis):
    shift %= x.shape[axis]
    return pltpu.roll(x, shift, axis) if shift else x


def reverse8(x):
    row = lax.broadcasted_iota(jnp.int32, x.shape, 0)
    x = jnp.where((row & 1) == 0, roll(x, -1, 0), roll(x, 1, 0))
    x = jnp.where((row & 2) == 0, roll(x, -2, 0), roll(x, 2, 0))
    return roll(x, 4, 0)


def upwind(u, total):
    return 0.5 * jnp.abs(u) * (1.0 - jnp.abs(u / (0.5 * total)))


def column(x, at):
    return x[:, at : at + 1]


def spread(z, values, k):
    at = lax.broadcasted_iota(jnp.int32, (8, 128), 1) + k * 128
    return jnp.where(at < z.group, values[0], jnp.where(at < 2 * z.group, values[1], values[2]))


def wide(x, width):
    return jnp.concatenate([x] * (width // 128), axis=-1) if width > 128 else x


def side_by_side(tiles, per):
    tiles = tiles + [tiles[0]] * (per - len(tiles))
    return jnp.concatenate(tiles, axis=-1) if per > 1 else tiles[0]


def pack_kernel(
    z, slot_in, mixing_in, dp_in, fx_in, fy_in,
    to_a_out, to_b_out, out_out, edges_out, own_out, order_out,
    to_a, to_b, out, edges, own, order, face_slot, mixing, fluxes, sems, out_sems,
):
    cuts = [z.species * n // CHUNKS for n in range(CHUNKS + 1)]
    copies = [pltpu.make_async_copy(slot_in, face_slot, sems.at[0])]
    for c, ref in enumerate((dp_in, fx_in, fy_in)):
        copies.append(pltpu.make_async_copy(ref, fluxes.at[c], sems.at[1 + c]))
    for n in range(CHUNKS):
        some = pl.ds(cuts[n], cuts[n + 1] - cuts[n])
        copies.append(pltpu.make_async_copy(mixing_in.at[some], mixing.at[some], sems.at[4 + n]))
    for copy in copies:
        copy.start()
    place = lax.axis_index("tile")
    half = lax.axis_index("spec")
    copies[0].wait()
    slot = slots(face_slot)
    even = lax.rem(place, 2) == 0
    first, last = place == 0, place == z.tiles - 1
    width, part, species, n_half = z.width, z.part, z.species, z.halves
    lane = lax.broadcasted_iota(jnp.int32, (8, 128), 1)
    order[...] = sum(jnp.where(lane == f, slot[f], 0) for f in range(6))
    results = [
        pltpu.make_async_copy(x, y, out_sems.at[n])
        for n, (x, y) in enumerate(
            ((to_a, to_a_out), (to_b, to_b_out), (edges, edges_out), (own, own_out), (order, order_out))
        )
    ]
    results[4].start()
    for copy in copies[1:4]:
        copy.wait()
    raw = [[fluxes[c, 0, slot[f]] for f in range(6)] for c in range(3)]
    flat = [raw[c][f] for c in range(3) for f in range(6)]
    for n in range(z.own):
        own[n] = side_by_side(flat[n * z.per : (n + 1) * z.per], z.per)
    results[3].start()

    def both(low, high, at):
        to_a[pl.ds(at, low.shape[0])] = jnp.where(even, high, low)
        to_b[pl.ds(at, low.shape[0])] = jnp.where(even, low, high)

    def padded(x):
        return jnp.concatenate([x, jnp.zeros((8, width - part), F32)], axis=-1) if width > part else x

    pad = jnp.zeros((2, part), F32)
    low_dp = jnp.concatenate([x[0:1] for x in raw[0]] + [pad], axis=0)
    high_dp = jnp.concatenate([x[7:8] for x in raw[0]] + [pad], axis=0)
    low_fy = padded(jnp.concatenate([x[0:1] for x in raw[2]] + [pad], axis=0))
    both(padded(low_dp), padded(high_dp), z.dp_at)
    both(low_fy, low_fy, z.fy_at)

    columns = [[jnp.zeros((8, 128), F32) for _ in range(z.vregs)] for _ in range(2)]
    for parity in range(2):
        for a in range(3):
            f = 2 * a + parity
            if z.group > 2 * species:
                zero = jnp.zeros((z.group - 2 * species, width), F32)
                both(zero, zero, parity * z.flux + a * z.group + 2 * species)
            for c in range(2):
                at = z.flux2 + 3 * c + a
                edge = side_by_side([raw[c][f]] * z.per, z.per)
                moved = roll(edge, at - (0 if parity == 0 else 127), 1)
                k = at // 128
                columns[parity][k] = jnp.where(lane == at % 128, moved, columns[parity][k])
    for n in range(CHUNKS):
        copies[4 + n].wait()
        for s in range(cuts[n], cuts[n + 1]):
            for f in range(6):
                a, parity = f // 2, f % 2
                tile = mixing[s, 0, slot[f]]
                at = a * z.group + 2 * s
                both(tile[0:2], tile[6:8], parity * z.flux + at)
                edge = tile[:, :128] if parity == 0 else tile[:, width - 128 :]
                moved = roll(edge, at - (0 if parity == 0 else 126), 1)
                k = at // 128
                columns[parity][k] = jnp.where((lane >> 1) == (at % 128) // 2, moved, columns[parity][k])
    turned = [[reverse8(x) for x in lanes] for lanes in columns]
    for k in range(z.vregs):
        for parity in range(2):
            edges[parity, :, k * 128 : (k + 1) * 128] = columns[parity][k]
        spare = wide(jnp.where(first, turned[0][k], turned[1][k]), width)
        to_a[pl.ds(z.extra + 8 * k, 8)] = spare
        to_b[pl.ds(z.extra + 8 * k, 8)] = spare
    for n in range(3):
        results[n].start()

    ends = ((0, turned[1]), (z.tiles - 1, turned[0]))

    @pl.when(first | last)
    def _():
        rows, dps, fys = [], [], []
        for a in range(3):
            for_odd, for_even = (a + 1) % 3, (a + 2) % 3
            start = jnp.where(first, z.flux + for_odd * z.group, for_even * z.group)
            rows.append(to_b[pl.ds(pl.multiple_of(start, 8), z.group)])
            for c, values in ((0, dps), (2, fys)):
                values.append(jnp.where(first, raw[c][2 * for_odd + 1][0:1], raw[c][2 * for_even][7:8]))
        flux = jnp.concatenate(dps + fys + [pad], axis=0)
        flux = jnp.concatenate([jnp.where(half == n, flux, 0.0) for n in range(n_half)], axis=-1)
        rows += [flux, jnp.zeros((z.lanes - z.flux - 8, width), F32)]
        messages = jnp.concatenate(rows, axis=0).T
        for t in range(z.tiles):
            at = 8 * (z.tiles - 1 - t)
            for n in range(n_half):
                out[z.rank[t][n]] = messages[at : at + 8]
        for t, cols in ends:
            at = 8 * (z.tiles - 1 - t)
            k = z.flux2 // 128
            here = (lane >= z.flux2 % 128) & (lane < z.flux2 % 128 + 8)
            mixed = jnp.where(here, cols[k], messages[at : at + 8, k * 128 : (k + 1) * 128])
            for n in range(n_half):
                out[z.rank[t][n], :, k * 128 : (k + 1) * 128] = mixed
        copy = pltpu.make_async_copy(out, out_out, out_sems.at[5])
        copy.start()
        copy.wait()

    @pl.when(jnp.logical_not(first | last))
    def _():
        for t, cols in ends:
            for n in range(n_half):
                for k in range(z.vregs):
                    out[z.rank[t][n], :, k * 128 : (k + 1) * 128] = cols[k]
        copies = []
        for e, (t, _) in enumerate(ends):
            for n in range(n_half):
                at = z.rank[t][n]
                copies.append(pltpu.make_async_copy(out.at[at], out_out.at[at], out_sems.at[5 + e * n_half + n]))
        for copy in copies:
            copy.start()
        for copy in copies:
            copy.wait()

    for copy in results:
        copy.wait()


def share_kernel(z, own, from_a, from_b, out):
    even = lax.rem(lax.axis_index("tile"), 2) == 0
    part = z.part
    dp_a, dp_b = from_a[z.dp_at : z.dp_at + 8, :part], from_b[z.dp_at : z.dp_at + 8, :part]
    fy_a, fy_b = from_a[z.fy_at : z.fy_at + 8, :part], from_b[z.fy_at : z.fy_at + 8, :part]
    halo = [jnp.where(even, dp_b, dp_a), jnp.where(even, dp_a, dp_b), jnp.where(even, fy_a, fy_b)]
    flat = [own[n // z.per][:, (n % z.per) * part : (n % z.per + 1) * part] for n in range(18)] + halo
    for n in range(z.shared):
        out[n] = side_by_side(flat[n * z.per : (n + 1) * z.per], z.per)


def interior_kernel(
    z, order_in, mixing, from_a, from_b, mine, others, partial, ends, aux, early,
    order, south, north, coef, order_sem,
):
    fetch = pltpu.make_async_copy(order_in, order, order_sem)
    fetch.start()
    place = lax.axis_index("tile")
    half = lax.axis_index("spec")
    even = lax.rem(place, 2) == 0
    first, last = place == 0, place == z.tiles - 1
    width, part, species = z.width, z.part, z.species
    lane = lax.broadcasted_iota(jnp.int32, (8, width), 1)
    row = lax.broadcasted_iota(jnp.int32, (8, width), 0)
    lane1 = lax.broadcasted_iota(jnp.int32, (8, 128), 1)

    a_rows, b_rows = from_a[0 : z.dp_at], from_b[0 : z.dp_at]
    south[...] = jnp.where(even, b_rows, a_rows)
    north[...] = jnp.where(even, a_rows, b_rows)

    full = []
    for n in range(z.pieces):
        cut = slice((n % z.per) * part, (n % z.per + 1) * part)
        if z.halves == 2:
            x, y = mine[n // z.per][:, cut], others[n // z.per][:, cut]
            parts = [jnp.where(half == 0, x, y), jnp.where(half == 0, y, x)]
        else:
            parts = [others[h, n // z.per][:, cut] for h in range(z.halves)]
        full.append(jnp.concatenate(parts, axis=-1))
    dp_south, dp_north, fy_north = full[18:]

    def left(x, ghost, n):
        return pltpu.roll(jnp.where(lane >= width - n, ghost, x), n, 1)

    def right(x, ghost, n):
        return pltpu.roll(jnp.where(lane < n, ghost, x), width - n, 1)

    def below(x, ghost, n):
        return pltpu.roll(jnp.where(row >= 8 - n, ghost, x), n, 0)

    def above(x, ghost, n):
        return pltpu.roll(jnp.where(row < n, ghost, x), 8 - n, 0)

    for f in range(6):
        parity = f % 2
        dp, fx, fy = full[f], full[6 + f], full[12 + f]
        if parity == 0:
            west, east, east_u = dp, full[f + 1], full[6 + f + 1]
            s_end, n_end, v_end = roll(dp_south, 7 - (f - 1) % 6, 0), dp, 0.0
            known = jnp.logical_not(last & (row == 7))
        else:
            west, east, east_u = full[f - 1], dp, 0.0
            s_end, n_end, v_end = dp, roll(dp_north, -((f + 1) % 6), 0), roll(fy_north, -((f + 1) % 6), 0)
            known = lane < width - 1
        dp_w, dp_e = left(dp, west, 1), right(dp, east, 1)
        u0, u1 = fx, right(fx, east_u, 1)
        dp_s = below(dp, jnp.where(first, s_end, roll(dp_south, 7 - f, 0)), 1)
        dp_n = above(dp, jnp.where(last, n_end, roll(dp_north, -f, 0)), 1)
        v0, v1 = fy, above(fy, jnp.where(last, v_end, roll(fy_north, -f, 0)), 1)
        new = dp - (u1 - u0) - (v1 - v0)
        inverse = jnp.where(known, 1.0 / jnp.where(known, new, 1.0), 1.0)
        for n, x in enumerate((fx, dp, inverse, new, v0, v1)):
            aux[f, n] = x
        center = dp
        for n, (w0, w1, d0, d1) in enumerate(((u0, u1, dp_w, dp_e), (v0, v1, dp_s, dp_n))):
            b0, b1 = upwind(w0, d0 + dp), upwind(w1, dp + d1)
            if n == 0 and parity == 0:
                b0 = jnp.where(lane == 0, 0.0, b0)
            if n == 1 and parity == 1:
                b0 = jnp.where(first & (row == 0), 0.0, b0)
            p0, p1 = w0 * (1.0 / 12.0), w1 * (1.0 / 12.0)
            coef[f, 4 * n] = -p0 * inverse
            coef[f, 4 * n + 1] = (7.0 * p0 + b0 + p1) * inverse
            coef[f, 4 * n + 2] = (-p0 - 7.0 * p1 + b1) * inverse
            coef[f, 4 * n + 3] = p1 * inverse
            center = center + (7.0 * p0 - b0) - (7.0 * p1 + b1)
        coef[f, 8] = center * inverse

    block = z.flux
    south_at, north_at = jnp.where(first, block, 0), jnp.where(last, 0, block)
    fetch.wait()
    slot = [order[0, f] for f in range(6)]

    def quad(it, count):
        for a in range(3):
            a_s, a_n = jnp.where(first, (a + 2) % 3, a), jnp.where(last, (a + 1) % 3, a)

            def ghosts(ref, at, ref_a):
                return ref[pl.ds(pl.multiple_of(at + ref_a * z.group + 8 * it, 8), 8)]

            south_rows = [ghosts(south, south_at, a_s), jnp.where(first, 0.0, ghosts(south, block, a))]
            north_rows = [jnp.where(last, 0.0, ghosts(north, 0, a)), ghosts(north, north_at, a_n)]
            fe, fo = 2 * a, 2 * a + 1
            ce = [coef[fe, n] for n in range(9)]
            co = [coef[fo, n] for n in range(9)]
            for u in range(count):
                s = 4 * it + u
                qe, qo = mixing[s, 0, slot[fe]], mixing[s, 0, slot[fo]]
                for q, west, east, c, parity, f in ((qe, 0.0, qo, ce, 0, fe), (qo, qe, 0.0, co, 1, fo)):
                    sv = roll(south_rows[parity], 6 - 2 * u, 0)
                    nv = roll(north_rows[parity], -2 * u, 0)
                    value = c[8] * q
                    value += c[0] * left(q, west, 2)
                    value += c[1] * left(q, west, 1)
                    value += c[2] * right(q, east, 1)
                    value += c[3] * right(q, east, 2)
                    value += c[4] * below(q, sv, 2)
                    value += c[5] * below(q, sv, 1)
                    value += c[6] * above(q, nv, 1)
                    value += c[7] * above(q, nv, 2)
                    partial[s, f] = value

    @pl.loop(0, species // 4)
    def _(it):
        quad(it, 4)

    if species % 4:
        quad(species // 4, species % 4)

    for parity in range(2):
        values = []
        for a in range(3):
            f = 2 * a + parity
            fx, dp, inverse, new = (aux[f, n] for n in range(4))
            if parity == 0:
                u0, p0, p1 = column(fx, 0), column(fx, 0) * (1.0 / 12.0), column(fx, 1) * (1.0 / 12.0)
                i0, i1 = column(inverse, 0), column(inverse, 1)
                values.append((u0, column(dp, 0), i0, -p0 * i0, (7.0 * p0 + p1) * i0, -p1 * i1))
            else:
                p0 = column(fx, width - 1) * (1.0 / 12.0)
                i0 = column(inverse, width - 2)
                values.append((column(dp, width - 1), column(new, width - 1), p0, p0 * i0, i0))
        for k in range(z.vregs):
            x = [spread(z, [v[n] for v in values], k) for n in range(len(values[0]))]
            if parity == 0:
                x[3] = jnp.where((lane1 & 1) == 1, x[5], x[3])
            for n in range(5):
                early[parity, n, :, k * 128 : (k + 1) * 128] = x[n]

    lanes = [[jnp.zeros((8, 128), F32) for _ in range(z.vregs)] for _ in range(2)]
    for s in range(species):
        for f in range(6):
            a, parity = f // 2, f % 2
            at = a * z.group + 2 * s
            cut = slice(0, 128) if parity == 0 else slice(width - 128, width)
            moved = roll(partial[s, f, :, cut], at - (0 if parity == 0 else 126), 1)
            k = at // 128
            lanes[parity][k] = jnp.where((lane1 >> 1) == (at % 128) // 2, moved, lanes[parity][k])
    for parity in range(2):
        for k in range(z.vregs):
            ends[parity, :, k * 128 : (k + 1) * 128] = lanes[parity][k]


def finish_kernel(
    z, order_in, mixing, from_b, partial, ends, aux, early, edges, arrived, out,
    turned, fixed, result, out_sem,
):
    place = lax.axis_index("tile")
    half = lax.axis_index("spec")
    first, last = place == 0, place == z.tiles - 1
    width, part, species, n_half = z.width, z.part, z.species, z.halves
    lane = lax.broadcasted_iota(jnp.int32, (8, width), 1)
    row = lax.broadcasted_iota(jnp.int32, (8, width), 0)
    lane1 = lax.broadcasted_iota(jnp.int32, (8, 128), 1)
    twelfth = 1.0 / 12.0
    holder = lax.div(width - 8 - 8 * place, part)

    def message(n, t, cut):
        rank = sum(jnp.where(n == h, z.rank[t][h], 0) for h in range(n_half))
        return arrived[rank, :, cut]

    places = order_in[0:1].astype(F32)
    slot = [jnp.sum(jnp.where(lane1[0:1] == f, places, 0.0)).astype(jnp.int32) for f in range(6)]

    east_flow = []
    odd_end = (lane1 & 1) == 1
    for parity in range(2):
        end = z.tiles - 1 if parity == 0 else 0
        flux = reverse8(message(holder, end, slice((z.flux // 128) * 128, (z.flux // 128 + 1) * 128)))
        ghost_dp = [column(flux, z.flux % 128 + a) for a in range(3)]
        if parity == 1:
            east_flow = [column(flux, z.flux % 128 + 3 + a) for a in range(3)]
        for k in range(z.vregs):
            cut = slice(k * 128, (k + 1) * 128)
            g = reverse8(message(half, end, cut))
            own, q = ends[parity, :, cut], edges[parity, :, cut]
            m = [early[parity, n, :, cut] for n in range(5)]
            ghost = spread(z, ghost_dp, k)
            if parity == 0:
                b = upwind(m[0], ghost + m[1]) * m[2]
                value = own + m[3] * g + jnp.where(odd_end, 0.0, (m[4] + b) * roll(g, -1, 1) - b * q)
            else:
                u = spread(z, east_flow, k)
                p, b = u * twelfth, upwind(u, m[0] + ghost)
                last_cell = own + p * (g + roll(q, 1, 1)) + (b - 7.0 * p - m[2]) * roll(g, 1, 1) - (7.0 * p + b) * q
                value = jnp.where(odd_end, last_cell / (m[1] - u), own + m[3] * g)
            fixed[parity, :, cut] = value

    cuts = [species * n // OUT_CHUNKS for n in range(OUT_CHUNKS + 1)]

    def store(n, special):
        for f in range(6):
            a, parity = f // 2, f % 2
            extra = special(a, parity) if special else None
            for s in range(cuts[n], cuts[n + 1]):
                at = a * z.group + 2 * s
                value = partial[s, f]
                end = fixed[parity, :, (at // 128) * 128 : (at // 128 + 1) * 128]
                end = wide(roll(end, -at if parity == 0 else 126 - at, 1), width)
                value = jnp.where(lane < 2 if parity == 0 else lane >= width - 2, end, value)
                if extra is not None:
                    value = extra(value, s, f)
                result[f, s] = value

    def send(n):
        some = pl.ds(cuts[n], cuts[n + 1] - cuts[n])
        for f in range(6):
            pltpu.make_async_copy(result.at[f, some], out.at[some, 0, slot[f]], out_sem).start()

    def everything(special=None):
        for n in range(OUT_CHUNKS):
            store(n, special)
            send(n)

    def gather():
        holder = jnp.where(first, n_half - 1, 0)
        pieces = []
        for k in range(z.vregs):
            cut = slice(k * 128, (k + 1) * 128)
            spare = from_b[z.extra + 8 * k : z.extra + 8 * k + 8, 0:128]
            mine = reverse8(jnp.where(first, edges[1, :, cut], edges[0, :, cut]))
            parts = []
            for t in reversed(range(z.tiles)):
                if t == 0:
                    x = jnp.where(first, mine, spare)
                elif t == z.tiles - 1:
                    x = jnp.where(first, spare, mine)
                else:
                    x = message(half, t, cut)
                if (k + 1) * 128 > z.flux:
                    x = jnp.where(lane1 + k * 128 < z.flux, x, message(holder, t, cut))
                parts.append(x)
            pieces.append(jnp.concatenate(parts, axis=0).T)
        turned[...] = jnp.concatenate(pieces, axis=0) if len(pieces) > 1 else pieces[0]
        return turned[z.flux2 : z.flux2 + 8]

    @pl.when(first)
    def _():
        flux = gather()

        def special(a, parity):
            if parity == 0:
                return None
            f, source = 2 * a + 1, (a + 2) % 3
            dp, inverse, new, v0, v1 = (aux[f, n] for n in range(1, 6))
            east = lane == width - 1
            inverse = jnp.where(east, 1.0 / jnp.where(east, new - east_flow[a], 1.0), inverse)
            ghost_dp = flux[source : source + 1]
            p0, p1, b0 = v0 * twelfth, v1 * twelfth, upwind(v0, ghost_dp + dp)
            zero = jnp.zeros_like(dp)
            on0, on1 = row == 0, row < 2
            two = jnp.where(on1, -p0 * inverse, zero)
            one = jnp.where(on0, (7.0 * p0 + b0 + p1) * inverse, zero)
            none = jnp.where(on0, -b0 * inverse, zero)

            def extra(value, s, f):
                rows = turned[source * z.group + 8 * (s // 4) : source * z.group + 8 * (s // 4) + 8]
                u = s % 4
                q = mixing[s, 0, slot[f]]
                return value + two * roll(rows, -2 * u, 0) + one * roll(rows, -2 * u - 1, 0) + none * q

            return extra

        everything(special)

    @pl.when(last)
    def _():
        flux = gather()

        def special(a, parity):
            if parity == 1:
                return None
            f, source = 2 * a, (a + 1) % 3
            dp, inverse, new, v0 = (aux[f, n] for n in (1, 2, 3, 4))
            ghost_dp, v1 = flux[source : source + 1], flux[3 + source : 4 + source]
            on7, on6 = row == 7, row >= 6
            inverse = jnp.where(on7, 1.0 / jnp.where(on7, new - v1, 1.0), inverse)
            zero = jnp.zeros_like(dp)
            p0, p1, b1 = v0 * twelfth, v1 * twelfth, upwind(v1, dp + ghost_dp)
            two = jnp.where(on7, p1 * inverse, jnp.where(on6, roll(p0, -1, 0) * inverse, zero))
            one = jnp.where(on7, (b1 - 7.0 * p1 - p0) * inverse, zero)
            none = jnp.where(on7, -(7.0 * p1 + b1) * inverse, zero)
            back = jnp.where(on7, p1 * inverse, zero)
            scale = jnp.where(on7, inverse, 1.0)

            def extra(value, s, f):
                rows = turned[source * z.group + 8 * (s // 4) : source * z.group + 8 * (s // 4) + 8]
                u = s % 4
                q = mixing[s, 0, slot[f]]
                value = value * scale + two * roll(rows, 6 - 2 * u, 0) + one * roll(rows, 7 - 2 * u, 0)
                return value + none * q + back * roll(q, 1, 0)

            return extra

        everything(special)

    @pl.when(jnp.logical_not(first | last))
    def _():
        everything()

    for f in range(6):
        pltpu.make_async_copy(result.at[f], out.at[:, 0, slot[f]], out_sem).wait()


def local(mixing, layer_mass, mass_east, mass_north, face_slot):
    tiles = lax.axis_size("tile")
    halves = lax.axis_size("spec")
    z = Sizes(mixing, halves, tiles)
    assert z.rows == 8 and mixing.shape[1] == 1 and tiles > 2 and tiles % 2 == 0
    assert z.width == 8 * tiles and z.width % 128 == 0 and 128 % z.part == 0
    vmem = pl.BlockSpec(memory_space=pltpu.VMEM)
    hbm = pl.BlockSpec(memory_space=pl.ANY)
    params = pltpu.CompilerParams(vmem_limit_bytes=VMEM_LIMIT)
    cells = (z.species, 6, 8, z.width)

    def f32(*shape):
        return jax.ShapeDtypeStruct(shape, F32)

    packed = (
        f32(z.sent, z.width),
        f32(z.sent, z.width),
        f32(halves * tiles, 8, z.lanes),
        f32(2, 8, z.lanes),
        f32(z.own, 8, 128),
        jax.ShapeDtypeStruct((8, 128), jnp.int32),
    )
    to_a, to_b, messages, edges, own, order = pl.pallas_call(
        lambda *refs: pack_kernel(z, *refs),
        out_shape=packed,
        in_specs=[hbm] * 5,
        out_specs=[hbm] * 6,
        scratch_shapes=[pltpu.VMEM(x.shape, x.dtype) for x in packed]
        + [
            pltpu.SMEM((6,), jnp.int32),
            pltpu.VMEM(mixing.shape, F32),
            pltpu.VMEM((3,) + layer_mass.shape, F32),
            pltpu.SemaphoreType.DMA((4 + CHUNKS,)),
            pltpu.SemaphoreType.DMA((5 + 2 * halves,)),
        ],
        name="pack",
    )(face_slot, mixing, layer_mass, mass_east, mass_north)
    arrived = lax.all_to_all(
        messages, ("tile", "spec"), 0, 0, axis_index_groups=[list(z.order)], tiled=True
    )
    from_a = lax.ppermute(to_a, "tile", [(i, i ^ 1) for i in range(tiles)])
    pairs = [(i, (i + 1) % tiles) if i % 2 else (i, (i - 1) % tiles) for i in range(tiles)]
    from_b = lax.ppermute(to_b, "tile", pairs)
    mine = pl.pallas_call(
        lambda *refs: share_kernel(z, *refs),
        out_shape=f32(z.shared, 8, 128),
        in_specs=[vmem] * 3,
        out_specs=vmem,
        compiler_params=params,
        cost_estimate=pl.CostEstimate(flops=23 * 10**9, bytes_accessed=0, transcendentals=0),
        name="share",
    )(own, from_a, from_b)
    if halves == 2:
        others = lax.ppermute(mine, "spec", [(0, 1), (1, 0)])
    else:
        others = lax.all_gather(mine, "spec", axis=0, tiled=False)
    partial, ends, aux, early = pl.pallas_call(
        lambda *refs: interior_kernel(z, *refs),
        out_shape=(f32(*cells), f32(2, 8, z.lanes), f32(6, 6, 8, z.width), f32(2, 5, 8, z.lanes)),
        in_specs=[vmem] * 6,
        out_specs=[vmem] * 4,
        scratch_shapes=[
            pltpu.SMEM((8, 128), jnp.int32),
            pltpu.VMEM((2 * z.flux, z.width), F32),
            pltpu.VMEM((2 * z.flux, z.width), F32),
            pltpu.VMEM((6, 9, 8, z.width), F32),
            pltpu.SemaphoreType.DMA,
        ],
        compiler_params=params,
        name="interior",
    )(order, mixing, from_a, from_b, mine, others)
    return pl.pallas_call(
        lambda *refs: finish_kernel(z, *refs),
        out_shape=f32(*mixing.shape),
        in_specs=[vmem] * 9,
        out_specs=hbm,
        scratch_shapes=[
            pltpu.VMEM((z.lanes, z.width), F32),
            pltpu.VMEM((2, 8, z.lanes), F32),
            pltpu.VMEM((6, z.species, 8, z.width), F32),
            pltpu.SemaphoreType.DMA,
        ],
        compiler_params=params,
        name="finish",
    )(order, mixing, from_b, partial, ends, aux, early, edges, arrived)


def solution(mesh):
    flux = P(None, None, "tile", "spec")
    cells = P("spec", None, None, "tile", None)
    return jax.shard_map(
        local,
        mesh=mesh,
        in_specs=(cells, flux, flux, flux, P()),
        out_specs=cells,
        check_vma=False,
    )
```

```python
import jax
import jax.numpy as jnp
from jax import lax
from jax.experimental import pallas as pl
from jax.experimental.pallas import tpu as pltpu
from jax.sharding import PartitionSpec as P

F32 = jnp.float32
VMEM_LIMIT = 12 << 20
CHUNKS = 2
OUT_CHUNKS = 6
ORDERS = {(16, 2): (
    19, 30, 2, 7, 17, 10, 26, 18, 20, 22, 16, 9, 25, 1, 5, 3,
    12, 31, 28, 0, 14, 27, 21, 8, 11, 15, 6, 13, 4, 29, 24, 23,
)}


def up(value, unit):
    return -(-value // unit) * unit


class Sizes:
    def __init__(self, mixing, halves, tiles):
        self.species, _, _, self.rows, self.width = mixing.shape
        self.tiles, self.halves = tiles, halves
        self.part = self.width // halves
        self.group = up(2 * self.species, 8)
        self.flux = 3 * self.group
        self.flux2 = self.flux + 8
        self.lanes = up(self.flux2 + 8, 128)
        self.vregs = self.lanes // 128
        self.dp_at = 2 * self.flux
        self.fy_at = self.dp_at + 8
        self.extra = self.fy_at + 8
        self.sent = self.extra + 8 * self.vregs
        self.per = 128 // self.part
        self.own = up(18, self.per) // self.per
        self.pieces = 21
        self.shared = up(self.pieces, self.per) // self.per
        natural = tuple(t * halves + n for n in range(halves) for t in range(tiles))
        self.order = ORDERS.get((tiles, halves), natural)
        ranks = {device: rank for rank, device in enumerate(self.order)}
        self.rank = [[ranks[t * halves + n] for n in range(halves)] for t in range(tiles)]


def slots(face_slot):
    return [sum(jnp.where(face_slot[s] == f, s, 0) for s in range(6)) for f in range(6)]


def roll(x, shift, axis):
    shift %= x.shape[axis]
    return pltpu.roll(x, shift, axis) if shift else x


def reverse8(x):
    row = lax.broadcasted_iota(jnp.int32, x.shape, 0)
    x = jnp.where((row & 1) == 0, roll(x, -1, 0), roll(x, 1, 0))
    x = jnp.where((row & 2) == 0, roll(x, -2, 0), roll(x, 2, 0))
    return roll(x, 4, 0)


def upwind(u, total):
    return 0.5 * jnp.abs(u) * (1.0 - jnp.abs(u / (0.5 * total)))


def column(x, at):
    return x[:, at : at + 1]


def spread(z, values, k):
    at = lax.broadcasted_iota(jnp.int32, (8, 128), 1) + k * 128
    return jnp.where(at < z.group, values[0], jnp.where(at < 2 * z.group, values[1], values[2]))


def wide(x, width):
    return jnp.concatenate([x] * (width // 128), axis=-1) if width > 128 else x


def side_by_side(tiles, per):
    tiles = tiles + [tiles[0]] * (per - len(tiles))
    return jnp.concatenate(tiles, axis=-1) if per > 1 else tiles[0]


def pack_kernel(
    z, slot_in, mixing_in, dp_in, fx_in, fy_in,
    to_a_out, to_b_out, out_out, edges_out, own_out, order_out,
    to_a, to_b, out, edges, own, order, face_slot, mixing, fluxes, sems, out_sems,
):
    cuts = [0, z.species * 5 // 12, z.species]
    copies = [pltpu.make_async_copy(slot_in, face_slot, sems.at[0])]
    for c, ref in enumerate((dp_in, fx_in, fy_in)):
        copies.append(pltpu.make_async_copy(ref, fluxes.at[c], sems.at[1 + c]))
    for n in range(CHUNKS):
        some = pl.ds(cuts[n], cuts[n + 1] - cuts[n])
        copies.append(pltpu.make_async_copy(mixing_in.at[some], mixing.at[some], sems.at[4 + n]))
    for copy in copies:
        copy.start()
    place = lax.axis_index("tile")
    half = lax.axis_index("spec")
    copies[0].wait()
    slot = slots(face_slot)
    even = lax.rem(place, 2) == 0
    first, last = place == 0, place == z.tiles - 1
    width, part, species, n_half = z.width, z.part, z.species, z.halves
    lane = lax.broadcasted_iota(jnp.int32, (8, 128), 1)
    order[...] = sum(jnp.where(lane == f, slot[f], 0) for f in range(6))
    results = [
        pltpu.make_async_copy(x, y, out_sems.at[n])
        for n, (x, y) in enumerate(
            ((to_a, to_a_out), (to_b, to_b_out), (edges, edges_out), (own, own_out), (order, order_out))
        )
    ]
    results[4].start()
    for copy in copies[1:4]:
        copy.wait()
    raw = [[fluxes[c, 0, slot[f]] for f in range(6)] for c in range(3)]
    flat = [raw[c][f] for c in range(3) for f in range(6)]
    for n in range(z.own):
        own[n] = side_by_side(flat[n * z.per : (n + 1) * z.per], z.per)
    results[3].start()

    def both(low, high, at):
        to_a[pl.ds(at, low.shape[0])] = jnp.where(even, high, low)
        to_b[pl.ds(at, low.shape[0])] = jnp.where(even, low, high)

    def padded(x):
        return jnp.concatenate([x, jnp.zeros((8, width - part), F32)], axis=-1) if width > part else x

    pad = jnp.zeros((2, part), F32)
    low_dp = jnp.concatenate([x[0:1] for x in raw[0]] + [pad], axis=0)
    high_dp = jnp.concatenate([x[7:8] for x in raw[0]] + [pad], axis=0)
    low_fy = padded(jnp.concatenate([x[0:1] for x in raw[2]] + [pad], axis=0))
    both(padded(low_dp), padded(high_dp), z.dp_at)
    both(low_fy, low_fy, z.fy_at)

    columns = [[jnp.zeros((8, 128), F32) for _ in range(z.vregs)] for _ in range(2)]
    for parity in range(2):
        for a in range(3):
            f = 2 * a + parity
            if z.group > 2 * species:
                zero = jnp.zeros((z.group - 2 * species, width), F32)
                both(zero, zero, parity * z.flux + a * z.group + 2 * species)
            for c in range(2):
                at = z.flux2 + 3 * c + a
                edge = side_by_side([raw[c][f]] * z.per, z.per)
                moved = roll(edge, at - (0 if parity == 0 else 127), 1)
                k = at // 128
                columns[parity][k] = jnp.where(lane == at % 128, moved, columns[parity][k])
    for n in range(CHUNKS):
        copies[4 + n].wait()
        for s in range(cuts[n], cuts[n + 1]):
            for f in range(6):
                a, parity = f // 2, f % 2
                tile = mixing[s, 0, slot[f]]
                at = a * z.group + 2 * s
                both(tile[0:2], tile[6:8], parity * z.flux + at)
                edge = tile[:, :128] if parity == 0 else tile[:, width - 128 :]
                moved = roll(edge, at - (0 if parity == 0 else 126), 1)
                k = at // 128
                columns[parity][k] = jnp.where((lane >> 1) == (at % 128) // 2, moved, columns[parity][k])
    turned = [[reverse8(x) for x in lanes] for lanes in columns]
    for k in range(z.vregs):
        for parity in range(2):
            edges[parity, :, k * 128 : (k + 1) * 128] = columns[parity][k]
        spare = wide(jnp.where(first, turned[0][k], turned[1][k]), width)
        to_a[pl.ds(z.extra + 8 * k, 8)] = spare
        to_b[pl.ds(z.extra + 8 * k, 8)] = spare
    for n in range(3):
        results[n].start()

    ends = ((0, turned[1]), (z.tiles - 1, turned[0]))

    @pl.when(first | last)
    def _():
        rows, dps, fys = [], [], []
        for a in range(3):
            for_odd, for_even = (a + 1) % 3, (a + 2) % 3
            start = jnp.where(first, z.flux + for_odd * z.group, for_even * z.group)
            rows.append(to_b[pl.ds(pl.multiple_of(start, 8), z.group)])
            for c, values in ((0, dps), (2, fys)):
                values.append(jnp.where(first, raw[c][2 * for_odd + 1][0:1], raw[c][2 * for_even][7:8]))
        flux = jnp.concatenate(dps + fys + [pad], axis=0)
        flux = jnp.concatenate([jnp.where(half == n, flux, 0.0) for n in range(n_half)], axis=-1)
        rows += [flux, jnp.zeros((z.lanes - z.flux - 8, width), F32)]
        messages = jnp.concatenate(rows, axis=0).T
        for t in range(z.tiles):
            at = 8 * (z.tiles - 1 - t)
            for n in range(n_half):
                out[z.rank[t][n]] = messages[at : at + 8]
        for t, cols in ends:
            at = 8 * (z.tiles - 1 - t)
            k = z.flux2 // 128
            here = (lane >= z.flux2 % 128) & (lane < z.flux2 % 128 + 8)
            mixed = jnp.where(here, cols[k], messages[at : at + 8, k * 128 : (k + 1) * 128])
            for n in range(n_half):
                out[z.rank[t][n], :, k * 128 : (k + 1) * 128] = mixed
        copy = pltpu.make_async_copy(out, out_out, out_sems.at[5])
        copy.start()
        copy.wait()

    @pl.when(jnp.logical_not(first | last))
    def _():
        for t, cols in ends:
            for n in range(n_half):
                for k in range(z.vregs):
                    out[z.rank[t][n], :, k * 128 : (k + 1) * 128] = cols[k]
        copies = []
        for e, (t, _) in enumerate(ends):
            for n in range(n_half):
                at = z.rank[t][n]
                copies.append(pltpu.make_async_copy(out.at[at], out_out.at[at], out_sems.at[5 + e * n_half + n]))
        for copy in copies:
            copy.start()
        for copy in copies:
            copy.wait()

    for copy in results:
        copy.wait()


def share_kernel(z, own, from_a, from_b, out):
    even = lax.rem(lax.axis_index("tile"), 2) == 0
    part = z.part
    dp_a, dp_b = from_a[z.dp_at : z.dp_at + 8, :part], from_b[z.dp_at : z.dp_at + 8, :part]
    fy_a, fy_b = from_a[z.fy_at : z.fy_at + 8, :part], from_b[z.fy_at : z.fy_at + 8, :part]
    halo = [jnp.where(even, dp_b, dp_a), jnp.where(even, dp_a, dp_b), jnp.where(even, fy_a, fy_b)]
    flat = [own[n // z.per][:, (n % z.per) * part : (n % z.per + 1) * part] for n in range(18)] + halo
    for n in range(z.shared):
        out[n] = side_by_side(flat[n * z.per : (n + 1) * z.per], z.per)


def interior_kernel(
    z, order_in, mixing, from_a, from_b, mine, others, partial, ends, aux, early,
    order, south, north, coef, order_sem,
):
    fetch = pltpu.make_async_copy(order_in, order, order_sem)
    fetch.start()
    place = lax.axis_index("tile")
    half = lax.axis_index("spec")
    even = lax.rem(place, 2) == 0
    first, last = place == 0, place == z.tiles - 1
    width, part, species = z.width, z.part, z.species
    lane = lax.broadcasted_iota(jnp.int32, (8, width), 1)
    row = lax.broadcasted_iota(jnp.int32, (8, width), 0)
    lane1 = lax.broadcasted_iota(jnp.int32, (8, 128), 1)

    a_rows, b_rows = from_a[0 : z.dp_at], from_b[0 : z.dp_at]
    south[...] = jnp.where(even, b_rows, a_rows)
    north[...] = jnp.where(even, a_rows, b_rows)

    full = []
    for n in range(z.pieces):
        cut = slice((n % z.per) * part, (n % z.per + 1) * part)
        if z.halves == 2:
            x, y = mine[n // z.per][:, cut], others[n // z.per][:, cut]
            parts = [jnp.where(half == 0, x, y), jnp.where(half == 0, y, x)]
        else:
            parts = [others[h, n // z.per][:, cut] for h in range(z.halves)]
        full.append(jnp.concatenate(parts, axis=-1))
    dp_south, dp_north, fy_north = full[18:]

    def left(x, ghost, n):
        return pltpu.roll(jnp.where(lane >= width - n, ghost, x), n, 1)

    def right(x, ghost, n):
        return pltpu.roll(jnp.where(lane < n, ghost, x), width - n, 1)

    def below(x, ghost, n):
        return pltpu.roll(jnp.where(row >= 8 - n, ghost, x), n, 0)

    def above(x, ghost, n):
        return pltpu.roll(jnp.where(row < n, ghost, x), 8 - n, 0)

    for f in range(6):
        parity = f % 2
        dp, fx, fy = full[f], full[6 + f], full[12 + f]
        if parity == 0:
            west, east, east_u = dp, full[f + 1], full[6 + f + 1]
            s_end, n_end, v_end = roll(dp_south, 7 - (f - 1) % 6, 0), dp, 0.0
            known = jnp.logical_not(last & (row == 7))
        else:
            west, east, east_u = full[f - 1], dp, 0.0
            s_end, n_end, v_end = dp, roll(dp_north, -((f + 1) % 6), 0), roll(fy_north, -((f + 1) % 6), 0)
            known = lane < width - 1
        dp_w, dp_e = left(dp, west, 1), right(dp, east, 1)
        u0, u1 = fx, right(fx, east_u, 1)
        dp_s = below(dp, jnp.where(first, s_end, roll(dp_south, 7 - f, 0)), 1)
        dp_n = above(dp, jnp.where(last, n_end, roll(dp_north, -f, 0)), 1)
        v0, v1 = fy, above(fy, jnp.where(last, v_end, roll(fy_north, -f, 0)), 1)
        new = dp - (u1 - u0) - (v1 - v0)
        inverse = jnp.where(known, 1.0 / jnp.where(known, new, 1.0), 1.0)
        for n, x in enumerate((fx, dp, inverse, new, v0, v1)):
            aux[f, n] = x
        center = dp
        for n, (w0, w1, d0, d1) in enumerate(((u0, u1, dp_w, dp_e), (v0, v1, dp_s, dp_n))):
            b0, b1 = upwind(w0, d0 + dp), upwind(w1, dp + d1)
            if n == 0 and parity == 0:
                b0 = jnp.where(lane == 0, 0.0, b0)
            if n == 1 and parity == 1:
                b0 = jnp.where(first & (row == 0), 0.0, b0)
            p0, p1 = w0 * (1.0 / 12.0), w1 * (1.0 / 12.0)
            coef[f, 4 * n] = -p0 * inverse
            coef[f, 4 * n + 1] = (7.0 * p0 + b0 + p1) * inverse
            coef[f, 4 * n + 2] = (-p0 - 7.0 * p1 + b1) * inverse
            coef[f, 4 * n + 3] = p1 * inverse
            center = center + (7.0 * p0 - b0) - (7.0 * p1 + b1)
        coef[f, 8] = center * inverse

    block = z.flux
    south_at, north_at = jnp.where(first, block, 0), jnp.where(last, 0, block)
    fetch.wait()
    slot = [order[0, f] for f in range(6)]

    def quad(it, count):
        for a in range(3):
            a_s, a_n = jnp.where(first, (a + 2) % 3, a), jnp.where(last, (a + 1) % 3, a)

            def ghosts(ref, at, ref_a):
                return ref[pl.ds(pl.multiple_of(at + ref_a * z.group + 8 * it, 8), 8)]

            south_rows = [ghosts(south, south_at, a_s), jnp.where(first, 0.0, ghosts(south, block, a))]
            north_rows = [jnp.where(last, 0.0, ghosts(north, 0, a)), ghosts(north, north_at, a_n)]
            fe, fo = 2 * a, 2 * a + 1
            ce = [coef[fe, n] for n in range(9)]
            co = [coef[fo, n] for n in range(9)]
            for u in range(count):
                s = 4 * it + u
                qe, qo = mixing[s, 0, slot[fe]], mixing[s, 0, slot[fo]]
                for q, west, east, c, parity, f in ((qe, 0.0, qo, ce, 0, fe), (qo, qe, 0.0, co, 1, fo)):
                    sv = roll(south_rows[parity], 6 - 2 * u, 0)
                    nv = roll(north_rows[parity], -2 * u, 0)
                    value = c[8] * q
                    value += c[0] * left(q, west, 2)
                    value += c[1] * left(q, west, 1)
                    value += c[2] * right(q, east, 1)
                    value += c[3] * right(q, east, 2)
                    value += c[4] * below(q, sv, 2)
                    value += c[5] * below(q, sv, 1)
                    value += c[6] * above(q, nv, 1)
                    value += c[7] * above(q, nv, 2)
                    partial[s, f] = value

    @pl.loop(0, species // 4)
    def _(it):
        quad(it, 4)

    if species % 4:
        quad(species // 4, species % 4)

    for parity in range(2):
        values = []
        for a in range(3):
            f = 2 * a + parity
            fx, dp, inverse, new = (aux[f, n] for n in range(4))
            if parity == 0:
                u0, p0, p1 = column(fx, 0), column(fx, 0) * (1.0 / 12.0), column(fx, 1) * (1.0 / 12.0)
                i0, i1 = column(inverse, 0), column(inverse, 1)
                values.append((u0, column(dp, 0), i0, -p0 * i0, (7.0 * p0 + p1) * i0, -p1 * i1))
            else:
                p0 = column(fx, width - 1) * (1.0 / 12.0)
                i0 = column(inverse, width - 2)
                values.append((column(dp, width - 1), column(new, width - 1), p0, p0 * i0, i0))
        for k in range(z.vregs):
            x = [spread(z, [v[n] for v in values], k) for n in range(len(values[0]))]
            if parity == 0:
                x[3] = jnp.where((lane1 & 1) == 1, x[5], x[3])
            for n in range(5):
                early[parity, n, :, k * 128 : (k + 1) * 128] = x[n]

    lanes = [[jnp.zeros((8, 128), F32) for _ in range(z.vregs)] for _ in range(2)]
    for s in range(species):
        for f in range(6):
            a, parity = f // 2, f % 2
            at = a * z.group + 2 * s
            cut = slice(0, 128) if parity == 0 else slice(width - 128, width)
            moved = roll(partial[s, f, :, cut], at - (0 if parity == 0 else 126), 1)
            k = at // 128
            lanes[parity][k] = jnp.where((lane1 >> 1) == (at % 128) // 2, moved, lanes[parity][k])
    for parity in range(2):
        for k in range(z.vregs):
            ends[parity, :, k * 128 : (k + 1) * 128] = lanes[parity][k]


def finish_kernel(
    z, order_in, mixing, from_b, partial, ends, aux, early, edges, arrived, out,
    turned, fixed, result, out_sem,
):
    place = lax.axis_index("tile")
    half = lax.axis_index("spec")
    first, last = place == 0, place == z.tiles - 1
    width, part, species, n_half = z.width, z.part, z.species, z.halves
    lane = lax.broadcasted_iota(jnp.int32, (8, width), 1)
    row = lax.broadcasted_iota(jnp.int32, (8, width), 0)
    lane1 = lax.broadcasted_iota(jnp.int32, (8, 128), 1)
    twelfth = 1.0 / 12.0
    holder = lax.div(width - 8 - 8 * place, part)

    def message(n, t, cut):
        rank = sum(jnp.where(n == h, z.rank[t][h], 0) for h in range(n_half))
        return arrived[rank, :, cut]

    places = order_in[0:1].astype(F32)
    slot = [jnp.sum(jnp.where(lane1[0:1] == f, places, 0.0)).astype(jnp.int32) for f in range(6)]

    east_flow = []
    odd_end = (lane1 & 1) == 1
    for parity in range(2):
        end = z.tiles - 1 if parity == 0 else 0
        flux = reverse8(message(holder, end, slice((z.flux // 128) * 128, (z.flux // 128 + 1) * 128)))
        ghost_dp = [column(flux, z.flux % 128 + a) for a in range(3)]
        if parity == 1:
            east_flow = [column(flux, z.flux % 128 + 3 + a) for a in range(3)]
        for k in range(z.vregs):
            cut = slice(k * 128, (k + 1) * 128)
            g = reverse8(message(half, end, cut))
            own, q = ends[parity, :, cut], edges[parity, :, cut]
            m = [early[parity, n, :, cut] for n in range(5)]
            ghost = spread(z, ghost_dp, k)
            if parity == 0:
                b = upwind(m[0], ghost + m[1]) * m[2]
                value = own + m[3] * g + jnp.where(odd_end, 0.0, (m[4] + b) * roll(g, -1, 1) - b * q)
            else:
                u = spread(z, east_flow, k)
                p, b = u * twelfth, upwind(u, m[0] + ghost)
                last_cell = own + p * (g + roll(q, 1, 1)) + (b - 7.0 * p - m[2]) * roll(g, 1, 1) - (7.0 * p + b) * q
                value = jnp.where(odd_end, last_cell / (m[1] - u), own + m[3] * g)
            fixed[parity, :, cut] = value

    cuts = [species * n // OUT_CHUNKS for n in range(OUT_CHUNKS + 1)]

    def store(n, special):
        for f in range(6):
            a, parity = f // 2, f % 2
            extra = special(a, parity) if special else None
            for s in range(cuts[n], cuts[n + 1]):
                at = a * z.group + 2 * s
                value = partial[s, f]
                end = fixed[parity, :, (at // 128) * 128 : (at // 128 + 1) * 128]
                end = wide(roll(end, -at if parity == 0 else 126 - at, 1), width)
                value = jnp.where(lane < 2 if parity == 0 else lane >= width - 2, end, value)
                if extra is not None:
                    value = extra(value, s, f)
                result[f, s] = value

    def send(n):
        some = pl.ds(cuts[n], cuts[n + 1] - cuts[n])
        for f in range(6):
            pltpu.make_async_copy(result.at[f, some], out.at[some, 0, slot[f]], out_sem).start()

    def everything(special=None):
        for n in range(OUT_CHUNKS):
            store(n, special)
            send(n)

    def gather():
        holder = jnp.where(first, n_half - 1, 0)
        pieces = []
        for k in range(z.vregs):
            cut = slice(k * 128, (k + 1) * 128)
            spare = from_b[z.extra + 8 * k : z.extra + 8 * k + 8, 0:128]
            mine = reverse8(jnp.where(first, edges[1, :, cut], edges[0, :, cut]))
            parts = []
            for t in reversed(range(z.tiles)):
                if t == 0:
                    x = jnp.where(first, mine, spare)
                elif t == z.tiles - 1:
                    x = jnp.where(first, spare, mine)
                else:
                    x = message(half, t, cut)
                if (k + 1) * 128 > z.flux:
                    x = jnp.where(lane1 + k * 128 < z.flux, x, message(holder, t, cut))
                parts.append(x)
            pieces.append(jnp.concatenate(parts, axis=0).T)
        turned[...] = jnp.concatenate(pieces, axis=0) if len(pieces) > 1 else pieces[0]
        return turned[z.flux2 : z.flux2 + 8]

    @pl.when(first)
    def _():
        flux = gather()

        def special(a, parity):
            if parity == 0:
                return None
            f, source = 2 * a + 1, (a + 2) % 3
            dp, inverse, new, v0, v1 = (aux[f, n] for n in range(1, 6))
            east = lane == width - 1
            inverse = jnp.where(east, 1.0 / jnp.where(east, new - east_flow[a], 1.0), inverse)
            ghost_dp = flux[source : source + 1]
            p0, p1, b0 = v0 * twelfth, v1 * twelfth, upwind(v0, ghost_dp + dp)
            zero = jnp.zeros_like(dp)
            on0, on1 = row == 0, row < 2
            two = jnp.where(on1, -p0 * inverse, zero)
            one = jnp.where(on0, (7.0 * p0 + b0 + p1) * inverse, zero)
            none = jnp.where(on0, -b0 * inverse, zero)

            def extra(value, s, f):
                rows = turned[source * z.group + 8 * (s // 4) : source * z.group + 8 * (s // 4) + 8]
                u = s % 4
                q = mixing[s, 0, slot[f]]
                return value + two * roll(rows, -2 * u, 0) + one * roll(rows, -2 * u - 1, 0) + none * q

            return extra

        everything(special)

    @pl.when(last)
    def _():
        flux = gather()

        def special(a, parity):
            if parity == 1:
                return None
            f, source = 2 * a, (a + 1) % 3
            dp, inverse, new, v0 = (aux[f, n] for n in (1, 2, 3, 4))
            ghost_dp, v1 = flux[source : source + 1], flux[3 + source : 4 + source]
            on7, on6 = row == 7, row >= 6
            inverse = jnp.where(on7, 1.0 / jnp.where(on7, new - v1, 1.0), inverse)
            zero = jnp.zeros_like(dp)
            p0, p1, b1 = v0 * twelfth, v1 * twelfth, upwind(v1, dp + ghost_dp)
            two = jnp.where(on7, p1 * inverse, jnp.where(on6, roll(p0, -1, 0) * inverse, zero))
            one = jnp.where(on7, (b1 - 7.0 * p1 - p0) * inverse, zero)
            none = jnp.where(on7, -(7.0 * p1 + b1) * inverse, zero)
            back = jnp.where(on7, p1 * inverse, zero)
            scale = jnp.where(on7, inverse, 1.0)

            def extra(value, s, f):
                rows = turned[source * z.group + 8 * (s // 4) : source * z.group + 8 * (s // 4) + 8]
                u = s % 4
                q = mixing[s, 0, slot[f]]
                value = value * scale + two * roll(rows, 6 - 2 * u, 0) + one * roll(rows, 7 - 2 * u, 0)
                return value + none * q + back * roll(q, 1, 0)

            return extra

        everything(special)

    @pl.when(jnp.logical_not(first | last))
    def _():
        everything()

    for f in range(6):
        pltpu.make_async_copy(result.at[f], out.at[:, 0, slot[f]], out_sem).wait()


def local(mixing, layer_mass, mass_east, mass_north, face_slot):
    tiles = lax.axis_size("tile")
    halves = lax.axis_size("spec")
    z = Sizes(mixing, halves, tiles)
    assert z.rows == 8 and mixing.shape[1] == 1 and tiles > 2 and tiles % 2 == 0
    assert z.width == 8 * tiles and z.width % 128 == 0 and 128 % z.part == 0
    vmem = pl.BlockSpec(memory_space=pltpu.VMEM)
    hbm = pl.BlockSpec(memory_space=pl.ANY)
    params = pltpu.CompilerParams(vmem_limit_bytes=VMEM_LIMIT)
    cells = (z.species, 6, 8, z.width)

    def f32(*shape):
        return jax.ShapeDtypeStruct(shape, F32)

    packed = (
        f32(z.sent, z.width),
        f32(z.sent, z.width),
        f32(halves * tiles, 8, z.lanes),
        f32(2, 8, z.lanes),
        f32(z.own, 8, 128),
        jax.ShapeDtypeStruct((8, 128), jnp.int32),
    )
    to_a, to_b, messages, edges, own, order = pl.pallas_call(
        lambda *refs: pack_kernel(z, *refs),
        out_shape=packed,
        in_specs=[hbm] * 5,
        out_specs=[hbm] * 6,
        scratch_shapes=[pltpu.VMEM(x.shape, x.dtype) for x in packed]
        + [
            pltpu.SMEM((6,), jnp.int32),
            pltpu.VMEM(mixing.shape, F32),
            pltpu.VMEM((3,) + layer_mass.shape, F32),
            pltpu.SemaphoreType.DMA((4 + CHUNKS,)),
            pltpu.SemaphoreType.DMA((5 + 2 * halves,)),
        ],
        name="pack",
    )(face_slot, mixing, layer_mass, mass_east, mass_north)
    arrived = lax.all_to_all(
        messages, ("tile", "spec"), 0, 0, axis_index_groups=[list(z.order)], tiled=True
    )
    from_a = lax.ppermute(to_a, "tile", [(i, i ^ 1) for i in range(tiles)])
    pairs = [(i, (i + 1) % tiles) if i % 2 else (i, (i - 1) % tiles) for i in range(tiles)]
    from_b = lax.ppermute(to_b, "tile", pairs)
    mine = pl.pallas_call(
        lambda *refs: share_kernel(z, *refs),
        out_shape=f32(z.shared, 8, 128),
        in_specs=[vmem] * 3,
        out_specs=vmem,
        compiler_params=params,
        cost_estimate=pl.CostEstimate(flops=23 * 10**9, bytes_accessed=0, transcendentals=0),
        name="share",
    )(own, from_a, from_b)
    if halves == 2:
        others = lax.ppermute(mine, "spec", [(0, 1), (1, 0)])
    else:
        others = lax.all_gather(mine, "spec", axis=0, tiled=False)
    partial, ends, aux, early = pl.pallas_call(
        lambda *refs: interior_kernel(z, *refs),
        out_shape=(f32(*cells), f32(2, 8, z.lanes), f32(6, 6, 8, z.width), f32(2, 5, 8, z.lanes)),
        in_specs=[vmem] * 6,
        out_specs=[vmem] * 4,
        scratch_shapes=[
            pltpu.SMEM((8, 128), jnp.int32),
            pltpu.VMEM((2 * z.flux, z.width), F32),
            pltpu.VMEM((2 * z.flux, z.width), F32),
            pltpu.VMEM((6, 9, 8, z.width), F32),
            pltpu.SemaphoreType.DMA,
        ],
        compiler_params=params,
        name="interior",
    )(order, mixing, from_a, from_b, mine, others)
    return pl.pallas_call(
        lambda *refs: finish_kernel(z, *refs),
        out_shape=f32(*mixing.shape),
        in_specs=[vmem] * 9,
        out_specs=hbm,
        scratch_shapes=[
            pltpu.VMEM((z.lanes, z.width), F32),
            pltpu.VMEM((2, 8, z.lanes), F32),
            pltpu.VMEM((6, z.species, 8, z.width), F32),
            pltpu.SemaphoreType.DMA,
        ],
        compiler_params=params,
        name="finish",
    )(order, mixing, from_b, partial, ends, aux, early, edges, arrived)


def solution(mesh):
    flux = P(None, None, "tile", "spec")
    cells = P("spec", None, None, "tile", None)
    return jax.shard_map(
        local,
        mesh=mesh,
        in_specs=(cells, flux, flux, flux, P()),
        out_specs=cells,
        check_vma=False,
    )
```
